32 devices in a mesh: rep: 2 (over x), dp: 4 (over z), tp: 4 (over y, core).
Axes of the slice: x: 2, y: 2, z: 4, core: 2. Of those that a mesh axis runs over, the one named last changes fastest.
Arguments:
- attention_output: bfloat16 [4, 1024, 8192], P(None, ('rep', 'dp'), 'tp'), parts along dimension 1, may hold values from -6 to 6
- output_projection_weight: bfloat16 [8192, 8192], P('tp'), may hold values from -0.09375 to 0.09375
- shrink_matrix_store: bfloat16 [256, 16, 8192], P('dp', None, 'tp'), may hold values from -0.0625 to 0.0625
- expand_matrix_store: bfloat16 [256, 16, 8192], P('dp', None, 'tp'), may hold values from -1.5 to 1.5
- segment_adapter: int32 [4, 64], P(None, ('rep', 'dp')), parts along dimension 1, may hold values from 0 to 255, as said below
- segment_live_rows: int32 [4, 64], P(None, ('rep', 'dp')), parts along dimension 1, may hold values from 1 to 16, as said below
- adapter_store_index: int32 [512], P('rep'), parts along dimension 0, may hold values from 0 to 255, as said below
Outputs:
- projected: bfloat16 [4, 1024, 8192], P(None, ('rep', 'dp'), 'tp'), parts along dimension 1
The draws below stay inside these ranges and needn't reach their ends.
There are 2 independent parts, one for each index of `rep`. The reference program is written for one: setup_inputs(seed, part) draws one part's arguments, and reference() takes and returns one part's arrays. A program takes and returns all parts, laid end to end along the dimension named above; an argument that names none is the same for every part. Nothing has to cross between parts.
Inputs may be any that keep to these rules, and one draw needn't show every extreme that they name: `segment_adapter`: adapter stored at position p lies on index p // 64 of dp. Over all 4 steps, the segments of one index of dp name adapters of which at most 16 lie on any one index of dp, and exactly 16 lie on one of them. `segment_live_rows`: every step of every index of dp has a segment with all 16 rows live. `adapter_store_index`: A permutation: each store position holds one adapter.
All inputs are finite; a program needn't handle non-finite values.
Results may differ from the reference program's by a relative error of at most 0.0095.
Values may be sent and summed in bfloat16 or wider, within the bound.
No kernel may reach another device: no remote copies, remote signals or barrier semaphores. Data moves between devices by JAX's collectives and lax.ppermute only.
A program may use at most 192 MiB of HBM per device.

```python
import jax
import jax.numpy as jnp
from jax import lax

MODEL_WIDTH = 8192
ADAPTER_RANK = 16
STEPS = 4
ROWS_DEV = 128
SEG = 16
ADP_DEV = 64
CAP = 16
ROWS = 512
SEGMENTS = 32
ADAPTER_TOTAL = 256
N_DP = 4
N_TP = 4


def shared_table(key):
    return jax.random.permutation(key, ADAPTER_TOTAL).astype(jnp.int32)


def draw_adapter_store_index(key, part):
    return shared_table(key)


def draw_segment_adapter(key, part):
    table = shared_table(key)
    holder = jnp.argsort(table).astype(jnp.int32)
    key = jax.random.fold_in(key, 5)
    key_hot, key_order, key_other, key_local = jax.random.split(key, 4)
    count = STEPS * (ROWS_DEV // SEG)
    hot = jax.random.randint(key_hot, (N_DP,), 0, N_DP)
    scores = jax.random.randint(key_order, (N_DP, count), 0, 2 ** 20) * count + jnp.arange(count, dtype=jnp.int32)[None, :]
    ranks = jnp.argsort(jnp.argsort(scores, axis=1), axis=1)
    is_hot = ranks < CAP
    offset = jax.random.randint(key_other, (N_DP, count), 1, N_DP)
    owners = jnp.where(is_hot, hot[:, None], (hot[:, None] + offset) % N_DP)
    local_slot = jax.random.randint(key_local, (N_DP, count), 0, ADP_DEV)
    adapters = holder[owners * ADP_DEV + local_slot]
    adapters = adapters.reshape(N_DP, STEPS, ROWS_DEV // SEG).transpose(1, 0, 2)
    return adapters.reshape(STEPS, SEGMENTS).astype(jnp.int32)


def draw_segment_live_rows(key, part):
    key = jax.random.fold_in(key, 7)
    key_len, key_full = jax.random.split(key)
    lengths = jax.random.randint(key_len, (STEPS, N_DP, ROWS_DEV // SEG), 1, SEG + 1)
    chosen = jax.random.randint(key_full, (STEPS, N_DP, 1), 0, ROWS_DEV // SEG)
    full = jnp.arange(ROWS_DEV // SEG, dtype=jnp.int32)[None, None, :] == chosen
    lengths = jnp.where(full, SEG, lengths)
    return lengths.reshape(STEPS, SEGMENTS).astype(jnp.int32)


def spiked(drawn, own_key, source, target, blocks, factor):
    def block_of(dim):
        return (jnp.arange(drawn.shape[dim]) // (drawn.shape[dim] // blocks)).reshape((-1,) + (1,) * (drawn.ndim - 1 - dim))

    near = jax.random.permutation(own_key, blocks)[block_of(target)]
    other_side = (block_of(target) + blocks // 2) % blocks
    return jnp.where((block_of(source) == near) | (block_of(source) == other_side), factor * drawn, drawn)


def steps_of(rng, extent, pieces, smallest, largest):
    loudness, own = 1.0, jax.random.fold_in(rng, 6)
    for dim, parts in pieces:
        steps = jnp.exp(jax.random.uniform(jax.random.fold_in(own, dim), (parts,), jnp.float32, smallest / len(pieces), largest / len(pieces)))
        loudness = loudness * jnp.repeat(steps, extent[dim] // parts).reshape([-1 if axis == dim else 1 for axis in range(len(extent))])
    return loudness


def gaussian(own_key, shape, deviation, bound, cuts=(), held_as=jnp.bfloat16):
    result = jax.random.normal(own_key, shape, jnp.float32) * deviation
    if len(cuts) > 0:
        result = steps_of(own_key, shape, cuts, -0.22, 0.18) * result
    return jnp.clip(result, min=-bound, max=bound).astype(held_as)


def gaussian_with(key, extent, spread, limit, cuts, heavy, kind=jnp.bfloat16):
    result = spread * jax.random.normal(key, extent, jnp.float32)
    if cuts:
        result = result * steps_of(key, extent, cuts, -0.22, 0.18)
    return jnp.clip(spiked(result, jax.random.fold_in(key, 3), *heavy), -limit, limit).astype(kind)


def setup_inputs(seed: int = 0, part: int = 0) -> dict:
    seeds = jax.random.split(jax.random.key(seed), 8)
    own_keys = jax.random.split(jax.random.fold_in(seeds[7], part), 8)
    return {
        "attention_output": gaussian(own_keys[0], (STEPS, ROWS, MODEL_WIDTH), 1.0, 6.0, ((1, 4), (2, 4))),
        "output_projection_weight": gaussian_with(seeds[1], (MODEL_WIDTH, MODEL_WIDTH), MODEL_WIDTH ** -0.5, 0.09375, ((0, 4),), (0, 1, 4, 2.0)),
        "shrink_matrix_store": gaussian(seeds[2], (ADAPTER_TOTAL, ADAPTER_RANK, MODEL_WIDTH), MODEL_WIDTH ** -0.5, 0.0625, ((0, 4), (2, 4))),
        "expand_matrix_store": gaussian(seeds[3], (ADAPTER_TOTAL, ADAPTER_RANK, MODEL_WIDTH), ADAPTER_RANK ** -0.5, 1.5, ((0, 4), (2, 4))),
        "segment_adapter": draw_segment_adapter(jax.random.fold_in(jax.random.fold_in(seeds[7], part), 71), part),
        "segment_live_rows": draw_segment_live_rows(jax.random.fold_in(jax.random.fold_in(seeds[7], part), 71), part),
        "adapter_store_index": draw_adapter_store_index(jax.random.fold_in(jax.random.fold_in(seeds[7], part), 71), part),
    }


def reference(attention_output, output_projection_weight, shrink_matrix_store, expand_matrix_store, segment_adapter, segment_live_rows, adapter_store_index):
    store_location = adapter_store_index[segment_adapter]
    live = (jnp.arange(SEG, dtype=jnp.int32)[None, None, :] < segment_live_rows[:, :, None]).astype(jnp.float32)
    block = MODEL_WIDTH // N_TP
    results = []
    for decode_step_index in range(STEPS):
        rows_in = attention_output[decode_step_index]
        base = jnp.zeros((ROWS, MODEL_WIDTH), jnp.float32)
        for shard in range(N_TP):
            partial_sum = jnp.dot(rows_in[:, shard * block:(shard + 1) * block], output_projection_weight[shard * block:(shard + 1) * block, :], preferred_element_type=jnp.float32)
            base = base + partial_sum.astype(jnp.bfloat16).astype(jnp.float32)
        selected_shrink = shrink_matrix_store[store_location[decode_step_index]].astype(jnp.float32)
        selected_expand = expand_matrix_store[store_location[decode_step_index]].astype(jnp.float32)
        grouped = rows_in.reshape(SEGMENTS, SEG, MODEL_WIDTH).astype(jnp.float32)
        shrink = jnp.einsum("gsd,grd->gsr", grouped, selected_shrink, precision=lax.Precision.HIGHEST)
        shrink = shrink * live[decode_step_index][:, :, None]
        delta = jnp.einsum("gsr,grd->gsd", shrink, selected_expand, precision=lax.Precision.HIGHEST)
        results.append((base + delta.reshape(ROWS, MODEL_WIDTH)).astype(jnp.bfloat16))
    return jnp.stack(results)
```

```python
import jax
import jax.numpy as jnp
from jax import lax
from jax.sharding import PartitionSpec as P

GROUPS = (96, 96)


def per_device(
    attention_output,
    output_projection_weight,
    shrink_matrix_store,
    expand_matrix_store,
    segment_adapter,
    segment_live_rows,
    adapter_store_index,
):
    steps, rows_dev, width = attention_output.shape
    seg_count = segment_adapter.shape[1]
    seg_len = rows_dev // seg_count
    store, rank, _ = shrink_matrix_store.shape
    n_dp = lax.axis_size("dp")
    rows = steps * rows_dev
    count = steps * seg_count
    most = (count // 2) * seg_len
    base_rows = sum(GROUPS)

    x = attention_output.reshape(rows, width)
    shrink_store = shrink_matrix_store.reshape(store * rank, width)
    expand_store = expand_matrix_store.reshape(store * rank, width)

    ids = segment_adapter.reshape(count)
    lives = segment_live_rows.reshape(count)
    table = jnp.arange(adapter_store_index.shape[0], dtype=jnp.int32)
    position = jnp.sum(
        jnp.where(ids[:, None] == table[None, :], adapter_store_index[None, :], 0), axis=1
    )
    owner = position // store
    slot = position % store
    order = jnp.arange(count, dtype=jnp.int32)
    before = (owner[:, None] == owner[None, :]) & (order[:, None] > order[None, :])
    start = jnp.sum(jnp.where(before, lives[None, :], 0), axis=1)
    lane = jnp.arange(seg_len, dtype=jnp.int32)
    live = lane[None, :] < lives[:, None]
    key = jnp.where(live, (owner * most + start)[:, None] + lane[None, :], -1).reshape(rows)
    row_slot = jnp.broadcast_to(slot[:, None], (count, seg_len)).reshape(rows)

    owners = jnp.arange(n_dp, dtype=jnp.int32)
    totals = jnp.sum(jnp.where(owner[None, :] == owners[:, None], lives[None, :], 0), axis=1)
    fullest = lax.pmax(jnp.max(totals), ("rep", "dp"))

    def wanted(low, size):
        target = (owners * most)[:, None] + low + jnp.arange(size, dtype=jnp.int32)[None, :]
        return target.reshape(n_dp * size)

    def a2a(v):
        return lax.all_to_all(v, "dp", split_axis=0, concat_axis=0, tiled=True)

    def sum_tp(v):
        n = lax.axis_size("tp")
        if n & (n - 1):
            return lax.psum(v, "tp")
        bit = 1
        while bit < n:
            v = v + lax.ppermute(v, "tp", [(i, i ^ bit) for i in range(n)])
            bit *= 2
        return v

    def send_slots(low, size):
        hit = wanted(low, size)[:, None] == key[None, :]
        sent = jnp.max(jnp.where(hit, row_slot[None, :], -1), axis=1)
        return a2a(sent.reshape(n_dp, 1, size)).reshape(n_dp * size)

    def send_rows(low, size):
        pick = (wanted(low, size)[:, None] == key[None, :]).astype(jnp.bfloat16)
        packed = jnp.dot(pick, x, preferred_element_type=jnp.float32).astype(jnp.bfloat16)
        return a2a(packed.reshape(n_dp, size, width)).reshape(n_dp * size, width)

    def answer(got, slots):
        n = got.shape[0]
        scores = lax.dot_general(
            shrink_store, got, (((1,), (1,)), ((), ())), preferred_element_type=jnp.float32
        ).reshape(store, rank, n)
        own = jnp.arange(store, dtype=jnp.int32)[:, None, None] == slots[None, None, :]
        part = jnp.sum(jnp.where(own, scores, 0.0), axis=0)
        shrink = sum_tp(part).astype(jnp.bfloat16)
        spread = jnp.where(own, shrink[None], jnp.bfloat16(0)).reshape(store * rank, n)
        delta = lax.dot_general(
            spread, expand_store, (((0,), (0,)), ((), ())), preferred_element_type=jnp.float32
        ).astype(jnp.bfloat16)
        return a2a(delta.reshape(n_dp, n // n_dp, width)).reshape(n, width)

    def place(low, size, back):
        put = (key[:, None] == wanted(low, size)[None, :]).astype(jnp.bfloat16)
        return jnp.dot(put, back, preferred_element_type=jnp.float32)

    slots_all = send_slots(0, base_rows).reshape(n_dp, base_rows)
    lows = [sum(GROUPS[:i]) for i in range(len(GROUPS))]
    got = [send_rows(low, size) for low, size in zip(lows, GROUPS)]

    bases = []
    for t in range(steps):
        part = jnp.dot(
            attention_output[t], output_projection_weight, preferred_element_type=jnp.float32
        )
        bases.append(
            lax.psum_scatter(part.astype(jnp.bfloat16), "tp", scatter_dimension=1, tiled=True)
        )

    back = []
    for low, size, g in zip(lows, GROUPS, got):
        back.append(answer(g, slots_all[:, low:low + size].reshape(n_dp * size)))

    base = jnp.concatenate(bases, axis=0)
    total = base.astype(jnp.float32)
    for low, size, b in zip(lows, GROUPS, back):
        total = total + place(low, size, b)

    def rest(total):
        size = most - base_rows
        slots = send_slots(base_rows, size)
        b = answer(send_rows(base_rows, size), slots)
        return (total + place(base_rows, size, b)).astype(jnp.bfloat16)

    out = lax.cond(fullest > base_rows, rest, lambda v: v.astype(jnp.bfloat16), total)
    return out.reshape(steps, rows_dev, width)


def solution(mesh):
    return jax.shard_map(
        per_device,
        mesh=mesh,
        in_specs=(
            P(None, ("rep", "dp"), "tp"),
            P("tp", None),
            P("dp", None, "tp"),
            P("dp", None, "tp"),
            P(None, ("rep", "dp")),
            P(None, ("rep", "dp")),
            P("rep"),
        ),
        out_specs=P(None, ("rep", "dp"), "tp"),
        check_vma=False,
    )
```

```python
import functools

import jax
import jax.numpy as jnp
from jax import lax
from jax.experimental import pallas as pl
from jax.experimental.pallas import tpu as pltpu
from jax.sharding import PartitionSpec as P

NEAR = 208
OWN = 72
SHARED = 64
ROUND = 64
VMEM = 48 * 2**20


def group_of(shape):
    return lax.broadcasted_iota(jnp.int32, shape, 1) // 16


def row_of(shape):
    return lax.broadcasted_iota(jnp.int32, shape, 0) % 8


def fold(v):
    for shift in (64, 32, 16):
        v = v + pltpu.roll(v, shift, axis=1)
    return v


def score_kernel(sizes, *refs):
    m = len(sizes)
    slots, got, a_ref, out_ref, acc = refs[:m], refs[m:2 * m], refs[2 * m], refs[2 * m + 1], refs[2 * m + 2]
    g = pl.program_id(0)
    per = a_ref.shape[0] // 16

    @pl.when(g == 0)
    def _():
        acc[...] = jnp.zeros_like(acc)

    off = 0
    for i, n in enumerate(sizes):
        s = lax.dot_general(
            got[i][...], a_ref[...], (((1,), (1,)), ((), ())), preferred_element_type=jnp.float32
        )
        s = jnp.where(group_of(s.shape) + g * per == slots[i][...], s, 0.0)
        v = s[:, :128]
        for c in range(128, s.shape[1], 128):
            v = v + s[:, c:c + 128]
        acc[off:off + n, :] += v
        off += n

    @pl.when(g == pl.num_programs(0) - 1)
    def _():
        off = 0
        for n in sizes:
            v = fold(acc[off:off + n, :])
            v = jnp.where(group_of(v.shape) == row_of(v.shape), v, 0.0)
            out_ref[off // 8:(off + n) // 8, :] = jnp.sum(v.reshape(n // 8, 8, 128), axis=1)
            off += n


def scores(slots, got, store):
    sizes = tuple(v.shape[0] for v in got)
    total, width = sum(sizes), store.shape[1]
    blk = 256
    whole = lambda v: pl.BlockSpec(v.shape, lambda g: (0, 0))
    return pl.pallas_call(
        functools.partial(score_kernel, sizes),
        grid=(store.shape[0] // blk,),
        in_specs=[whole(v) for v in slots] + [whole(v) for v in got]
        + [pl.BlockSpec((blk, width), lambda g: (g, 0))],
        out_specs=pl.BlockSpec((total // 8, 128), lambda g: (0, 0)),
        out_shape=jax.ShapeDtypeStruct((total // 8, 128), jnp.float32),
        scratch_shapes=[pltpu.VMEM((total, 128), jnp.float32)],
        compiler_params=pltpu.CompilerParams(vmem_limit_bytes=VMEM),
        cost_estimate=pl.CostEstimate(
            flops=2 * total * width * store.shape[0],
            bytes_accessed=2 * width * (total + store.shape[0]),
            transcendentals=0,
        ),
        name="scores",
    )(*slots, *got, store)


def delta_kernel(sizes, *refs):
    m = len(sizes)
    slots, packed, b_ref, outs, spread = refs[:m], refs[m], refs[m + 1], refs[m + 2:2 * m + 2], refs[2 * m + 2:]

    @pl.when(pl.program_id(0) == 0)
    def _():
        off = 0
        for i, n in enumerate(sizes):
            v = packed[off // 8:(off + n) // 8, :]
            v = jnp.broadcast_to(v[:, None, :], (n // 8, 8, 128)).reshape(n, 128)
            group = group_of(v.shape)
            v = fold(jnp.where(group == row_of(v.shape), v, 0.0))
            for c in range(b_ref.shape[0] // 128):
                hit = group + c * 8 == slots[i][...]
                spread[i][:, c * 128:(c + 1) * 128] = jnp.where(hit, v, 0.0).astype(jnp.bfloat16)
            off += n

    for i in range(m):
        outs[i][...] = jnp.dot(
            spread[i][...], b_ref[...], preferred_element_type=jnp.float32
        ).astype(jnp.bfloat16)


def deltas(slots, packed, store):
    sizes = tuple(v.shape[0] for v in slots)
    depth, width = store.shape
    cols = width // 4
    whole = lambda v: pl.BlockSpec(v.shape, lambda g: (0, 0))
    return pl.pallas_call(
        functools.partial(delta_kernel, sizes),
        grid=(width // cols,),
        in_specs=[whole(v) for v in slots] + [whole(packed)]
        + [pl.BlockSpec((depth, cols), lambda g: (0, g))],
        out_specs=[pl.BlockSpec((n, cols), lambda g: (0, g)) for n in sizes],
        out_shape=[jax.ShapeDtypeStruct((n, width), jnp.bfloat16) for n in sizes],
        scratch_shapes=[pltpu.VMEM((n, depth), jnp.bfloat16) for n in sizes],
        compiler_params=pltpu.CompilerParams(vmem_limit_bytes=VMEM),
        cost_estimate=pl.CostEstimate(
            flops=2 * sum(sizes) * width * depth,
            bytes_accessed=2 * width * (sum(sizes) + depth),
            transcendentals=0,
        ),
        name="deltas",
    )(*slots, packed, store)


def finish_kernel(m, a, row_ref, *refs):
    codes, back, adds, out_ref = refs[:m], refs[m:2 * m], refs[2 * m:2 * m + a], refs[2 * m + a]
    total = adds[0][...].astype(jnp.float32)
    for v in adds[1:]:
        total += v[...].astype(jnp.float32)
    for code, b in zip(codes, back):
        put = jnp.where(row_ref[...] == code[...], 1.0, 0.0).astype(jnp.bfloat16)
        total += jnp.dot(put, b[...], preferred_element_type=jnp.float32)
    out_ref[...] = total.astype(out_ref.dtype)


def finish(row_code, codes, back, adds):
    rows, width = adds[0].shape
    cols = width // 4
    whole = lambda v: pl.BlockSpec(v.shape, lambda g: (0, 0))
    part = lambda v: pl.BlockSpec((v.shape[0], cols), lambda g: (0, g))
    return pl.pallas_call(
        functools.partial(finish_kernel, len(codes), len(adds)),
        grid=(width // cols,),
        in_specs=[whole(row_code)] + [whole(v) for v in codes] + [part(v) for v in back] + [part(v) for v in adds],
        out_specs=pl.BlockSpec((rows, cols), lambda g: (0, g)),
        out_shape=jax.ShapeDtypeStruct((rows, width), jnp.bfloat16),
        compiler_params=pltpu.CompilerParams(vmem_limit_bytes=VMEM),
        name="finish",
    )(row_code, *codes, *back, *adds)


def per_device(
    attention_output,
    output_projection_weight,
    shrink_matrix_store,
    expand_matrix_store,
    segment_adapter,
    segment_live_rows,
    adapter_store_index,
):
    steps, rows_dev, width = attention_output.shape
    seg_count = segment_adapter.shape[1]
    seg_len = rows_dev // seg_count
    store, rank, _ = shrink_matrix_store.shape
    n_rep, n_dp, n_tp = (lax.axis_size(a) for a in ("rep", "dp", "tp"))
    me = lax.axis_index("dp")
    rows = steps * rows_dev
    count = steps * seg_count
    big = 2 * rows

    x = attention_output.reshape(rows, width)
    shrink_store = shrink_matrix_store.reshape(store * rank, width)
    expand_store = expand_matrix_store.reshape(store * rank, width)
    far = range(2, n_dp)

    def swap(v, axis, k):
        n = lax.axis_size(axis)
        return lax.ppermute(v, axis, [(i, i ^ k) for i in range(n)])

    def butterfly(v, axis, op):
        k = 1
        while k < lax.axis_size(axis):
            v = op(v, swap(v, axis, k))
            k *= 2
        return v

    ids = segment_adapter.reshape(count)
    lives = segment_live_rows.reshape(count)
    index = jnp.arange(adapter_store_index.shape[0], dtype=jnp.int32)
    position = jnp.sum(
        jnp.where(ids[:, None] == index[None, :], adapter_store_index[None, :], 0), axis=1
    )
    table = jnp.stack([position, lives])
    tables = [table] + [swap(table, "dp", k) for k in range(1, n_dp)]

    order = jnp.arange(count, dtype=jnp.int32)

    def layout(k):
        pos, alive = tables[k][0], tables[k][1]
        dist = (pos // store) ^ (me ^ k)
        before = (dist[:, None] == dist[None, :]) & (order[:, None] > order[None, :])
        start = jnp.sum(jnp.where(before, alive[None, :], 0), axis=1)
        totals = [jnp.sum(jnp.where(dist == j, alive, 0)) for j in range(n_dp)]
        held, over = [None, jnp.int32(NEAR)], [None, None]
        for j in range(2, n_dp, 2):
            extra = jnp.maximum(totals[j] - OWN, 0)
            over += [extra, extra]
            held += [jnp.int32(OWN + 2 * SHARED), OWN + jnp.maximum(2 * SHARED - extra, 0)]
        left = functools.reduce(jnp.maximum, [totals[j] - held[j] for j in range(1, n_dp)])
        return dict(dist=dist, slot=pos % store, alive=alive, start=start, held=held, over=over, left=left)

    lay = [layout(k) for k in range(n_dp)]

    def near():
        return big + jnp.arange(NEAR, dtype=jnp.int32)

    def own(j):
        return j * big + jnp.arange(OWN, dtype=jnp.int32)

    def shared(k, j):
        f = jnp.arange(SHARED, dtype=jnp.int32) + (j % 2) * SHARED
        even, over = j - j % 2, lay[k]["over"][j]
        return OWN + jnp.where(f < over, even * big + f, (even + 1) * big + f - over)

    def late(k, j, low):
        return j * big + lay[k]["held"][j] + low + jnp.arange(ROUND, dtype=jnp.int32)

    def slots_of(k, code):
        seg = lay[k]["dist"] * big + lay[k]["start"]
        hit = (code[:, None] >= seg[None, :]) & (code[:, None] < (seg + lay[k]["alive"])[None, :])
        hit = hit & (lay[k]["dist"] == k)[None, :]
        return jnp.max(jnp.where(hit, lay[k]["slot"][None, :], -1), axis=1, keepdims=True)

    lane = jnp.arange(seg_len, dtype=jnp.int32)
    live = lane[None, :] < lives[:, None]
    row_code = (lay[0]["dist"] * big + lay[0]["start"])[:, None] + lane[None, :]
    row_code = jnp.where(live, row_code, -1).reshape(rows)
    self_slots = jnp.where(live & (lay[0]["dist"] == 0)[:, None], lay[0]["slot"][:, None], -1).reshape(rows, 1)

    def pack(code):
        pick = (code[:, None] == row_code[None, :]).astype(jnp.bfloat16)
        return jnp.dot(pick, x, preferred_element_type=jnp.float32).astype(jnp.bfloat16)

    def answer(slots, got):
        part = butterfly(scores(slots, got, shrink_store), "tp", jnp.add)
        return deltas(slots, part, expand_store)

    out_shared = {j: pack(shared(0, j)) for j in far}
    out_own = {j: pack(own(j)) for j in far}
    out_near = pack(near())
    weight, out_shared, out_own, out_near = lax.optimization_barrier(
        (output_projection_weight, out_shared, out_own, out_near)
    )
    in_shared = {j: swap(out_shared[j], "dp", j) for j in far}
    in_own = {j: swap(out_own[j], "dp", j) for j in far}
    in_near = swap(out_near, "dp", 1)
    in_relay = {j: swap(in_shared[j], "dp", 1) for j in far}

    at = lax.axis_index("tp")
    cols = weight.shape[1] // n_tp

    def share(k):
        w = lax.dynamic_slice_in_dim(weight, (at ^ k) * cols, cols, axis=1)
        return jnp.dot(x, w, preferred_element_type=jnp.float32).astype(jnp.bfloat16)

    held = {k: [share(k)] for k in reversed(range(n_tp))}
    bit = 1
    while bit < n_tp:
        for k in sorted((k for k in held if k & bit), reverse=True):
            v = held.pop(k)
            if len(v) > 1:
                v = [functools.reduce(jnp.add, [u.astype(jnp.float32) for u in v]).astype(jnp.bfloat16)]
            held[k ^ bit].append(swap(v[0], "tp", bit))
        bit *= 2
    base = held[0]

    (self_delta,) = answer([self_slots], [x])

    slots_s = [slots_of(j, shared(j, j)) for j in far]
    slots_r = [slots_of(j ^ 1, shared(j ^ 1, j)) for j in far]
    both = answer(slots_s + slots_r, [in_shared[j] for j in far] + [in_relay[j] for j in far])
    back_shared = []
    for i, j in enumerate(far):
        v = both[i] + swap(both[len(far) + i], "dp", 1)
        back_shared.append(swap(v, "dp", j))

    slots_o = [slots_of(j, own(j)) for j in far] + [slots_of(1, near())]
    direct = answer(slots_o, [in_own[j] for j in far] + [in_near])
    back_own = [swap(direct[i], "dp", j) for i, j in enumerate(far)]
    back_near = swap(direct[-1], "dp", 1)

    codes = [shared(0, j) for j in far] + [own(j) for j in far] + [near()]
    codes = [v.reshape(1, -1) for v in codes]
    back = back_shared + back_own + [back_near]
    adds = base + [self_delta]

    left = functools.reduce(jnp.maximum, [v["left"] for v in lay])
    left = butterfly(left.reshape(1), "rep", jnp.maximum)[0]

    def rest(args):
        row_code, codes, back, adds = args

        def body(i, extra):
            low = i * ROUND
            got = [swap(pack(late(0, j, low)), "dp", j) for j in range(1, n_dp)]
            slots = [slots_of(j, late(j, j, low)) for j in range(1, n_dp)]
            for j, v in zip(range(1, n_dp), answer(slots, got)):
                put = (row_code == late(0, j, low)[None, :]).astype(jnp.bfloat16)
                extra = extra + jnp.dot(put, swap(v, "dp", j), preferred_element_type=jnp.float32)
            return extra

        rounds = (left + ROUND - 1) // ROUND
        extra = lax.fori_loop(0, rounds, body, jnp.zeros((rows, width), jnp.float32))
        return finish(row_code, codes, back, adds + [extra])

    out = lax.cond(left > 0, rest, lambda args: finish(*args), (row_code.reshape(rows, 1), codes, back, adds))
    return out.reshape(steps, rows_dev, width)


def solution(mesh):
    return jax.shard_map(
        per_device,
        mesh=mesh,
        in_specs=(
            P(None, ("rep", "dp"), "tp"),
            P("tp", None),
            P("dp", None, "tp"),
            P("dp", None, "tp"),
            P(None, ("rep", "dp")),
            P(None, ("rep", "dp")),
            P("rep"),
        ),
        out_specs=P(None, ("rep", "dp"), "tp"),
        check_vma=False,
    )
```

```python
import functools

import jax
import jax.numpy as jnp
from jax import lax
from jax.experimental import pallas as pl
from jax.experimental.pallas import tpu as pltpu
from jax.sharding import PartitionSpec as P

NEAR = 208
OWN = 72
SHARED = 64
ROUND = 64
VMEM = 48 * 2**20
FREE = pl.CostEstimate(flops=0, bytes_accessed=0, transcendentals=0)


def group_of(shape):
    return lax.broadcasted_iota(jnp.int32, shape, 1) // 16


def row_of(shape):
    return lax.broadcasted_iota(jnp.int32, shape, 0) % 8


def fold(v):
    for shift in (64, 32, 16):
        v = v + pltpu.roll(v, shift, axis=1)
    return v


def score_kernel(sizes, *refs):
    m = len(sizes)
    slots, got, a_ref, out_ref, acc = refs[:m], refs[m:2 * m], refs[2 * m], refs[2 * m + 1], refs[2 * m + 2]
    g = pl.program_id(0)
    per = a_ref.shape[0] // 16

    @pl.when(g == 0)
    def _():
        acc[...] = jnp.zeros_like(acc)

    off = 0
    for i, n in enumerate(sizes):
        s = lax.dot_general(
            got[i][...], a_ref[...], (((1,), (1,)), ((), ())), preferred_element_type=jnp.float32
        )
        s = jnp.where(group_of(s.shape) + g * per == slots[i][...], s, 0.0)
        v = s[:, :128]
        for c in range(128, s.shape[1], 128):
            v = v + s[:, c:c + 128]
        acc[off:off + n, :] += v
        off += n

    @pl.when(g == pl.num_programs(0) - 1)
    def _():
        off = 0
        for n in sizes:
            v = fold(acc[off:off + n, :])
            v = jnp.where(group_of(v.shape) == row_of(v.shape), v, 0.0)
            out_ref[off // 8:(off + n) // 8, :] = jnp.sum(v.reshape(n // 8, 8, 128), axis=1)
            off += n


def scores(slots, got, store):
    sizes = tuple(v.shape[0] for v in got)
    total, width = sum(sizes), store.shape[1]
    blk = 256
    whole = lambda v: pl.BlockSpec(v.shape, lambda g: (0, 0))
    return pl.pallas_call(
        functools.partial(score_kernel, sizes),
        grid=(store.shape[0] // blk,),
        in_specs=[whole(v) for v in slots] + [whole(v) for v in got]
        + [pl.BlockSpec((blk, width), lambda g: (g, 0))],
        out_specs=pl.BlockSpec((total // 8, 128), lambda g: (0, 0)),
        out_shape=jax.ShapeDtypeStruct((total // 8, 128), jnp.float32),
        scratch_shapes=[pltpu.VMEM((total, 128), jnp.float32)],
        compiler_params=pltpu.CompilerParams(vmem_limit_bytes=VMEM),
        cost_estimate=FREE,
        name="scores",
    )(*slots, *got, store)


def delta_kernel(sizes, *refs):
    m = len(sizes)
    slots, packed, b_ref, outs, spread = refs[:m], refs[m], refs[m + 1], refs[m + 2:2 * m + 2], refs[2 * m + 2:]

    @pl.when(pl.program_id(0) == 0)
    def _():
        off = 0
        for i, n in enumerate(sizes):
            v = packed[off // 8:(off + n) // 8, :]
            v = jnp.broadcast_to(v[:, None, :], (n // 8, 8, 128)).reshape(n, 128)
            group = group_of(v.shape)
            v = fold(jnp.where(group == row_of(v.shape), v, 0.0))
            for c in range(b_ref.shape[0] // 128):
                hit = group + c * 8 == slots[i][...]
                spread[i][:, c * 128:(c + 1) * 128] = jnp.where(hit, v, 0.0).astype(jnp.bfloat16)
            off += n

    for i in range(m):
        outs[i][...] = jnp.dot(
            spread[i][...], b_ref[...], preferred_element_type=jnp.float32
        ).astype(jnp.bfloat16)


def deltas(slots, packed, store):
    sizes = tuple(v.shape[0] for v in slots)
    depth, width = store.shape
    cols = width // 4
    whole = lambda v: pl.BlockSpec(v.shape, lambda g: (0, 0))
    return pl.pallas_call(
        functools.partial(delta_kernel, sizes),
        grid=(width // cols,),
        in_specs=[whole(v) for v in slots] + [whole(packed)]
        + [pl.BlockSpec((depth, cols), lambda g: (0, g))],
        out_specs=[pl.BlockSpec((n, cols), lambda g: (0, g)) for n in sizes],
        out_shape=[jax.ShapeDtypeStruct((n, width), jnp.bfloat16) for n in sizes],
        scratch_shapes=[pltpu.VMEM((n, depth), jnp.bfloat16) for n in sizes],
        compiler_params=pltpu.CompilerParams(vmem_limit_bytes=VMEM),
        cost_estimate=FREE,
        name="deltas",
    )(*slots, packed, store)


def finish_kernel(m, a, row_ref, *refs):
    codes, back, adds, out_ref = refs[:m], refs[m:2 * m], refs[2 * m:2 * m + a], refs[2 * m + a]
    total = adds[0][...].astype(jnp.float32)
    for v in adds[1:]:
        total += v[...].astype(jnp.float32)
    for code, b in zip(codes, back):
        put = jnp.where(row_ref[...] == code[...], 1.0, 0.0).astype(jnp.bfloat16)
        total += jnp.dot(put, b[...], preferred_element_type=jnp.float32)
    out_ref[...] = total.astype(out_ref.dtype)


def finish(row_code, codes, back, adds):
    rows, width = adds[0].shape
    cols = width // 4
    whole = lambda v: pl.BlockSpec(v.shape, lambda g: (0, 0))
    part = lambda v: pl.BlockSpec((v.shape[0], cols), lambda g: (0, g))
    return pl.pallas_call(
        functools.partial(finish_kernel, len(codes), len(adds)),
        grid=(width // cols,),
        in_specs=[whole(row_code)] + [whole(v) for v in codes] + [part(v) for v in back] + [part(v) for v in adds],
        out_specs=pl.BlockSpec((rows, cols), lambda g: (0, g)),
        out_shape=jax.ShapeDtypeStruct((rows, width), jnp.bfloat16),
        compiler_params=pltpu.CompilerParams(vmem_limit_bytes=VMEM),
        name="finish",
    )(row_code, *codes, *back, *adds)


def column(row):
    n = row.shape[1]
    eye = lax.broadcasted_iota(jnp.int32, (n, n), 0) == lax.broadcasted_iota(jnp.int32, (n, n), 1)
    return jnp.sum(jnp.where(eye, jnp.broadcast_to(row, (n, n)), 0), axis=1, keepdims=True)


def row(col):
    n = col.shape[0]
    eye = lax.broadcasted_iota(jnp.int32, (n, n), 0) == lax.broadcasted_iota(jnp.int32, (n, n), 1)
    return jnp.sum(jnp.where(eye, jnp.broadcast_to(col, (n, n)), 0), axis=0, keepdims=True)


def segments(pos, alive, device, shift):
    n = pos.shape[1]
    dist = (pos >> shift) ^ device
    i = lax.broadcasted_iota(jnp.int32, (n, n), 0)
    j = lax.broadcasted_iota(jnp.int32, (n, n), 1)
    before = (column(dist) == dist) & (i < j)
    start = jnp.sum(jnp.where(before, column(alive), 0), axis=0, keepdims=True)
    return dist, start


def total(dist, alive, j):
    return jnp.sum(jnp.where(dist == j, alive, 0), axis=1, keepdims=True)


def over_of(dist, alive, j):
    return jnp.maximum(total(dist, alive, j - j % 2) - OWN, 0)


def iota_of(n, axis):
    return lax.broadcasted_iota(jnp.int32, (n, 1) if axis == 0 else (1, n), axis)


def near_code(big, axis):
    return big + iota_of(NEAR, axis)


def own_code(big, j, axis):
    return j * big + iota_of(OWN, axis)


def shared_code(big, j, over, axis):
    f = iota_of(SHARED, axis) + (j % 2) * SHARED
    even = j - j % 2
    return OWN + jnp.where(f < over, even * big + f, (even + 1) * big + f - over)


def far_code(big, j, over, axis):
    f = iota_of(SHARED + OWN, axis)
    g = f + (j % 2) * SHARED
    even = j - j % 2
    code = OWN + jnp.where(g < over, even * big + g, (even + 1) * big + g - over)
    return jnp.where(f < SHARED, code, j * big + f - SHARED)


def pack_kernel(n_dp, seg_len, shift, me_ref, ids_ref, lives_ref, index_ref, x_ref,
                table_ref, row_ref, self_ref, *outs):
    me = me_ref[0]
    count, rows = ids_ref.shape[1], x_ref.shape[0]
    big = 2 * rows
    lives = lives_ref[...]
    index = index_ref[...]
    hit = column(ids_ref[...]) == lax.broadcasted_iota(jnp.int32, (count, index.shape[1]), 1)
    pos = row(jnp.sum(jnp.where(hit, index, 0), axis=1, keepdims=True))
    table_ref[0:1, :] = pos
    table_ref[1:2, :] = lives
    dist, start = segments(pos, lives, me, shift)
    code = dist * big + start
    slot = jnp.where(dist == 0, pos & ((1 << shift) - 1), -1)

    def spread(value, axis):
        shape = (count, rows) if axis == 1 else (rows, count)
        r = lax.broadcasted_iota(jnp.int32, shape, axis)
        seg = lax.broadcasted_iota(jnp.int32, shape, 1 - axis)
        v = column(value) if axis == 1 else value
        return jnp.sum(jnp.where(r // seg_len == seg, v, 0), axis=1 - axis, keepdims=True)

    def rows_code(axis):
        lane = iota_of(rows, axis) % seg_len
        return jnp.where(lane < spread(lives, axis), spread(code, axis) + lane, -1)

    by_row = rows_code(0)
    row_ref[...] = by_row
    self_ref[...] = jnp.where(by_row >= 0, spread(slot, 0), -1)
    by_lane = rows_code(1)

    far = range(2, n_dp)
    codes = [far_code(big, j, over_of(dist, lives, j), 0) for j in far] + [near_code(big, 0)]
    m = len(codes)
    for c, out in zip(codes, outs[:m]):
        pick = jnp.where(c == by_lane, 1.0, 0.0).astype(jnp.bfloat16)
        out[...] = jnp.dot(pick, x_ref[...], preferred_element_type=jnp.float32).astype(jnp.bfloat16)
    lanes = [shared_code(big, j, over_of(dist, lives, j), 1) for j in far]
    lanes += [own_code(big, j, 1) for j in far] + [near_code(big, 1)]
    for c, out in zip(lanes, outs[m:]):
        out[...] = c


def vmem(count):
    return [pl.BlockSpec(memory_space=pltpu.VMEM) for _ in range(count)]


def packs(me, ids, lives, index, x, n_dp, seg_len, shift):
    count, (rows, width) = ids.shape[1], x.shape
    sizes = [SHARED + OWN] * (n_dp - 2) + [NEAR]
    parts = [SHARED] * (n_dp - 2) + [OWN] * (n_dp - 2) + [NEAR]
    shapes = [((2, count), jnp.int32), ((rows, 1), jnp.int32), ((rows, 1), jnp.int32)]
    shapes += [((n, width), jnp.bfloat16) for n in sizes] + [((1, n), jnp.int32) for n in parts]
    return pl.pallas_call(
        functools.partial(pack_kernel, n_dp, seg_len, shift),
        in_specs=[pl.BlockSpec(memory_space=pltpu.SMEM)] + vmem(4),
        out_specs=vmem(len(shapes)),
        out_shape=[jax.ShapeDtypeStruct(*v) for v in shapes],
        compiler_params=pltpu.CompilerParams(vmem_limit_bytes=VMEM),
        cost_estimate=FREE,
        name="pack",
    )(me, ids, lives, index, x)


def slots_kernel(n_dp, rows, shift, me_ref, *refs):
    tables, outs, left_ref = refs[:n_dp], refs[n_dp:-1], refs[-1]
    big = 2 * rows
    me = me_ref[0]
    plans, left = [], None
    for k in range(n_dp):
        pos, alive = tables[k][0:1, :], tables[k][1:2, :]
        dist, start = segments(pos, alive, me ^ k, shift)
        plans.append((pos, alive, dist, start))
        rest = [total(dist, alive, 1) - NEAR]
        for j in range(2, n_dp):
            held = OWN + 2 * SHARED if j % 2 == 0 else OWN + jnp.maximum(2 * SHARED - over_of(dist, alive, j), 0)
            rest.append(total(dist, alive, j) - held)
        for v in rest:
            left = v if left is None else jnp.maximum(left, v)
    left_ref[...] = left

    def slots_of(k, code, out):
        pos, alive, dist, start = plans[k]
        seg = dist * big + start
        hit = (code >= seg) & (code < seg + alive) & (dist == k)
        out[...] = jnp.max(jnp.where(hit, pos & ((1 << shift) - 1), -1), axis=1, keepdims=True)

    far = range(2, n_dp)
    over = [over_of(p[2], p[1], k) for k, p in enumerate(plans)]
    todo = [(j ^ 1, shared_code(big, j, over_of(plans[j ^ 1][2], plans[j ^ 1][1], j), 0)) for j in far]
    todo += [(j, shared_code(big, j, over[j], 0)) for j in far]
    todo += [(j, own_code(big, j, 0)) for j in far]
    todo += [(j, far_code(big, j, over[j], 0)) for j in far]
    todo += [(1, near_code(big, 0))]
    for (k, code), out in zip(todo, outs):
        slots_of(k, code, out)


def slots(me, tables, rows, shift):
    n_dp = len(tables)
    sizes = [n for n in (SHARED, SHARED, OWN, SHARED + OWN) for _ in range(2, n_dp)] + [NEAR]
    shapes = [(n, 1) for n in sizes] + [(1, 1)]
    return pl.pallas_call(
        functools.partial(slots_kernel, n_dp, rows, shift),
        in_specs=[pl.BlockSpec(memory_space=pltpu.SMEM)] + vmem(n_dp),
        out_specs=vmem(len(shapes)),
        out_shape=[jax.ShapeDtypeStruct(v, jnp.int32) for v in shapes],
        cost_estimate=FREE,
        name="slots",
    )(me, *tables)


def share_kernel(at_ref, x_ref, w_ref, *refs):
    v = jnp.dot(x_ref[...], w_ref[...], preferred_element_type=jnp.float32)
    for r in refs[:-1]:
        v += r[...].astype(jnp.float32)
    refs[-1][...] = v.astype(jnp.bfloat16)


def share(at, x, weight, cols, adds):
    rows, depth = x.shape
    tile = min(512, cols)
    part = pl.BlockSpec((rows, tile), lambda g, at: (0, g))
    return pl.pallas_call(
        share_kernel,
        grid_spec=pltpu.PrefetchScalarGridSpec(
            num_scalar_prefetch=1,
            grid=(cols // tile,),
            in_specs=[
                pl.BlockSpec((rows, depth), lambda g, at: (0, 0)),
                pl.BlockSpec((depth, tile), lambda g, at: (0, at[0] * (cols // tile) + g)),
            ] + [part] * len(adds),
            out_specs=part,
        ),
        out_shape=jax.ShapeDtypeStruct((rows, cols), jnp.bfloat16),
        compiler_params=pltpu.CompilerParams(vmem_limit_bytes=VMEM),
        cost_estimate=FREE,
        name="share",
    )(at, x, weight, *adds)


def per_device(
    attention_output,
    output_projection_weight,
    shrink_matrix_store,
    expand_matrix_store,
    segment_adapter,
    segment_live_rows,
    adapter_store_index,
):
    steps, rows_dev, width = attention_output.shape
    seg_count = segment_adapter.shape[1]
    seg_len = rows_dev // seg_count
    store, rank, _ = shrink_matrix_store.shape
    n_dp, n_tp = lax.axis_size("dp"), lax.axis_size("tp")
    me = lax.axis_index("dp").reshape(1)
    rows = steps * rows_dev
    count = steps * seg_count
    shift = store.bit_length() - 1
    big = 2 * rows
    far = range(2, n_dp)

    x = attention_output.reshape(rows, width)
    shrink_store = shrink_matrix_store.reshape(store * rank, width)
    expand_store = expand_matrix_store.reshape(store * rank, width)
    weight = output_projection_weight

    def swap(v, axis, k):
        n = lax.axis_size(axis)
        return lax.ppermute(v, axis, [(i, i ^ k) for i in range(n)])

    def butterfly(v, axis, op):
        k = 1
        while k < lax.axis_size(axis):
            v = op(v, swap(v, axis, k))
            k *= 2
        return v

    def answer(slots, parts, got):
        part = butterfly(scores(slots, got, shrink_store), "tp", jnp.add)
        return deltas(parts, part, expand_store)

    packed = list(packs(
        me,
        segment_adapter.reshape(1, count),
        segment_live_rows.reshape(1, count),
        adapter_store_index.reshape(1, -1),
        x, n_dp, seg_len, shift,
    ))
    table, row_code, self_slots = packed[:3]
    m = len(far)
    out_far, out_near, codes = packed[3:3 + m], packed[3 + m], packed[4 + m:]

    in_far = [swap(v, "dp", j) for v, j in zip(out_far, far)]
    in_near = swap(out_near, "dp", 1)
    tables = [table] + [swap(table, "dp", k) for k in range(1, n_dp)]

    at = lax.axis_index("tp").reshape(1)
    cols = weight.shape[1] // n_tp
    at, _ = lax.optimization_barrier((at, table))
    adds = {k: [] for k in range(n_tp)}
    bit = 1
    while bit < n_tp:
        for k in sorted((k for k in adds if k & bit), reverse=True):
            v = share(at ^ k, x, weight, cols, adds.pop(k))
            adds[k ^ bit].append(swap(v, "tp", bit))
        bit *= 2
    base = [share(at, x, weight, cols, adds[0][:1])] + adds[0][1:]

    found = list(slots(me, tables, rows, shift))
    left = butterfly(found[-1], "rep", jnp.maximum)[0, 0]
    relay_slots, shared_slots, own_slots, far_slots = (found[i * m:(i + 1) * m] for i in range(4))
    near_slots = found[4 * m]

    (self_delta,) = answer([self_slots], [self_slots], [x])
    base[0], self_delta, far_slots = lax.optimization_barrier((base[0], self_delta, far_slots))

    in_relay = [swap(v[:SHARED], "dp", 1) for v in in_far]
    split = [v for pair in zip(shared_slots, own_slots) for v in pair] + [near_slots]
    direct = answer(far_slots + [near_slots], split, in_far + [in_near])
    relayed = answer(relay_slots, relay_slots, in_relay)
    back_shared = [direct[2 * i] + swap(relayed[i], "dp", 1) for i in range(m)]
    back_shared = [swap(v, "dp", j) for v, j in zip(back_shared, far)]
    back_own = [swap(direct[2 * i + 1], "dp", j) for i, j in enumerate(far)]
    back_near = swap(direct[-1], "dp", 1)

    back = back_shared + back_own + [back_near]
    adds = base + [self_delta]

    def layout(k):
        pos, alive = tables[k][0], tables[k][1]
        dist = (pos >> shift) ^ (me[0] ^ k)
        order = jnp.arange(count, dtype=jnp.int32)
        before = (dist[:, None] == dist[None, :]) & (order[:, None] > order[None, :])
        start = jnp.sum(jnp.where(before, alive[None, :], 0), axis=1)
        held = [None, jnp.int32(NEAR)]
        for j in range(2, n_dp, 2):
            extra = jnp.maximum(jnp.sum(jnp.where(dist == j, alive, 0)) - OWN, 0)
            held += [jnp.int32(OWN + 2 * SHARED), OWN + jnp.maximum(2 * SHARED - extra, 0)]
        return dist, start, alive, pos & (store - 1), held

    def rest():
        lay = [layout(k) for k in range(n_dp)]

        def code_of(k, j, low):
            return j * big + lay[k][4][j] + low + jnp.arange(ROUND, dtype=jnp.int32)

        def slots_of(k, code):
            dist, start, alive, slot, _ = lay[k]
            seg = dist * big + start
            hit = (code[:, None] >= seg[None, :]) & (code[:, None] < (seg + alive)[None, :])
            hit = hit & (dist == k)[None, :]
            return jnp.max(jnp.where(hit, slot[None, :], -1), axis=1, keepdims=True)

        def body(i, extra):
            low = i * ROUND
            got, found = [], []
            for j in range(1, n_dp):
                pick = (code_of(0, j, low)[:, None] == row_code.reshape(1, rows)).astype(jnp.bfloat16)
                v = jnp.dot(pick, x, preferred_element_type=jnp.float32).astype(jnp.bfloat16)
                got.append(swap(v, "dp", j))
                found.append(slots_of(j, code_of(j, j, low)))
            for j, v in zip(range(1, n_dp), answer(found, found, got)):
                put = (row_code == code_of(0, j, low)[None, :]).astype(jnp.bfloat16)
                extra = extra + jnp.dot(put, swap(v, "dp", j), preferred_element_type=jnp.float32)
            return extra

        rounds = (left + ROUND - 1) // ROUND
        extra = lax.fori_loop(0, rounds, body, jnp.zeros((rows, width), jnp.float32))
        return finish(row_code, codes, back, adds + [extra])

    out = lax.cond(left > 0, rest, lambda: finish(row_code, codes, back, adds))
    return out.reshape(steps, rows_dev, width)


def solution(mesh):
    return jax.shard_map(
        per_device,
        mesh=mesh,
        in_specs=(
            P(None, ("rep", "dp"), "tp"),
            P("tp", None),
            P("dp", None, "tp"),
            P("dp", None, "tp"),
            P(None, ("rep", "dp")),
            P(None, ("rep", "dp")),
            P("rep"),
        ),
        out_specs=P(None, ("rep", "dp"), "tp"),
        check_vma=False,
    )
```

```python
import functools

import jax
import jax.numpy as jnp
from jax import lax
from jax.experimental import pallas as pl
from jax.experimental.pallas import tpu as pltpu
from jax.sharding import PartitionSpec as P

NEAR = 208
OWN = 72
SHARED = 64
ROUND = 64
META = 128
RELAY = -1
VMEM = 48 * 2**20
FREE = pl.CostEstimate(flops=0, bytes_accessed=0, transcendentals=0)


def group_of(shape):
    return lax.broadcasted_iota(jnp.int32, shape, 1) // 16


def row_of(shape):
    return lax.broadcasted_iota(jnp.int32, shape, 0) % 8


def fold(v):
    for shift in (64, 32, 16):
        v = v + pltpu.roll(v, shift, axis=1)
    return v


def score_kernel(dists, *refs):
    m = len(dists)
    got, known, a_ref = refs[:m], refs[m:-m - 3], refs[-m - 3]
    out_ref, slots, acc = refs[-m - 2], refs[-m - 1:-1], refs[-1]
    g = pl.program_id(0)
    per, width = a_ref.shape[0] // 16, a_ref.shape[1]

    @pl.when(g == 0)
    def _():
        acc[...] = jnp.zeros_like(acc)
        for i, dist in enumerate(dists):
            if dist is None:
                slots[i][...] = known[0][...]
            else:
                meta = got[i][:, width:].astype(jnp.float32).astype(jnp.int32)
                if dist == RELAY:
                    dist = (2 + lax.broadcasted_iota(jnp.int32, (meta.shape[0], 1), 0) // SHARED) ^ 1
                slots[i][...] = jnp.where(meta[:, 1:2] == dist, meta[:, 0:1] - 1, -1)

    off = 0
    for i in range(m):
        n = got[i].shape[0]
        s = lax.dot_general(
            got[i][:, :width], a_ref[...], (((1,), (1,)), ((), ())), preferred_element_type=jnp.float32
        )
        s = jnp.where(group_of(s.shape) + g * per == slots[i][...], s, 0.0)
        v = s[:, :128]
        for c in range(128, s.shape[1], 128):
            v = v + s[:, c:c + 128]
        acc[off:off + n, :] += v
        off += n

    @pl.when(g == pl.num_programs(0) - 1)
    def _():
        off = 0
        for i in range(m):
            n = got[i].shape[0]
            v = fold(acc[off:off + n, :])
            v = jnp.where(group_of(v.shape) == row_of(v.shape), v, 0.0)
            out_ref[off // 8:(off + n) // 8, :] = jnp.sum(v.reshape(n // 8, 8, 128), axis=1)
            off += n


def whole(shape):
    return pl.BlockSpec(shape, lambda g: (0, 0))


def scores(dists, got, known, store):
    sizes = [v.shape[0] for v in got]
    total, width = sum(sizes), store.shape[1]
    blk = 256
    out = pl.pallas_call(
        functools.partial(score_kernel, tuple(dists)),
        grid=(store.shape[0] // blk,),
        in_specs=[whole(v.shape) for v in got + known] + [pl.BlockSpec((blk, width), lambda g: (g, 0))],
        out_specs=[whole((total // 8, 128))] + [whole((n, 1)) for n in sizes],
        out_shape=[jax.ShapeDtypeStruct((total // 8, 128), jnp.float32)]
        + [jax.ShapeDtypeStruct((n, 1), jnp.int32) for n in sizes],
        scratch_shapes=[pltpu.VMEM((total, 128), jnp.float32)],
        compiler_params=pltpu.CompilerParams(vmem_limit_bytes=VMEM),
        cost_estimate=FREE,
        name="scores",
    )(*got, *known, store)
    return out[0], list(out[1:])


def delta_kernel(cuts, *refs):
    m = len(cuts)
    slots, packed, b_ref, outs, spread = refs[:m], refs[m], refs[m + 1], refs[m + 2:-m], refs[-m:]

    @pl.when(pl.program_id(0) == 0)
    def _():
        off = 0
        for i in range(m):
            n = slots[i].shape[0]
            v = packed[off // 8:(off + n) // 8, :]
            v = jnp.broadcast_to(v[:, None, :], (n // 8, 8, 128)).reshape(n, 128)
            group = group_of(v.shape)
            v = fold(jnp.where(group == row_of(v.shape), v, 0.0))
            for c in range(b_ref.shape[0] // 128):
                hit = group + c * 8 == slots[i][...]
                spread[i][:, c * 128:(c + 1) * 128] = jnp.where(hit, v, 0.0).astype(jnp.bfloat16)
            off += n

    o = 0
    for i, cut in enumerate(cuts):
        v = jnp.dot(spread[i][...], b_ref[...], preferred_element_type=jnp.float32).astype(jnp.bfloat16)
        if cut:
            outs[o][...] = v[:cut]
            o += 1
        outs[o][...] = v[cut:]
        o += 1


def deltas(cuts, slots, packed, store):
    depth, width = store.shape
    cols = width // 4
    sizes = []
    for cut, v in zip(cuts, slots):
        sizes += ([cut] if cut else []) + [v.shape[0] - cut]
    return list(pl.pallas_call(
        functools.partial(delta_kernel, tuple(cuts)),
        grid=(width // cols,),
        in_specs=[whole(v.shape) for v in slots] + [whole(packed.shape)]
        + [pl.BlockSpec((depth, cols), lambda g: (0, g))],
        out_specs=[pl.BlockSpec((n, cols), lambda g: (0, g)) for n in sizes],
        out_shape=[jax.ShapeDtypeStruct((n, width), jnp.bfloat16) for n in sizes],
        scratch_shapes=[pltpu.VMEM((v.shape[0], depth), jnp.bfloat16) for v in slots],
        compiler_params=pltpu.CompilerParams(vmem_limit_bytes=VMEM),
        cost_estimate=FREE,
        name="deltas",
    )(*slots, packed, store))


def finish_kernel(m, groups, row_ref, *refs):
    codes, back, adds, out_ref = refs[:m], refs[m:2 * m], refs[2 * m:-1], refs[-1]
    total = jnp.zeros(out_ref.shape, jnp.float32)
    at = 0
    for count in groups:
        v = [r[...].astype(jnp.float32) for r in adds[at:at + count]]
        total += jnp.concatenate(v, axis=0)
        at += count
    for code, b in zip(codes, back):
        put = jnp.where(row_ref[...] == code[...], 1.0, 0.0).astype(jnp.bfloat16)
        total += jnp.dot(put, b[...], preferred_element_type=jnp.float32)
    out_ref[...] = total.astype(out_ref.dtype)


def finish(row_code, codes, back, adds):
    rows, width = row_code.shape[0], back[0].shape[1]
    cols = width // 4
    flat = [v for group in adds for v in group]
    part = lambda v: pl.BlockSpec((v.shape[0], cols), lambda g: (0, g))
    return pl.pallas_call(
        functools.partial(finish_kernel, len(codes), tuple(len(group) for group in adds)),
        grid=(width // cols,),
        in_specs=[whole(row_code.shape)] + [whole(v.shape) for v in codes] + [part(v) for v in back + flat],
        out_specs=pl.BlockSpec((rows, cols), lambda g: (0, g)),
        out_shape=jax.ShapeDtypeStruct((rows, width), jnp.bfloat16),
        compiler_params=pltpu.CompilerParams(vmem_limit_bytes=VMEM),
        name="finish",
    )(row_code, *codes, *back, *flat)


def column(row):
    n = row.shape[1]
    eye = lax.broadcasted_iota(jnp.int32, (n, n), 0) == lax.broadcasted_iota(jnp.int32, (n, n), 1)
    return jnp.sum(jnp.where(eye, jnp.broadcast_to(row, (n, n)), 0), axis=1, keepdims=True)


def row(col):
    n = col.shape[0]
    eye = lax.broadcasted_iota(jnp.int32, (n, n), 0) == lax.broadcasted_iota(jnp.int32, (n, n), 1)
    return jnp.sum(jnp.where(eye, jnp.broadcast_to(col, (n, n)), 0), axis=0, keepdims=True)


def segments(pos, alive, device, shift):
    n = pos.shape[1]
    dist = (pos >> shift) ^ device
    i = lax.broadcasted_iota(jnp.int32, (n, n), 0)
    j = lax.broadcasted_iota(jnp.int32, (n, n), 1)
    before = (column(dist) == dist) & (i < j)
    start = jnp.sum(jnp.where(before, column(alive), 0), axis=0, keepdims=True)
    return dist, start


def total(dist, alive, j):
    return jnp.sum(jnp.where(dist == j, alive, 0), axis=1, keepdims=True)


def over_of(dist, alive, j):
    return jnp.maximum(total(dist, alive, j - j % 2) - OWN, 0)


def iota_of(n, axis):
    return lax.broadcasted_iota(jnp.int32, (n, 1) if axis == 0 else (1, n), axis)


def near_code(big, axis):
    return big + iota_of(NEAR, axis)


def own_code(big, j, axis):
    return j * big + iota_of(OWN, axis)


def shared_code(big, j, over, axis):
    f = iota_of(SHARED, axis) + (j % 2) * SHARED
    even = j - j % 2
    return OWN + jnp.where(f < over, even * big + f, (even + 1) * big + f - over)


def far_code(big, j, over, axis):
    f = iota_of(SHARED + OWN, axis)
    g = f + (j % 2) * SHARED
    even = j - j % 2
    code = OWN + jnp.where(g < over, even * big + g, (even + 1) * big + g - over)
    return jnp.where(f < SHARED, code, j * big + f - SHARED)


def pack_kernel(n_dp, seg_len, shift, me_ref, ids_ref, lives_ref, index_ref, x_ref,
                table_ref, row_ref, self_ref, meta_ref, *outs):
    me = me_ref[0]
    count, (rows, width) = ids_ref.shape[1], x_ref.shape
    big = 2 * rows
    lives = lives_ref[...]
    hit = column(ids_ref[...]) == lax.broadcasted_iota(jnp.int32, (count, index_ref.shape[1]), 1)
    pos = row(jnp.sum(jnp.where(hit, index_ref[...], 0), axis=1, keepdims=True))
    table_ref[0:1, :] = pos
    table_ref[1:2, :] = lives
    dist, start = segments(pos, lives, me, shift)
    code = dist * big + start
    slot = pos & ((1 << shift) - 1)

    def spread(value, axis):
        shape = (count, rows) if axis == 1 else (rows, count)
        r = lax.broadcasted_iota(jnp.int32, shape, axis)
        seg = lax.broadcasted_iota(jnp.int32, shape, 1 - axis)
        v = column(value) if axis == 1 else value
        return jnp.sum(jnp.where(r // seg_len == seg, v, 0), axis=1 - axis, keepdims=True)

    def rows_code(axis):
        lane = iota_of(rows, axis) % seg_len
        return jnp.where(lane < spread(lives, axis), spread(code, axis) + lane, -1)

    by_row, by_lane = rows_code(0), rows_code(1)
    row_slot, row_dist = spread(slot, 0), spread(dist, 0)
    row_ref[...] = by_row
    self_ref[...] = jnp.where((by_row >= 0) & (row_dist == 0), row_slot, -1)
    lane = lax.broadcasted_iota(jnp.int32, (rows, META), 1)
    meta = jnp.where(lane == 0, row_slot + 1, jnp.where(lane == 1, row_dist, 0))
    meta = meta.astype(jnp.float32).astype(jnp.bfloat16)
    meta_ref[...] = meta

    left = total(dist, lives, 1) - NEAR
    for j in range(2, n_dp):
        held = OWN + 2 * SHARED if j % 2 == 0 else OWN + jnp.maximum(2 * SHARED - over_of(dist, lives, j), 0)
        left = jnp.maximum(left, total(dist, lives, j) - held)
    rounds = ((jnp.maximum(left, 0) + ROUND - 1) // ROUND).astype(jnp.float32)
    told = jnp.where(lax.broadcasted_iota(jnp.int32, (1, META), 1) == 2, rounds, 0.0)

    far = range(2, n_dp)
    codes = [far_code(big, j, over_of(dist, lives, j), 0) for j in far] + [near_code(big, 0)]
    m = len(codes)
    for c, out in zip(codes, outs[:m]):
        pick = jnp.where(c == by_lane, 1.0, 0.0).astype(jnp.bfloat16)
        out[:, :width] = jnp.dot(pick, x_ref[...], preferred_element_type=jnp.float32).astype(jnp.bfloat16)
        out[:, width:] = (jnp.dot(pick, meta, preferred_element_type=jnp.float32) + told).astype(jnp.bfloat16)
    lanes = [shared_code(big, j, over_of(dist, lives, j), 1) for j in far]
    lanes += [own_code(big, j, 1) for j in far] + [near_code(big, 1)]
    for c, out in zip(lanes, outs[m:]):
        out[...] = c


def vmem(count):
    return [pl.BlockSpec(memory_space=pltpu.VMEM) for _ in range(count)]


def packs(me, ids, lives, index, x, n_dp, seg_len, shift):
    count, (rows, width) = ids.shape[1], x.shape
    sizes = [SHARED + OWN] * (n_dp - 2) + [NEAR]
    parts = [SHARED] * (n_dp - 2) + [OWN] * (n_dp - 2) + [NEAR]
    shapes = [((2, count), jnp.int32), ((rows, 1), jnp.int32), ((rows, 1), jnp.int32)]
    shapes += [((rows, META), jnp.bfloat16)]
    shapes += [((n, width + META), jnp.bfloat16) for n in sizes] + [((1, n), jnp.int32) for n in parts]
    return pl.pallas_call(
        functools.partial(pack_kernel, n_dp, seg_len, shift),
        in_specs=[pl.BlockSpec(memory_space=pltpu.SMEM)] + vmem(4),
        out_specs=vmem(len(shapes)),
        out_shape=[jax.ShapeDtypeStruct(*v) for v in shapes],
        compiler_params=pltpu.CompilerParams(vmem_limit_bytes=VMEM),
        cost_estimate=FREE,
        name="pack",
    )(me, ids, lives, index, x)


def share_kernel(chunks, at_ref, x_ref, w_ref, *refs):
    adds, outs = refs[:-len(chunks)], refs[-len(chunks):]
    v = jnp.dot(x_ref[...], w_ref[...], preferred_element_type=jnp.float32)
    for r in adds:
        v += r[...].astype(jnp.float32)
    low = 0
    for n, out in zip(chunks, outs):
        out[...] = v[low:low + n].astype(jnp.bfloat16)
        low += n


def share(at, x, weight, cols, adds, chunks=None):
    rows, depth = x.shape
    tile = min(512, cols)
    chunks = chunks or (rows,)
    part = lambda n: pl.BlockSpec((n, tile), lambda g, at: (0, g))
    return list(pl.pallas_call(
        functools.partial(share_kernel, chunks),
        grid_spec=pltpu.PrefetchScalarGridSpec(
            num_scalar_prefetch=1,
            grid=(cols // tile,),
            in_specs=[
                pl.BlockSpec((rows, depth), lambda g, at: (0, 0)),
                pl.BlockSpec((depth, tile), lambda g, at: (0, at[0] * (cols // tile) + g)),
            ] + [part(rows)] * len(adds),
            out_specs=[part(n) for n in chunks],
        ),
        out_shape=[jax.ShapeDtypeStruct((n, cols), jnp.bfloat16) for n in chunks],
        compiler_params=pltpu.CompilerParams(vmem_limit_bytes=VMEM),
        cost_estimate=FREE,
        name="share",
    )(at, x, weight, *adds))


def per_device(
    attention_output,
    output_projection_weight,
    shrink_matrix_store,
    expand_matrix_store,
    segment_adapter,
    segment_live_rows,
    adapter_store_index,
):
    steps, rows_dev, width = attention_output.shape
    seg_count = segment_adapter.shape[1]
    seg_len = rows_dev // seg_count
    store, rank, _ = shrink_matrix_store.shape
    n_dp, n_tp = lax.axis_size("dp"), lax.axis_size("tp")
    me = lax.axis_index("dp").reshape(1)
    rows = steps * rows_dev
    count = steps * seg_count
    shift = store.bit_length() - 1
    big = 2 * rows
    far = range(2, n_dp)

    x = attention_output.reshape(rows, width)
    shrink_store = shrink_matrix_store.reshape(store * rank, width)
    expand_store = expand_matrix_store.reshape(store * rank, width)
    weight = output_projection_weight

    def swap(v, axis, k):
        n = lax.axis_size(axis)
        return lax.ppermute(v, axis, [(i, i ^ k) for i in range(n)])

    def butterfly(v, axis, op):
        k = 1
        while k < lax.axis_size(axis):
            v = op(v, swap(v, axis, k))
            k *= 2
        return v

    def answer(dists, cuts, got, known=()):
        scored, slots = scores(dists, got, list(known), shrink_store)
        part = butterfly(scored, "tp", jnp.add)
        return lambda part: deltas(cuts, slots, part, expand_store), part, scored

    def after(v, *others):
        return lax.optimization_barrier((v, others))[0]

    packed = list(packs(
        me,
        segment_adapter.reshape(1, count),
        segment_live_rows.reshape(1, count),
        adapter_store_index.reshape(1, -1),
        x, n_dp, seg_len, shift,
    ))
    table, row_code, self_slots, meta = packed[:4]
    m = len(far)
    out_far, out_near, codes = packed[4:4 + m], packed[4 + m], packed[5 + m:]

    in_far = [swap(v, "dp", j) for v, j in zip(out_far, far)]
    in_near = swap(out_near, "dp", 1)

    self_deltas, self_part, _ = answer([None], [0], [after(x, table)], [self_slots])

    at = after(lax.axis_index("tp").reshape(1), table)
    cols = weight.shape[1] // n_tp
    adds = {k: [] for k in range(n_tp)}
    late = []
    bit = 1
    while 2 * bit < n_tp:
        for k in sorted((k for k in adds if k & bit), reverse=True):
            if k == bit:
                late.append((k, adds.pop(k)))
            else:
                (v,) = share(at ^ k, x, weight, cols, adds.pop(k))
                adds[k ^ bit].append(swap(v, "tp", bit))
        bit *= 2
    last = share(after(at, self_part) ^ bit, x, weight, cols, adds.pop(bit), (rows // 4, rows - rows // 4))
    over_y = [swap(last[0], "tp", bit)]
    (base,) = share(at, x, weight, cols, [])
    (self_delta,) = self_deltas(self_part)
    (in_far, in_near, over_y), _ = lax.optimization_barrier(((in_far, in_near, over_y), (base, self_delta, last)))
    told = [v[0, width + 2] for v in in_far + [in_near, out_near]]
    rounds = functools.reduce(jnp.maximum, told).astype(jnp.int32).reshape(1, 1)
    rounds = butterfly(rounds, "rep", jnp.maximum)

    in_relay = swap(jnp.concatenate([v[:SHARED] for v in in_far]), "dp", 1)
    direct_deltas, part, scored = answer(list(far) + [1], [SHARED] * m + [0], in_far + [in_near])
    to_own = []
    for k, more in late:
        (v,) = share(after(at, scored) ^ k, x, weight, cols, more)
        to_own.append(swap(v, "tp", k))
    relay_deltas, relay_part, _ = answer([RELAY], [0], [after(in_relay, scored)])
    direct = direct_deltas(part)
    relay_part, to_own, rounds, direct = lax.optimization_barrier((relay_part, to_own, rounds, direct))
    back_own = [swap(direct[2 * i + 1], "dp", j) for i, j in enumerate(far)]
    back_near = swap(direct[-1], "dp", 1)
    rounds = rounds[0, 0]
    (relayed,) = relay_deltas(relay_part)
    over_y += [swap(after(last[1], relay_part), "tp", bit)]
    relayed = swap(relayed, "dp", 1)
    back_shared = [direct[2 * i] + relayed[i * SHARED:(i + 1) * SHARED] for i in range(m)]
    back_shared = [swap(v, "dp", j) for v, j in zip(back_shared, far)]

    back = back_shared + back_own + [back_near]
    adds = [[base], over_y, [self_delta]] + [[v] for v in to_own]

    def rest():
        pos, alive = table[0], table[1]
        dist = (pos >> shift) ^ me[0]
        held = [None, jnp.int32(NEAR)]
        for j in range(2, n_dp, 2):
            extra = jnp.maximum(jnp.sum(jnp.where(dist == j, alive, 0)) - OWN, 0)
            held += [jnp.int32(OWN + 2 * SHARED), OWN + jnp.maximum(2 * SHARED - extra, 0)]
        x_meta = jnp.concatenate([x, meta], axis=1)

        def body(i, extra):
            code = [j * big + held[j] + i * ROUND + jnp.arange(ROUND, dtype=jnp.int32) for j in range(1, n_dp)]
            got = []
            for j, c in zip(range(1, n_dp), code):
                pick = (c[:, None] == row_code.reshape(1, rows)).astype(jnp.bfloat16)
                v = jnp.dot(pick, x_meta, preferred_element_type=jnp.float32).astype(jnp.bfloat16)
                got.append(swap(v, "dp", j))
            late_deltas, part, _ = answer(list(range(1, n_dp)), [0] * (n_dp - 1), got)
            for j, c, v in zip(range(1, n_dp), code, late_deltas(part)):
                put = (row_code == c[None, :]).astype(jnp.bfloat16)
                extra = extra + jnp.dot(put, swap(v, "dp", j), preferred_element_type=jnp.float32)
            return extra

        extra = lax.fori_loop(0, rounds, body, jnp.zeros((rows, width), jnp.float32))
        return finish(row_code, codes, back, adds + [[extra]])

    out = lax.cond(rounds > 0, rest, lambda: finish(row_code, codes, back, adds))
    return out.reshape(steps, rows_dev, width)


def solution(mesh):
    return jax.shard_map(
        per_device,
        mesh=mesh,
        in_specs=(
            P(None, ("rep", "dp"), "tp"),
            P("tp", None),
            P("dp", None, "tp"),
            P("dp", None, "tp"),
            P(None, ("rep", "dp")),
            P(None, ("rep", "dp")),
            P("rep"),
        ),
        out_specs=P(None, ("rep", "dp"), "tp"),
        check_vma=False,
    )
```

```python
import functools

import jax
import jax.numpy as jnp
from jax import lax
from jax.experimental import pallas as pl
from jax.experimental.pallas import tpu as pltpu
from jax.sharding import PartitionSpec as P

NEAR = 208
OWN = 72
SHARED = 64
ROUND = 64
META = 128
RELAY = -1
VMEM = 48 * 2**20
FREE = pl.CostEstimate(flops=0, bytes_accessed=0, transcendentals=0)


def group_of(shape):
    return lax.broadcasted_iota(jnp.int32, shape, 1) // 16


def row_of(shape):
    return lax.broadcasted_iota(jnp.int32, shape, 0) % 8


def fold(v):
    for shift in (64, 32, 16):
        v = v + pltpu.roll(v, shift, axis=1)
    return v


def score_kernel(dists, *refs):
    m = len(dists)
    got, known, a_ref = refs[:m], refs[m:-m - 3], refs[-m - 3]
    out_ref, slots, acc = refs[-m - 2], refs[-m - 1:-1], refs[-1]
    g = pl.program_id(0)
    per, width = a_ref.shape[0] // 16, a_ref.shape[1]

    @pl.when(g == 0)
    def _():
        acc[...] = jnp.zeros_like(acc)
        for i, dist in enumerate(dists):
            if dist is None:
                slots[i][...] = known[0][...]
            else:
                meta = got[i][:, width:].astype(jnp.float32).astype(jnp.int32)
                if dist == RELAY:
                    dist = (2 + lax.broadcasted_iota(jnp.int32, (meta.shape[0], 1), 0) // SHARED) ^ 1
                slots[i][...] = jnp.where(meta[:, 1:2] == dist, meta[:, 0:1] - 1, -1)

    off = 0
    for i in range(m):
        n = got[i].shape[0]
        s = lax.dot_general(
            got[i][:, :width], a_ref[...], (((1,), (1,)), ((), ())), preferred_element_type=jnp.float32
        )
        s = jnp.where(group_of(s.shape) + g * per == slots[i][...], s, 0.0)
        v = s[:, :128]
        for c in range(128, s.shape[1], 128):
            v = v + s[:, c:c + 128]
        acc[off:off + n, :] += v
        off += n

    @pl.when(g == pl.num_programs(0) - 1)
    def _():
        off = 0
        for i in range(m):
            n = got[i].shape[0]
            v = fold(acc[off:off + n, :])
            v = jnp.where(group_of(v.shape) == row_of(v.shape), v, 0.0)
            out_ref[off // 8:(off + n) // 8, :] = jnp.sum(v.reshape(n // 8, 8, 128), axis=1)
            off += n


def whole(shape):
    return pl.BlockSpec(shape, lambda g: (0, 0))


def scores(dists, got, known, store):
    sizes = [v.shape[0] for v in got]
    total, width = sum(sizes), store.shape[1]
    blk = 256
    out = pl.pallas_call(
        functools.partial(score_kernel, tuple(dists)),
        grid=(store.shape[0] // blk,),
        in_specs=[whole(v.shape) for v in got + known] + [pl.BlockSpec((blk, width), lambda g: (g, 0))],
        out_specs=[whole((total // 8, 128))] + [whole((n, 1)) for n in sizes],
        out_shape=[jax.ShapeDtypeStruct((total // 8, 128), jnp.float32)]
        + [jax.ShapeDtypeStruct((n, 1), jnp.int32) for n in sizes],
        scratch_shapes=[pltpu.VMEM((total, 128), jnp.float32)],
        compiler_params=pltpu.CompilerParams(vmem_limit_bytes=VMEM),
        cost_estimate=FREE,
        name="scores",
    )(*got, *known, store)
    return out[0], list(out[1:])


def spread_out(slots, packed, depth, spread):
    off = 0
    for i in range(len(slots)):
        n = slots[i].shape[0]
        v = packed[off // 8:(off + n) // 8, :]
        v = jnp.broadcast_to(v[:, None, :], (n // 8, 8, 128)).reshape(n, 128)
        group = group_of(v.shape)
        v = fold(jnp.where(group == row_of(v.shape), v, 0.0))
        for c in range(depth // 128):
            hit = group + c * 8 == slots[i][...]
            spread[i][:, c * 128:(c + 1) * 128] = jnp.where(hit, v, 0.0).astype(jnp.bfloat16)
        off += n


def delta_kernel(m, *refs):
    slots, packed, b_ref, outs, spread = refs[:m], refs[m], refs[m + 1], refs[m + 2:-m], refs[-m:]

    @pl.when(pl.program_id(0) == 0)
    def _():
        spread_out(slots, packed, b_ref.shape[0], spread)

    for i in range(m):
        outs[i][...] = jnp.dot(spread[i][...], b_ref[...], preferred_element_type=jnp.float32).astype(jnp.bfloat16)


def direct_kernel(n_dp, me_ref, *refs):
    m = n_dp - 1
    slots, packed, b_ref, outs, spread = refs[:m], refs[m], refs[m + 1], refs[m + 2:-m], refs[-m:]
    me = me_ref[0]

    @pl.when(pl.program_id(0) == 0)
    def _():
        spread_out(slots, packed, b_ref.shape[0], spread)

    block = outs[-1]
    block[me] = jnp.zeros(block.shape[1:], block.dtype)
    for i in range(m):
        v = jnp.dot(spread[i][...], b_ref[...], preferred_element_type=jnp.float32)
        if i < m - 1:
            outs[i][...] = v[:SHARED].astype(jnp.bfloat16)
            block[me ^ (i + 2)] = v[SHARED:].astype(jnp.bfloat16)
        else:
            block[me ^ 1] = v[:OWN].astype(jnp.bfloat16)
            outs[i][...] = v[OWN:].astype(jnp.bfloat16)


def deltas(slots, packed, store, me=None, n_dp=None):
    depth, width = store.shape
    cols = width // 4
    part = lambda n: pl.BlockSpec((n, cols), lambda g: (0, g))
    ins = [whole(v.shape) for v in slots] + [whole(packed.shape), part(depth)]
    if me is None:
        kernel, first, args = functools.partial(delta_kernel, len(slots)), [], []
        sizes, shapes = [v.shape[0] for v in slots], []
        outs = [part(n) for n in sizes]
    else:
        kernel, first, args = functools.partial(direct_kernel, n_dp), [pl.BlockSpec(memory_space=pltpu.SMEM)], [me]
        sizes, shapes = [SHARED] * (n_dp - 2) + [NEAR - OWN], [(n_dp, OWN, width)]
        outs = [part(n) for n in sizes] + [pl.BlockSpec((n_dp, OWN, cols), lambda g: (0, 0, g))]
    shapes = [(n, width) for n in sizes] + shapes
    return list(pl.pallas_call(
        kernel,
        grid=(width // cols,),
        in_specs=first + ins,
        out_specs=outs,
        out_shape=[jax.ShapeDtypeStruct(v, jnp.bfloat16) for v in shapes],
        scratch_shapes=[pltpu.VMEM((v.shape[0], depth), jnp.bfloat16) for v in slots],
        compiler_params=pltpu.CompilerParams(vmem_limit_bytes=VMEM),
        cost_estimate=FREE,
        name="deltas",
    )(*args, *slots, packed, store))


def finish_kernel(m, n_dp, me_ref, row_ref, *refs):
    codes, block_codes = refs[:m], refs[m:m + n_dp - 1]
    back, block, adds, out_ref = refs[m + n_dp - 1:2 * m + n_dp - 1], refs[2 * m + n_dp - 1], refs[2 * m + n_dp:-1], refs[-1]
    total = adds[0][...].astype(jnp.float32)
    for v in adds[1:]:
        total += v[...].astype(jnp.float32)
    codes = [c[...] for c in codes + block_codes]
    back = [b[...] for b in back] + [block[me_ref[0] ^ (1 + i)] for i in range(n_dp - 1)]
    for code, b in zip(codes, back):
        put = jnp.where(row_ref[...] == code, 1.0, 0.0).astype(jnp.bfloat16)
        total += jnp.dot(put, b, preferred_element_type=jnp.float32)
    out_ref[...] = total.astype(out_ref.dtype)


def finish(me, row_code, codes, block_codes, back, block, adds):
    rows, width = adds[0].shape
    cols = width // 4
    n_dp = block.shape[0]
    part = lambda v: pl.BlockSpec((v.shape[0], cols), lambda g: (0, g))
    return pl.pallas_call(
        functools.partial(finish_kernel, len(codes), n_dp),
        grid=(width // cols,),
        in_specs=[pl.BlockSpec(memory_space=pltpu.SMEM), whole(row_code.shape)]
        + [whole(v.shape) for v in codes + block_codes] + [part(v) for v in back]
        + [pl.BlockSpec((n_dp, OWN, cols), lambda g: (0, 0, g))] + [part(v) for v in adds],
        out_specs=pl.BlockSpec((rows, cols), lambda g: (0, g)),
        out_shape=jax.ShapeDtypeStruct((rows, width), jnp.bfloat16),
        compiler_params=pltpu.CompilerParams(vmem_limit_bytes=VMEM),
        name="finish",
    )(me, row_code, *codes, *block_codes, *back, block, *adds)


def column(row):
    n = row.shape[1]
    eye = lax.broadcasted_iota(jnp.int32, (n, n), 0) == lax.broadcasted_iota(jnp.int32, (n, n), 1)
    return jnp.sum(jnp.where(eye, jnp.broadcast_to(row, (n, n)), 0), axis=1, keepdims=True)


def row(col):
    n = col.shape[0]
    eye = lax.broadcasted_iota(jnp.int32, (n, n), 0) == lax.broadcasted_iota(jnp.int32, (n, n), 1)
    return jnp.sum(jnp.where(eye, jnp.broadcast_to(col, (n, n)), 0), axis=0, keepdims=True)


def segments(pos, alive, device, shift):
    n = pos.shape[1]
    dist = (pos >> shift) ^ device
    i = lax.broadcasted_iota(jnp.int32, (n, n), 0)
    j = lax.broadcasted_iota(jnp.int32, (n, n), 1)
    before = (column(dist) == dist) & (i < j)
    start = jnp.sum(jnp.where(before, column(alive), 0), axis=0, keepdims=True)
    return dist, start


def total(dist, alive, j):
    return jnp.sum(jnp.where(dist == j, alive, 0), axis=1, keepdims=True)


def over_of(dist, alive, j):
    return jnp.maximum(total(dist, alive, j - j % 2) - OWN, 0)


def iota_of(n, axis):
    return lax.broadcasted_iota(jnp.int32, (n, 1) if axis == 0 else (1, n), axis)


def near_code(big, axis):
    return big + iota_of(NEAR, axis)


def own_code(big, j, axis):
    return j * big + iota_of(OWN, axis)


def shared_code(big, j, over, axis):
    f = iota_of(SHARED, axis) + (j % 2) * SHARED
    even = j - j % 2
    return OWN + jnp.where(f < over, even * big + f, (even + 1) * big + f - over)


def far_code(big, j, over, axis):
    f = iota_of(SHARED + OWN, axis)
    g = f + (j % 2) * SHARED
    even = j - j % 2
    code = OWN + jnp.where(g < over, even * big + g, (even + 1) * big + g - over)
    return jnp.where(f < SHARED, code, j * big + f - SHARED)


def pack_kernel(n_dp, seg_len, shift, me_ref, ids_ref, lives_ref, index_ref, x_ref,
                table_ref, row_ref, self_ref, meta_ref, *outs):
    me = me_ref[0]
    count, (rows, width) = ids_ref.shape[1], x_ref.shape
    big = 2 * rows
    lives = lives_ref[...]
    hit = column(ids_ref[...]) == lax.broadcasted_iota(jnp.int32, (count, index_ref.shape[1]), 1)
    pos = row(jnp.sum(jnp.where(hit, index_ref[...], 0), axis=1, keepdims=True))
    table_ref[0:1, :] = pos
    table_ref[1:2, :] = lives
    dist, start = segments(pos, lives, me, shift)
    code = dist * big + start
    slot = pos & ((1 << shift) - 1)

    def spread(value, axis):
        shape = (count, rows) if axis == 1 else (rows, count)
        r = lax.broadcasted_iota(jnp.int32, shape, axis)
        seg = lax.broadcasted_iota(jnp.int32, shape, 1 - axis)
        v = column(value) if axis == 1 else value
        return jnp.sum(jnp.where(r // seg_len == seg, v, 0), axis=1 - axis, keepdims=True)

    def rows_code(axis):
        lane = iota_of(rows, axis) % seg_len
        return jnp.where(lane < spread(lives, axis), spread(code, axis) + lane, -1)

    by_row, by_lane = rows_code(0), rows_code(1)
    row_slot, row_dist = spread(slot, 0), spread(dist, 0)
    row_ref[...] = by_row
    self_ref[...] = jnp.where((by_row >= 0) & (row_dist == 0), row_slot, -1)
    lane = lax.broadcasted_iota(jnp.int32, (rows, META), 1)
    meta = jnp.where(lane == 0, row_slot + 1, jnp.where(lane == 1, row_dist, 0))
    meta = meta.astype(jnp.float32).astype(jnp.bfloat16)
    meta_ref[...] = meta

    left = total(dist, lives, 1) - NEAR
    for j in range(2, n_dp):
        held = OWN + 2 * SHARED if j % 2 == 0 else OWN + jnp.maximum(2 * SHARED - over_of(dist, lives, j), 0)
        left = jnp.maximum(left, total(dist, lives, j) - held)
    rounds = ((jnp.maximum(left, 0) + ROUND - 1) // ROUND).astype(jnp.float32)
    told = jnp.where(lax.broadcasted_iota(jnp.int32, (1, META), 1) == 2, rounds, 0.0)

    far = range(2, n_dp)
    codes = [far_code(big, j, over_of(dist, lives, j), 0) for j in far] + [near_code(big, 0)]
    m = len(codes)
    for c, out in zip(codes, outs[:m]):
        pick = jnp.where(c == by_lane, 1.0, 0.0).astype(jnp.bfloat16)
        out[:, :width] = jnp.dot(pick, x_ref[...], preferred_element_type=jnp.float32).astype(jnp.bfloat16)
        out[:, width:] = (jnp.dot(pick, meta, preferred_element_type=jnp.float32) + told).astype(jnp.bfloat16)
    lanes = [shared_code(big, j, over_of(dist, lives, j), 1) for j in far]
    lanes += [big + OWN + iota_of(NEAR - OWN, 1)]
    lanes += [own_code(big, j, 1) for j in range(1, n_dp)]
    for c, out in zip(lanes, outs[m:]):
        out[...] = c


def vmem(count):
    return [pl.BlockSpec(memory_space=pltpu.VMEM) for _ in range(count)]


def packs(me, ids, lives, index, x, n_dp, seg_len, shift):
    count, (rows, width) = ids.shape[1], x.shape
    sizes = [SHARED + OWN] * (n_dp - 2) + [NEAR]
    parts = [SHARED] * (n_dp - 2) + [NEAR - OWN] + [OWN] * (n_dp - 1)
    shapes = [((2, count), jnp.int32), ((rows, 1), jnp.int32), ((rows, 1), jnp.int32)]
    shapes += [((rows, META), jnp.bfloat16)]
    shapes += [((n, width + META), jnp.bfloat16) for n in sizes] + [((1, n), jnp.int32) for n in parts]
    return pl.pallas_call(
        functools.partial(pack_kernel, n_dp, seg_len, shift),
        in_specs=[pl.BlockSpec(memory_space=pltpu.SMEM)] + vmem(4),
        out_specs=vmem(len(shapes)),
        out_shape=[jax.ShapeDtypeStruct(*v) for v in shapes],
        compiler_params=pltpu.CompilerParams(vmem_limit_bytes=VMEM),
        cost_estimate=FREE,
        name="pack",
    )(me, ids, lives, index, x)


def share_kernel(at_ref, x_ref, w_ref, out_ref):
    out_ref[...] = jnp.dot(x_ref[...], w_ref[...], preferred_element_type=jnp.float32).astype(jnp.bfloat16)


def share(at, x, weight, cols):
    rows, depth = x.shape
    tile = min(512, cols)
    return pl.pallas_call(
        share_kernel,
        grid_spec=pltpu.PrefetchScalarGridSpec(
            num_scalar_prefetch=1,
            grid=(cols // tile,),
            in_specs=[
                pl.BlockSpec((rows, depth), lambda g, at: (0, 0)),
                pl.BlockSpec((depth, tile), lambda g, at: (0, at[0] * (cols // tile) + g)),
            ],
            out_specs=pl.BlockSpec((rows, tile), lambda g, at: (0, g)),
        ),
        out_shape=jax.ShapeDtypeStruct((rows, cols), jnp.bfloat16),
        compiler_params=pltpu.CompilerParams(vmem_limit_bytes=VMEM),
        cost_estimate=FREE,
        name="share",
    )(at, x, weight)


def per_device(
    attention_output,
    output_projection_weight,
    shrink_matrix_store,
    expand_matrix_store,
    segment_adapter,
    segment_live_rows,
    adapter_store_index,
):
    steps, rows_dev, width = attention_output.shape
    seg_count = segment_adapter.shape[1]
    seg_len = rows_dev // seg_count
    store, rank, _ = shrink_matrix_store.shape
    n_dp, n_tp = lax.axis_size("dp"), lax.axis_size("tp")
    me = lax.axis_index("dp").reshape(1)
    rows = steps * rows_dev
    count = steps * seg_count
    shift = store.bit_length() - 1
    big = 2 * rows
    far = range(2, n_dp)

    x = attention_output.reshape(rows, width)
    shrink_store = shrink_matrix_store.reshape(store * rank, width)
    expand_store = expand_matrix_store.reshape(store * rank, width)
    weight = output_projection_weight

    def swap(v, axis, k):
        n = lax.axis_size(axis)
        return lax.ppermute(v, axis, [(i, i ^ k) for i in range(n)])

    def butterfly(v, axis, op):
        k = 1
        while k < lax.axis_size(axis):
            v = op(v, swap(v, axis, k))
            k *= 2
        return v

    def answer(dists, got, known=()):
        scored, slots = scores(dists, got, list(known), shrink_store)
        return slots, butterfly(scored, "tp", jnp.add)

    def after(v, *others):
        return lax.optimization_barrier((v, others))[0]

    packed = list(packs(
        me,
        segment_adapter.reshape(1, count),
        segment_live_rows.reshape(1, count),
        adapter_store_index.reshape(1, -1),
        x, n_dp, seg_len, shift,
    ))
    table, row_code, self_slots, meta = packed[:4]
    m = len(far)
    out_far, out_near = packed[4:4 + m], packed[4 + m]
    codes, block_codes = packed[5 + m:6 + 2 * m], packed[6 + 2 * m:]

    in_far = [swap(v, "dp", j) for v, j in zip(out_far, far)]
    in_near = swap(out_near, "dp", 1)

    found, self_part = answer([None], [after(x, table)], [self_slots])
    (self_delta,) = deltas(found, self_part, expand_store)

    at = after(lax.axis_index("tp").reshape(1), table)
    cols = weight.shape[1] // n_tp
    shares = {k: share(at ^ k, x, weight, cols) for k in reversed(range(n_tp))}
    (in_far, in_near, shares), _ = lax.optimization_barrier(((in_far, in_near, shares), self_delta))

    in_relay = swap(jnp.concatenate([v[:SHARED] for v in in_far]), "dp", 1)
    found, part = answer(list(far) + [1], in_far + [in_near])
    direct = deltas(found, part, expand_store, me, n_dp)
    block = lax.all_to_all(direct[-1], "dp", split_axis=0, concat_axis=0, tiled=True)

    adds = {k: [shares[k]] for k in shares}
    for k in range(1, n_tp, 2):
        adds[k ^ 1].append(swap(adds.pop(k)[0], "tp", 1))
    told = [v[0, width + 2] for v in in_far + [in_near, out_near]]
    rounds = functools.reduce(jnp.maximum, told).astype(jnp.int32).reshape(1, 1)
    rounds = butterfly(rounds, "rep", jnp.maximum)

    found, part = answer([RELAY], [after(in_relay, direct)])
    part, adds, rounds = lax.optimization_barrier((part, adds, rounds))
    rounds = rounds[0, 0]
    (relayed,) = deltas(found, part, expand_store)
    relayed = swap(relayed, "dp", 1)
    bit = 2
    while bit < n_tp:
        for k in sorted((k for k in adds if k & bit), reverse=True):
            v = functools.reduce(jnp.add, [u.astype(jnp.float32) for u in adds.pop(k)])
            adds[k ^ bit].append(swap(v.astype(jnp.bfloat16), "tp", bit))
        bit *= 2
    near, _ = lax.optimization_barrier((direct[m], relayed))
    back = [swap(direct[i] + relayed[i * SHARED:(i + 1) * SHARED], "dp", j) for i, j in enumerate(far)]
    back.append(swap(near, "dp", 1))
    adds = adds[0] + [self_delta]

    def rest():
        pos, alive = table[0], table[1]
        dist = (pos >> shift) ^ me[0]
        held = [None, jnp.int32(NEAR)]
        for j in range(2, n_dp, 2):
            extra = jnp.maximum(jnp.sum(jnp.where(dist == j, alive, 0)) - OWN, 0)
            held += [jnp.int32(OWN + 2 * SHARED), OWN + jnp.maximum(2 * SHARED - extra, 0)]
        x_meta = jnp.concatenate([x, meta], axis=1)

        def body(i, extra):
            code = [j * big + held[j] + i * ROUND + jnp.arange(ROUND, dtype=jnp.int32) for j in range(1, n_dp)]
            got = []
            for j, c in zip(range(1, n_dp), code):
                pick = (c[:, None] == row_code.reshape(1, rows)).astype(jnp.bfloat16)
                v = jnp.dot(pick, x_meta, preferred_element_type=jnp.float32).astype(jnp.bfloat16)
                got.append(swap(v, "dp", j))
            found, part = answer(list(range(1, n_dp)), got)
            for j, c, v in zip(range(1, n_dp), code, deltas(found, part, expand_store)):
                put = (row_code == c[None, :]).astype(jnp.bfloat16)
                extra = extra + jnp.dot(put, swap(v, "dp", j), preferred_element_type=jnp.float32)
            return extra

        extra = lax.fori_loop(0, rounds, body, jnp.zeros((rows, width), jnp.float32))
        return finish(me, row_code, codes, block_codes, back, block, adds + [extra])

    out = lax.cond(rounds > 0, rest, lambda: finish(me, row_code, codes, block_codes, back, block, adds))
    return out.reshape(steps, rows_dev, width)


def solution(mesh):
    return jax.shard_map(
        per_device,
        mesh=mesh,
        in_specs=(
            P(None, ("rep", "dp"), "tp"),
            P("tp", None),
            P("dp", None, "tp"),
            P("dp", None, "tp"),
            P(None, ("rep", "dp")),
            P(None, ("rep", "dp")),
            P("rep"),
        ),
        out_specs=P(None, ("rep", "dp"), "tp"),
        check_vma=False,
    )
```

```python
import functools

import jax
import jax.numpy as jnp
from jax import lax
from jax.experimental import pallas as pl
from jax.experimental.pallas import tpu as pltpu
from jax.sharding import PartitionSpec as P

NEAR = 208
OWN = 72
SHARED = 64
ROUND = 64
META = 128
RELAY = -1
VMEM = 48 * 2**20
FREE = pl.CostEstimate(flops=0, bytes_accessed=0, transcendentals=0)


def group_of(shape):
    return lax.broadcasted_iota(jnp.int32, shape, 1) // 16


def row_of(shape):
    return lax.broadcasted_iota(jnp.int32, shape, 0) % 8


def fold(v):
    for shift in (64, 32, 16):
        v = v + pltpu.roll(v, shift, axis=1)
    return v


def score_kernel(dists, block, *refs):
    me_ref, known_ref, refs = refs[0], refs[1], refs[2:]
    m = len(dists)
    got, a_ref, refs = refs[:1 if block else m], refs[1 if block else m], refs[(2 if block else m + 1):]
    out_ref, told_ref, slots, acc = refs[0], refs[1], refs[2:-1], refs[-1]
    g = pl.program_id(0)
    per, width = a_ref.shape[0] // 16, a_ref.shape[1]

    def view(i, low, high):
        return got[0][me_ref[0] ^ (i + 1), :, low:high] if block else got[i][:, low:high]

    @pl.when(g == 0)
    def _():
        acc[...] = jnp.zeros_like(acc)
        told_ref[...] = known_ref[0:1, 0:1]
        for i, dist in enumerate(dists):
            if dist is None:
                slots[i][...] = known_ref[...]
                continue
            meta = view(i, width, width + META).astype(jnp.float32).astype(jnp.int32)
            if dist == RELAY:
                dist = (2 + lax.broadcasted_iota(jnp.int32, (meta.shape[0], 1), 0) // SHARED) ^ 1
            slots[i][...] = jnp.where(meta[:, 1:2] == dist, meta[:, 0:1] - 1, -1)
            told_ref[...] = jnp.maximum(told_ref[...], meta[0:1, 2:3])

    off = 0
    for i in range(m):
        n = slots[i].shape[0]
        s = lax.dot_general(
            view(i, 0, width), a_ref[...], (((1,), (1,)), ((), ())), preferred_element_type=jnp.float32
        )
        s = jnp.where(group_of(s.shape) + g * per == slots[i][...], s, 0.0)
        v = s[:, :128]
        for c in range(128, s.shape[1], 128):
            v = v + s[:, c:c + 128]
        acc[off:off + n, :] += v
        off += n

    @pl.when(g == pl.num_programs(0) - 1)
    def _():
        off = 0
        for i in range(m):
            n = slots[i].shape[0]
            v = fold(acc[off:off + n, :])
            v = jnp.where(group_of(v.shape) == row_of(v.shape), v, 0.0)
            out_ref[off // 8:(off + n) // 8, :] = jnp.sum(v.reshape(n // 8, 8, 128), axis=1)
            off += n


def whole(shape):
    return pl.BlockSpec(shape, lambda g: (0,) * len(shape))


def scores(me, known, dists, got, store):
    block = got[0].ndim == 3
    sizes = [got[0].shape[1]] * len(dists) if block else [v.shape[0] for v in got]
    total, width = sum(sizes), store.shape[1]
    blk = 256
    out = pl.pallas_call(
        functools.partial(score_kernel, tuple(dists), block),
        grid=(store.shape[0] // blk,),
        in_specs=[pl.BlockSpec(memory_space=pltpu.SMEM), whole(known.shape)]
        + [whole(v.shape) for v in got] + [pl.BlockSpec((blk, width), lambda g: (g, 0))],
        out_specs=[whole((total // 8, 128)), whole((1, 1))] + [whole((n, 1)) for n in sizes],
        out_shape=[jax.ShapeDtypeStruct((total // 8, 128), jnp.float32), jax.ShapeDtypeStruct((1, 1), jnp.int32)]
        + [jax.ShapeDtypeStruct((n, 1), jnp.int32) for n in sizes],
        scratch_shapes=[pltpu.VMEM((total, 128), jnp.float32)],
        compiler_params=pltpu.CompilerParams(vmem_limit_bytes=VMEM),
        cost_estimate=FREE,
        name="scores",
    )(me, known, *got, store)
    return out[0], out[1], list(out[2:])


def spread_out(slots, packed, depth, spread):
    off = 0
    for i in range(len(slots)):
        n = slots[i].shape[0]
        v = packed[off // 8:(off + n) // 8, :]
        v = jnp.broadcast_to(v[:, None, :], (n // 8, 8, 128)).reshape(n, 128)
        group = group_of(v.shape)
        v = fold(jnp.where(group == row_of(v.shape), v, 0.0))
        for c in range(depth // 128):
            hit = group + c * 8 == slots[i][...]
            spread[i][:, c * 128:(c + 1) * 128] = jnp.where(hit, v, 0.0).astype(jnp.bfloat16)
        off += n


def delta_kernel(m, *refs):
    slots, packed, b_ref, outs, spread = refs[:m], refs[m], refs[m + 1], refs[m + 2:-m], refs[-m:]

    @pl.when(pl.program_id(0) == 0)
    def _():
        spread_out(slots, packed, b_ref.shape[0], spread)

    for i in range(m):
        outs[i][...] = jnp.dot(spread[i][...], b_ref[...], preferred_element_type=jnp.float32).astype(jnp.bfloat16)


def direct_kernel(m, me_ref, *refs):
    slots, packed, b_ref, block, spread = refs[:m], refs[m], refs[m + 1], refs[m + 2], refs[m + 3:]
    me = me_ref[0]

    @pl.when(pl.program_id(0) == 0)
    def _():
        spread_out(slots, packed, b_ref.shape[0], spread)

    block[me] = jnp.zeros(block.shape[1:], block.dtype)
    for i in range(m):
        v = jnp.dot(spread[i][...], b_ref[...], preferred_element_type=jnp.float32)
        block[me ^ (i + 1)] = v.astype(jnp.bfloat16)


def deltas(slots, packed, store, me=None):
    depth, width = store.shape
    cols = width // 4
    m, sizes = len(slots), [v.shape[0] for v in slots]
    part = lambda n: pl.BlockSpec((n, cols), lambda g: (0, g))
    ins = [whole(v.shape) for v in slots] + [whole(packed.shape), part(depth)]
    args = [*slots, packed, store]
    if me is None:
        kernel, outs, shapes = delta_kernel, [part(n) for n in sizes], [(n, width) for n in sizes]
    else:
        kernel, ins, args = direct_kernel, [pl.BlockSpec(memory_space=pltpu.SMEM)] + ins, [me] + args
        outs = [pl.BlockSpec((m + 1, OWN, cols), lambda g: (0, 0, g))]
        shapes = [(m + 1, OWN, width)]
    return list(pl.pallas_call(
        functools.partial(kernel, m),
        grid=(width // cols,),
        in_specs=ins,
        out_specs=outs,
        out_shape=[jax.ShapeDtypeStruct(v, jnp.bfloat16) for v in shapes],
        scratch_shapes=[pltpu.VMEM((n, depth), jnp.bfloat16) for n in sizes],
        compiler_params=pltpu.CompilerParams(vmem_limit_bytes=VMEM),
        cost_estimate=FREE,
        name="deltas",
    )(*args))


def finish_kernel(m, n_dp, me_ref, row_ref, *refs):
    codes, block_codes = refs[:m], refs[m:m + n_dp - 1]
    back, block, adds, out_ref = refs[m + n_dp - 1:2 * m + n_dp - 1], refs[2 * m + n_dp - 1], refs[2 * m + n_dp:-1], refs[-1]
    total = adds[0][...].astype(jnp.float32)
    for v in adds[1:]:
        total += v[...].astype(jnp.float32)
    codes = [c[...] for c in codes + block_codes]
    back = [b[...] for b in back] + [block[me_ref[0] ^ (1 + i)] for i in range(n_dp - 1)]
    for code, b in zip(codes, back):
        put = jnp.where(row_ref[...] == code, 1.0, 0.0).astype(jnp.bfloat16)
        total += jnp.dot(put, b, preferred_element_type=jnp.float32)
    out_ref[...] = total.astype(out_ref.dtype)


def finish(me, row_code, codes, block_codes, back, block, adds):
    rows, width = adds[0].shape
    cols = width // 4
    n_dp = block.shape[0]
    part = lambda v: pl.BlockSpec((v.shape[0], cols), lambda g: (0, g))
    return pl.pallas_call(
        functools.partial(finish_kernel, len(codes), n_dp),
        grid=(width // cols,),
        in_specs=[pl.BlockSpec(memory_space=pltpu.SMEM), whole(row_code.shape)]
        + [whole(v.shape) for v in codes + block_codes] + [part(v) for v in back]
        + [pl.BlockSpec((n_dp, OWN, cols), lambda g: (0, 0, g))] + [part(v) for v in adds],
        out_specs=pl.BlockSpec((rows, cols), lambda g: (0, g)),
        out_shape=jax.ShapeDtypeStruct((rows, width), jnp.bfloat16),
        compiler_params=pltpu.CompilerParams(vmem_limit_bytes=VMEM),
        name="finish",
    )(me, row_code, *codes, *block_codes, *back, block, *adds)


def column(row):
    n = row.shape[1]
    eye = lax.broadcasted_iota(jnp.int32, (n, n), 0) == lax.broadcasted_iota(jnp.int32, (n, n), 1)
    return jnp.sum(jnp.where(eye, jnp.broadcast_to(row, (n, n)), 0), axis=1, keepdims=True)


def row(col):
    n = col.shape[0]
    eye = lax.broadcasted_iota(jnp.int32, (n, n), 0) == lax.broadcasted_iota(jnp.int32, (n, n), 1)
    return jnp.sum(jnp.where(eye, jnp.broadcast_to(col, (n, n)), 0), axis=0, keepdims=True)


def segments(pos, alive, device, shift):
    n = pos.shape[1]
    dist = (pos >> shift) ^ device
    i = lax.broadcasted_iota(jnp.int32, (n, n), 0)
    j = lax.broadcasted_iota(jnp.int32, (n, n), 1)
    before = (column(dist) == dist) & (i < j)
    start = jnp.sum(jnp.where(before, column(alive), 0), axis=0, keepdims=True)
    return dist, start


def total(dist, alive, j):
    return jnp.sum(jnp.where(dist == j, alive, 0), axis=1, keepdims=True)


def over_of(dist, alive, j):
    return jnp.maximum(total(dist, alive, j - j % 2) - OWN, 0)


def iota_of(n, axis):
    return lax.broadcasted_iota(jnp.int32, (n, 1) if axis == 0 else (1, n), axis)


def near_code(big, axis):
    return big + OWN + iota_of(NEAR - OWN, axis)


def own_code(big, j, axis):
    return j * big + iota_of(OWN, axis)


def shared_code(big, j, over, axis):
    f = iota_of(SHARED, axis) + (j % 2) * SHARED
    even = j - j % 2
    return OWN + jnp.where(f < over, even * big + f, (even + 1) * big + f - over)


def flat_column(v):
    a, b = v.shape
    i = lax.broadcasted_iota(jnp.int32, (a * b, b), 0)
    j = lax.broadcasted_iota(jnp.int32, (a * b, b), 1)
    out = jnp.zeros((a * b, b), jnp.int32)
    for k in range(a):
        out += jnp.where(i - j == k * b, v[k:k + 1, :], 0)
    return jnp.sum(out, axis=1, keepdims=True)


def pack_kernel(n_dp, seg_len, shift, me_ref, ids_ref, lives_ref, index_ref, x_ref,
                table_ref, row_ref, self_ref, meta_ref, rounds_ref, block, *outs):
    me = me_ref[0]
    count, (rows, width) = ids_ref.shape[0] * ids_ref.shape[1], x_ref.shape
    big = 2 * rows
    lives = row(flat_column(lives_ref[...]))
    hit = flat_column(ids_ref[...]) == lax.broadcasted_iota(jnp.int32, (count, index_ref.shape[1]), 1)
    pos = row(jnp.sum(jnp.where(hit, index_ref[...], 0), axis=1, keepdims=True))
    table_ref[0:1, :] = pos
    table_ref[1:2, :] = lives
    dist, start = segments(pos, lives, me, shift)
    code = dist * big + start
    slot = pos & ((1 << shift) - 1)

    def spread(value, axis):
        shape = (count, rows) if axis == 1 else (rows, count)
        r = lax.broadcasted_iota(jnp.int32, shape, axis)
        seg = lax.broadcasted_iota(jnp.int32, shape, 1 - axis)
        v = column(value) if axis == 1 else value
        return jnp.sum(jnp.where(r // seg_len == seg, v, 0), axis=1 - axis, keepdims=True)

    def rows_code(axis):
        lane = iota_of(rows, axis) % seg_len
        return jnp.where(lane < spread(lives, axis), spread(code, axis) + lane, -1)

    by_row, by_lane = rows_code(0), rows_code(1)
    row_slot, row_dist = spread(slot, 0), spread(dist, 0)
    row_ref[...] = by_row
    self_ref[...] = jnp.where((by_row >= 0) & (row_dist == 0), row_slot, -1)
    lane = lax.broadcasted_iota(jnp.int32, (rows, META), 1)
    meta = jnp.where(lane == 0, row_slot + 1, jnp.where(lane == 1, row_dist, 0))
    meta = meta.astype(jnp.float32).astype(jnp.bfloat16)
    meta_ref[...] = meta

    left = total(dist, lives, 1) - NEAR
    for j in range(2, n_dp):
        held = OWN + 2 * SHARED if j % 2 == 0 else OWN + jnp.maximum(2 * SHARED - over_of(dist, lives, j), 0)
        left = jnp.maximum(left, total(dist, lives, j) - held)
    rounds = (jnp.maximum(left, 0) + ROUND - 1) // ROUND
    rounds_ref[...] = rounds
    told = jnp.where(lax.broadcasted_iota(jnp.int32, (1, META), 1) == 2, rounds.astype(jnp.float32), 0.0)

    def chosen(c):
        pick = jnp.where(c == by_lane, 1.0, 0.0).astype(jnp.bfloat16)
        v = jnp.dot(pick, x_ref[...], preferred_element_type=jnp.float32).astype(jnp.bfloat16)
        return v, (jnp.dot(pick, meta, preferred_element_type=jnp.float32) + told).astype(jnp.bfloat16)

    far = range(2, n_dp)
    block[me] = jnp.zeros(block.shape[1:], block.dtype)
    for j in range(1, n_dp):
        v, u = chosen(own_code(big, j, 0))
        block[me ^ j, :, :width] = v
        block[me ^ j, :, width:] = u
    codes = [shared_code(big, j, over_of(dist, lives, j), 0) for j in far] + [near_code(big, 0)]
    m = len(codes)
    for c, out in zip(codes, outs[:m]):
        out[:, :width], out[:, width:] = chosen(c)
    lanes = [shared_code(big, j, over_of(dist, lives, j), 1) for j in far] + [near_code(big, 1)]
    lanes += [own_code(big, j, 1) for j in range(1, n_dp)]
    for c, out in zip(lanes, outs[m:]):
        out[...] = c


def vmem(count):
    return [pl.BlockSpec(memory_space=pltpu.VMEM) for _ in range(count)]


def packs(me, ids, lives, index, x, n_dp, seg_len, shift):
    count, (rows, width) = ids.shape[0] * ids.shape[1], x.shape
    sizes = [SHARED] * (n_dp - 2) + [NEAR - OWN]
    shapes = [((2, count), jnp.int32), ((rows, 1), jnp.int32), ((rows, 1), jnp.int32)]
    shapes += [((rows, META), jnp.bfloat16), ((1, 1), jnp.int32), ((n_dp, OWN, width + META), jnp.bfloat16)]
    shapes += [((n, width + META), jnp.bfloat16) for n in sizes]
    shapes += [((1, n), jnp.int32) for n in sizes + [OWN] * (n_dp - 1)]
    return pl.pallas_call(
        functools.partial(pack_kernel, n_dp, seg_len, shift),
        in_specs=[pl.BlockSpec(memory_space=pltpu.SMEM)] + vmem(4),
        out_specs=vmem(len(shapes)),
        out_shape=[jax.ShapeDtypeStruct(*v) for v in shapes],
        compiler_params=pltpu.CompilerParams(vmem_limit_bytes=VMEM),
        cost_estimate=FREE,
        name="pack",
    )(me, ids, lives, index, x)


def share_kernel(at_ref, x_ref, w_ref, out_ref):
    out_ref[...] = jnp.dot(x_ref[...], w_ref[...], preferred_element_type=jnp.float32).astype(jnp.bfloat16)


def share(at, x, weight, cols):
    rows, depth = x.shape
    tile = min(512, cols)
    return pl.pallas_call(
        share_kernel,
        grid_spec=pltpu.PrefetchScalarGridSpec(
            num_scalar_prefetch=1,
            grid=(cols // tile,),
            in_specs=[
                pl.BlockSpec((rows, depth), lambda g, at: (0, 0)),
                pl.BlockSpec((depth, tile), lambda g, at: (0, at[0] * (cols // tile) + g)),
            ],
            out_specs=pl.BlockSpec((rows, tile), lambda g, at: (0, g)),
        ),
        out_shape=jax.ShapeDtypeStruct((rows, cols), jnp.bfloat16),
        compiler_params=pltpu.CompilerParams(vmem_limit_bytes=VMEM),
        cost_estimate=FREE,
        name="share",
    )(at, x, weight)


def per_device(
    attention_output,
    output_projection_weight,
    shrink_matrix_store,
    expand_matrix_store,
    segment_adapter,
    segment_live_rows,
    adapter_store_index,
):
    steps, rows_dev, width = attention_output.shape
    seg_count = segment_adapter.shape[1]
    seg_len = rows_dev // seg_count
    store, rank, _ = shrink_matrix_store.shape
    n_dp, n_tp = lax.axis_size("dp"), lax.axis_size("tp")
    me = lax.axis_index("dp").reshape(1)
    rows = steps * rows_dev
    count = steps * seg_count
    shift = store.bit_length() - 1
    big = 2 * rows
    far = range(2, n_dp)

    x = attention_output.reshape(rows, width)
    shrink_store = shrink_matrix_store.reshape(store * rank, width)
    expand_store = expand_matrix_store.reshape(store * rank, width)
    weight = output_projection_weight

    def swap(v, axis, k):
        n = lax.axis_size(axis)
        return lax.ppermute(v, axis, [(i, i ^ k) for i in range(n)])

    def butterfly(v, axis, op):
        k = 1
        while k < lax.axis_size(axis):
            v = op(v, swap(v, axis, k))
            k *= 2
        return v

    def answer(dists, got, known):
        scored, told, slots = scores(me, known, dists, got, shrink_store)
        return slots, told, butterfly(scored, "tp", jnp.add)

    def total_of(parts):
        if len(parts) == 1:
            return parts[0]
        return functools.reduce(jnp.add, [v.astype(jnp.float32) for v in parts]).astype(jnp.bfloat16)

    def a2a(v):
        return lax.all_to_all(v, "dp", split_axis=0, concat_axis=0, tiled=True)

    def after(v, *others):
        return lax.optimization_barrier((v, others))[0]

    packed = list(packs(
        me, segment_adapter, segment_live_rows, adapter_store_index.reshape(1, -1), x, n_dp, seg_len, shift
    ))
    table, row_code, self_slots, meta, rounds, block = packed[:6]
    m = len(far)
    out_shared, out_near, codes = packed[6:6 + m], packed[6 + m], packed[7 + m:]
    codes, block_codes = codes[:m + 1], codes[m + 1:]

    block = a2a(block)
    in_shared = [swap(v, "dp", j) for v, j in zip(out_shared, far)]
    in_near = swap(out_near, "dp", 1)

    self_found, _, self_part = answer([None], [after(x, table)], self_slots)

    at = after(lax.axis_index("tp").reshape(1), self_part)
    cols = weight.shape[1] // n_tp
    early = [k for k in reversed(range(n_tp)) if k >= n_tp // 2]
    shares = {k: share(at ^ k, x, weight, cols) for k in early}

    block, shares = lax.optimization_barrier((block, shares))
    found, rounds, part = answer(list(range(1, n_dp)), [block], rounds)
    (block,) = deltas(found, part, expand_store, me)
    at = after(at, block)
    block = a2a(block)
    for k in reversed(range(n_tp)):
        if k not in early and k:
            shares[k] = share(at ^ k, x, weight, cols)

    in_shared, shares = lax.optimization_barrier((in_shared, shares))
    in_relay = jnp.concatenate(in_shared)
    at = after(at, in_relay)
    in_relay = swap(in_relay, "dp", 1)
    shares[0] = share(at, x, weight, cols)
    (self_delta,) = deltas(self_found, after(self_part, in_shared), expand_store)

    adds = {k: [shares[k]] for k in shares}
    for k in range(1, n_tp, 2):
        adds[k ^ 1].append(swap(adds.pop(k)[0], "tp", 1))
    for k in range(2, n_tp, 2):
        adds[k] = [total_of(adds[k])]

    got, self_delta, adds = lax.optimization_barrier((in_shared + [in_near, in_relay], self_delta, adds))
    found, _, part = answer(list(far) + [1, RELAY], got, rounds)
    part, adds, block = lax.optimization_barrier((part, adds, block))
    late = deltas(found, part, expand_store)
    relayed = swap(late[-1], "dp", 1)
    bit = 2
    while bit < n_tp:
        for k in sorted((k for k in adds if k & bit), reverse=True):
            adds[k ^ bit].append(swap(total_of(adds.pop(k)), "tp", bit))
        bit *= 2
    back = [swap(late[i] + relayed[i * SHARED:(i + 1) * SHARED], "dp", j) for i, j in enumerate(far)]
    back.append(swap(late[m], "dp", 1))
    adds = adds[0] + [self_delta]
    rounds = butterfly(rounds, "rep", jnp.maximum)[0, 0]

    def late_round(i, out):
        tab, rows_in, rows_meta, places = lax.optimization_barrier((table, x, meta, row_code, i))[:4]
        pos, alive = tab[0], tab[1]
        dist = (pos >> shift) ^ me[0]
        held = [None, jnp.int32(NEAR)]
        for j in range(2, n_dp, 2):
            extra = jnp.maximum(jnp.sum(jnp.where(dist == j, alive, 0)) - OWN, 0)
            held += [jnp.int32(OWN + 2 * SHARED), OWN + jnp.maximum(2 * SHARED - extra, 0)]
        x_meta = jnp.concatenate([rows_in, rows_meta], axis=1)
        code = [j * big + held[j] + i * ROUND + jnp.arange(ROUND, dtype=jnp.int32) for j in range(1, n_dp)]
        got = []
        for j, c in zip(range(1, n_dp), code):
            pick = (c[:, None] == places.reshape(1, rows)).astype(jnp.bfloat16)
            v = jnp.dot(pick, x_meta, preferred_element_type=jnp.float32).astype(jnp.bfloat16)
            got.append(swap(v, "dp", j))
        found, _, part = answer(list(range(1, n_dp)), got, rounds.reshape(1, 1))
        total = out.astype(jnp.float32)
        for j, c, v in zip(range(1, n_dp), code, deltas(found, part, expand_store)):
            put = (places == c[None, :]).astype(jnp.bfloat16)
            total = total + jnp.dot(put, swap(v, "dp", j), preferred_element_type=jnp.float32)
        return total.astype(jnp.bfloat16)

    out = finish(me, row_code, codes, block_codes, back, block, adds)
    out = lax.fori_loop(0, rounds, late_round, out)
    return out.reshape(steps, rows_dev, width)


def solution(mesh):
    return jax.shard_map(
        per_device,
        mesh=mesh,
        in_specs=(
            P(None, ("rep", "dp"), "tp"),
            P("tp", None),
            P("dp", None, "tp"),
            P("dp", None, "tp"),
            P(None, ("rep", "dp")),
            P(None, ("rep", "dp")),
            P("rep"),
        ),
        out_specs=P(None, ("rep", "dp"), "tp"),
        check_vma=False,
    )
```

```python
import functools

import jax
import jax.numpy as jnp
from jax import lax
from jax.experimental import pallas as pl
from jax.experimental.pallas import tpu as pltpu
from jax.sharding import PartitionSpec as P

NEAR = 208
OWN = 72
SHARED = 64
ROUND = 64
META = 128
RELAY = -1
VMEM = 48 * 2**20
FREE = pl.CostEstimate(flops=0, bytes_accessed=0, transcendentals=0)


def group_of(shape):
    return lax.broadcasted_iota(jnp.int32, shape, 1) // 16


def row_of(shape):
    return lax.broadcasted_iota(jnp.int32, shape, 0) % 8


def fold(v):
    for shift in (64, 32, 16):
        v = v + pltpu.roll(v, shift, axis=1)
    return v


def score_kernel(dists, block, *refs):
    me_ref, known_ref, refs = refs[0], refs[1], refs[2:]
    m = len(dists)
    got, a_ref, refs = refs[:1 if block else m], refs[1 if block else m], refs[(2 if block else m + 1):]
    out_ref, told_ref, slots, acc = refs[0], refs[1], refs[2:-1], refs[-1]
    g = pl.program_id(0)
    per, width = a_ref.shape[0] // 16, a_ref.shape[1]

    def view(i, low, high):
        return got[0][me_ref[0] ^ (i + 1), :, low:high] if block else got[i][:, low:high]

    @pl.when(g == 0)
    def _():
        acc[...] = jnp.zeros_like(acc)
        told_ref[...] = known_ref[0:1, 0:1]
        for i, dist in enumerate(dists):
            if dist is None:
                slots[i][...] = known_ref[...]
                continue
            meta = view(i, width, width + META).astype(jnp.float32).astype(jnp.int32)
            if dist == RELAY:
                dist = (2 + lax.broadcasted_iota(jnp.int32, (meta.shape[0], 1), 0) // SHARED) ^ 1
            slots[i][...] = jnp.where(meta[:, 1:2] == dist, meta[:, 0:1] - 1, -1)
            told_ref[...] = jnp.maximum(told_ref[...], meta[0:1, 2:3])

    off = 0
    for i in range(m):
        n = slots[i].shape[0]
        s = lax.dot_general(
            view(i, 0, width), a_ref[...], (((1,), (1,)), ((), ())), preferred_element_type=jnp.float32
        )
        s = jnp.where(group_of(s.shape) + g * per == slots[i][...], s, 0.0)
        v = s[:, :128]
        for c in range(128, s.shape[1], 128):
            v = v + s[:, c:c + 128]
        acc[off:off + n, :] += v
        off += n

    @pl.when(g == pl.num_programs(0) - 1)
    def _():
        off = 0
        for i in range(m):
            n = slots[i].shape[0]
            v = fold(acc[off:off + n, :])
            v = jnp.where(group_of(v.shape) == row_of(v.shape), v, 0.0)
            out_ref[off // 8:(off + n) // 8, :] = jnp.sum(v.reshape(n // 8, 8, 128), axis=1)
            off += n


def whole(shape):
    return pl.BlockSpec(shape, lambda g: (0,) * len(shape))


def scores(me, known, dists, got, store):
    block = got[0].ndim == 3
    sizes = [got[0].shape[1]] * len(dists) if block else [v.shape[0] for v in got]
    total, width = sum(sizes), store.shape[1]
    blk = 256
    out = pl.pallas_call(
        functools.partial(score_kernel, tuple(dists), block),
        grid=(store.shape[0] // blk,),
        in_specs=[pl.BlockSpec(memory_space=pltpu.SMEM), whole(known.shape)]
        + [whole(v.shape) for v in got] + [pl.BlockSpec((blk, width), lambda g: (g, 0))],
        out_specs=[whole((total // 8, 128)), whole((1, 1))] + [whole((n, 1)) for n in sizes],
        out_shape=[jax.ShapeDtypeStruct((total // 8, 128), jnp.float32), jax.ShapeDtypeStruct((1, 1), jnp.int32)]
        + [jax.ShapeDtypeStruct((n, 1), jnp.int32) for n in sizes],
        scratch_shapes=[pltpu.VMEM((total, 128), jnp.float32)],
        compiler_params=pltpu.CompilerParams(vmem_limit_bytes=VMEM),
        cost_estimate=FREE,
        name="scores",
    )(me, known, *got, store)
    return out[0], out[1], list(out[2:])


def spread_out(slots, packed, depth, spread):
    off = 0
    for i in range(len(slots)):
        n = slots[i].shape[0]
        v = packed[off // 8:(off + n) // 8, :]
        v = jnp.broadcast_to(v[:, None, :], (n // 8, 8, 128)).reshape(n, 128)
        group = group_of(v.shape)
        v = fold(jnp.where(group == row_of(v.shape), v, 0.0))
        for c in range(depth // 128):
            hit = group + c * 8 == slots[i][...]
            spread[i][:, c * 128:(c + 1) * 128] = jnp.where(hit, v, 0.0).astype(jnp.bfloat16)
        off += n


def delta_kernel(m, *refs):
    slots, packed, b_ref, outs, spread = refs[:m], refs[m], refs[m + 1], refs[m + 2:-m], refs[-m:]

    @pl.when(pl.program_id(0) == 0)
    def _():
        spread_out(slots, packed, b_ref.shape[0], spread)

    for i in range(m):
        outs[i][...] = jnp.dot(spread[i][...], b_ref[...], preferred_element_type=jnp.float32).astype(jnp.bfloat16)


def direct_kernel(n_dp, me_ref, *refs):
    m = n_dp - 1
    slots, packed, b_ref, outs, spread = refs[:m], refs[m], refs[m + 1], refs[m + 2:-m], refs[-m:]
    me = me_ref[0]

    @pl.when(pl.program_id(0) == 0)
    def _():
        spread_out(slots, packed, b_ref.shape[0], spread)

    block = outs[-1]
    block[me] = jnp.zeros(block.shape[1:], block.dtype)
    for i in range(m):
        v = jnp.dot(spread[i][...], b_ref[...], preferred_element_type=jnp.float32)
        if i < m - 1:
            outs[i][...] = v[:SHARED].astype(jnp.bfloat16)
            block[me ^ (i + 2)] = v[SHARED:].astype(jnp.bfloat16)
        else:
            block[me ^ 1] = v[:OWN].astype(jnp.bfloat16)
            outs[i][...] = v[OWN:].astype(jnp.bfloat16)


def deltas(slots, packed, store, me=None, n_dp=None):
    depth, width = store.shape
    cols = width // 4
    part = lambda n: pl.BlockSpec((n, cols), lambda g: (0, g))
    ins = [whole(v.shape) for v in slots] + [whole(packed.shape), part(depth)]
    if me is None:
        kernel, first, args = functools.partial(delta_kernel, len(slots)), [], []
        sizes, shapes = [v.shape[0] for v in slots], []
        outs = [part(n) for n in sizes]
    else:
        kernel, first, args = functools.partial(direct_kernel, n_dp), [pl.BlockSpec(memory_space=pltpu.SMEM)], [me]
        sizes, shapes = [SHARED] * (n_dp - 2) + [NEAR - OWN], [(n_dp, OWN, width)]
        outs = [part(n) for n in sizes] + [pl.BlockSpec((n_dp, OWN, cols), lambda g: (0, 0, g))]
    shapes = [(n, width) for n in sizes] + shapes
    return list(pl.pallas_call(
        kernel,
        grid=(width // cols,),
        in_specs=first + ins,
        out_specs=outs,
        out_shape=[jax.ShapeDtypeStruct(v, jnp.bfloat16) for v in shapes],
        scratch_shapes=[pltpu.VMEM((v.shape[0], depth), jnp.bfloat16) for v in slots],
        compiler_params=pltpu.CompilerParams(vmem_limit_bytes=VMEM),
        cost_estimate=FREE,
        name="deltas",
    )(*args, *slots, packed, store))


def finish_kernel(m, n_dp, me_ref, row_ref, *refs):
    codes, block_codes = refs[:m], refs[m:m + n_dp - 1]
    back, block, adds, out_ref = refs[m + n_dp - 1:2 * m + n_dp - 1], refs[2 * m + n_dp - 1], refs[2 * m + n_dp:-1], refs[-1]
    total = adds[0][...].astype(jnp.float32)
    for v in adds[1:]:
        total += v[...].astype(jnp.float32)
    codes = [c[...] for c in codes + block_codes]
    back = [b[...] for b in back] + [block[me_ref[0] ^ (1 + i)] for i in range(n_dp - 1)]
    for code, b in zip(codes, back):
        put = jnp.where(row_ref[...] == code, 1.0, 0.0).astype(jnp.bfloat16)
        total += jnp.dot(put, b, preferred_element_type=jnp.float32)
    out_ref[...] = total.astype(out_ref.dtype)


def finish(me, row_code, codes, block_codes, back, block, adds):
    rows, width = adds[0].shape
    cols = width // 4
    n_dp = block.shape[0]
    part = lambda v: pl.BlockSpec((v.shape[0], cols), lambda g: (0, g))
    return pl.pallas_call(
        functools.partial(finish_kernel, len(codes), n_dp),
        grid=(width // cols,),
        in_specs=[pl.BlockSpec(memory_space=pltpu.SMEM), whole(row_code.shape)]
        + [whole(v.shape) for v in codes + block_codes] + [part(v) for v in back]
        + [pl.BlockSpec((n_dp, OWN, cols), lambda g: (0, 0, g))] + [part(v) for v in adds],
        out_specs=pl.BlockSpec((rows, cols), lambda g: (0, g)),
        out_shape=jax.ShapeDtypeStruct((rows, width), jnp.bfloat16),
        compiler_params=pltpu.CompilerParams(vmem_limit_bytes=VMEM),
        name="finish",
    )(me, row_code, *codes, *block_codes, *back, block, *adds)


def column(row):
    n = row.shape[1]
    eye = lax.broadcasted_iota(jnp.int32, (n, n), 0) == lax.broadcasted_iota(jnp.int32, (n, n), 1)
    return jnp.sum(jnp.where(eye, jnp.broadcast_to(row, (n, n)), 0), axis=1, keepdims=True)


def row(col):
    n = col.shape[0]
    eye = lax.broadcasted_iota(jnp.int32, (n, n), 0) == lax.broadcasted_iota(jnp.int32, (n, n), 1)
    return jnp.sum(jnp.where(eye, jnp.broadcast_to(col, (n, n)), 0), axis=0, keepdims=True)


def segments(pos, alive, device, shift):
    n = pos.shape[1]
    dist = (pos >> shift) ^ device
    i = lax.broadcasted_iota(jnp.int32, (n, n), 0)
    j = lax.broadcasted_iota(jnp.int32, (n, n), 1)
    before = (column(dist) == dist) & (i < j)
    start = jnp.sum(jnp.where(before, column(alive), 0), axis=0, keepdims=True)
    return dist, start


def total(dist, alive, j):
    return jnp.sum(jnp.where(dist == j, alive, 0), axis=1, keepdims=True)


def over_of(dist, alive, j):
    return jnp.maximum(total(dist, alive, j - j % 2) - OWN, 0)


def iota_of(n, axis):
    return lax.broadcasted_iota(jnp.int32, (n, 1) if axis == 0 else (1, n), axis)


def near_code(big, axis):
    return big + iota_of(NEAR, axis)


def own_code(big, j, axis):
    return j * big + iota_of(OWN, axis)


def shared_code(big, j, over, axis):
    f = iota_of(SHARED, axis) + (j % 2) * SHARED
    even = j - j % 2
    return OWN + jnp.where(f < over, even * big + f, (even + 1) * big + f - over)


def far_code(big, j, over, axis):
    f = iota_of(SHARED + OWN, axis)
    g = f + (j % 2) * SHARED
    even = j - j % 2
    code = OWN + jnp.where(g < over, even * big + g, (even + 1) * big + g - over)
    return jnp.where(f < SHARED, code, j * big + f - SHARED)


def pack_kernel(n_dp, seg_len, shift, me_ref, ids_ref, lives_ref, index_ref, x_ref,
                table_ref, row_ref, self_ref, meta_ref, rounds_ref, *outs):
    me = me_ref[0]
    count, (rows, width) = ids_ref.shape[1], x_ref.shape
    big = 2 * rows
    lives = lives_ref[...]
    hit = column(ids_ref[...]) == lax.broadcasted_iota(jnp.int32, (count, index_ref.shape[1]), 1)
    pos = row(jnp.sum(jnp.where(hit, index_ref[...], 0), axis=1, keepdims=True))
    table_ref[0:1, :] = pos
    table_ref[1:2, :] = lives
    dist, start = segments(pos, lives, me, shift)
    code = dist * big + start
    slot = pos & ((1 << shift) - 1)

    def spread(value, axis):
        shape = (count, rows) if axis == 1 else (rows, count)
        r = lax.broadcasted_iota(jnp.int32, shape, axis)
        seg = lax.broadcasted_iota(jnp.int32, shape, 1 - axis)
        v = column(value) if axis == 1 else value
        return jnp.sum(jnp.where(r // seg_len == seg, v, 0), axis=1 - axis, keepdims=True)

    def rows_code(axis):
        lane = iota_of(rows, axis) % seg_len
        return jnp.where(lane < spread(lives, axis), spread(code, axis) + lane, -1)

    by_row, by_lane = rows_code(0), rows_code(1)
    row_slot, row_dist = spread(slot, 0), spread(dist, 0)
    row_ref[...] = by_row
    self_ref[...] = jnp.where((by_row >= 0) & (row_dist == 0), row_slot, -1)
    lane = lax.broadcasted_iota(jnp.int32, (rows, META), 1)
    meta = jnp.where(lane == 0, row_slot + 1, jnp.where(lane == 1, row_dist, 0))
    meta = meta.astype(jnp.float32).astype(jnp.bfloat16)
    meta_ref[...] = meta

    left = total(dist, lives, 1) - NEAR
    for j in range(2, n_dp):
        held = OWN + 2 * SHARED if j % 2 == 0 else OWN + jnp.maximum(2 * SHARED - over_of(dist, lives, j), 0)
        left = jnp.maximum(left, total(dist, lives, j) - held)
    rounds = (jnp.maximum(left, 0) + ROUND - 1) // ROUND
    rounds_ref[...] = rounds
    told = jnp.where(lax.broadcasted_iota(jnp.int32, (1, META), 1) == 2, rounds.astype(jnp.float32), 0.0)

    far = range(2, n_dp)
    codes = [far_code(big, j, over_of(dist, lives, j), 0) for j in far] + [near_code(big, 0)]
    m = len(codes)
    for c, out in zip(codes, outs[:m]):
        pick = jnp.where(c == by_lane, 1.0, 0.0).astype(jnp.bfloat16)
        out[:, :width] = jnp.dot(pick, x_ref[...], preferred_element_type=jnp.float32).astype(jnp.bfloat16)
        out[:, width:] = (jnp.dot(pick, meta, preferred_element_type=jnp.float32) + told).astype(jnp.bfloat16)
    lanes = [shared_code(big, j, over_of(dist, lives, j), 1) for j in far]
    lanes += [big + OWN + iota_of(NEAR - OWN, 1)]
    lanes += [own_code(big, j, 1) for j in range(1, n_dp)]
    for c, out in zip(lanes, outs[m:]):
        out[...] = c


def vmem(count):
    return [pl.BlockSpec(memory_space=pltpu.VMEM) for _ in range(count)]


def packs(me, ids, lives, index, x, n_dp, seg_len, shift):
    count, (rows, width) = ids.shape[1], x.shape
    sizes = [SHARED + OWN] * (n_dp - 2) + [NEAR]
    parts = [SHARED] * (n_dp - 2) + [NEAR - OWN] + [OWN] * (n_dp - 1)
    shapes = [((2, count), jnp.int32), ((rows, 1), jnp.int32), ((rows, 1), jnp.int32)]
    shapes += [((rows, META), jnp.bfloat16), ((1, 1), jnp.int32)]
    shapes += [((n, width + META), jnp.bfloat16) for n in sizes] + [((1, n), jnp.int32) for n in parts]
    return pl.pallas_call(
        functools.partial(pack_kernel, n_dp, seg_len, shift),
        in_specs=[pl.BlockSpec(memory_space=pltpu.SMEM)] + vmem(4),
        out_specs=vmem(len(shapes)),
        out_shape=[jax.ShapeDtypeStruct(*v) for v in shapes],
        compiler_params=pltpu.CompilerParams(vmem_limit_bytes=VMEM),
        cost_estimate=FREE,
        name="pack",
    )(me, ids, lives, index, x)


def share_kernel(at_ref, x_ref, w_ref, out_ref):
    out_ref[...] = jnp.dot(x_ref[...], w_ref[...], preferred_element_type=jnp.float32).astype(jnp.bfloat16)


def share(at, x, weight, cols):
    rows, depth = x.shape
    tile = min(512, cols)
    return pl.pallas_call(
        share_kernel,
        grid_spec=pltpu.PrefetchScalarGridSpec(
            num_scalar_prefetch=1,
            grid=(cols // tile,),
            in_specs=[
                pl.BlockSpec((rows, depth), lambda g, at: (0, 0)),
                pl.BlockSpec((depth, tile), lambda g, at: (0, at[0] * (cols // tile) + g)),
            ],
            out_specs=pl.BlockSpec((rows, tile), lambda g, at: (0, g)),
        ),
        out_shape=jax.ShapeDtypeStruct((rows, cols), jnp.bfloat16),
        compiler_params=pltpu.CompilerParams(vmem_limit_bytes=VMEM),
        cost_estimate=FREE,
        name="share",
    )(at, x, weight)


def per_device(
    attention_output,
    output_projection_weight,
    shrink_matrix_store,
    expand_matrix_store,
    segment_adapter,
    segment_live_rows,
    adapter_store_index,
):
    steps, rows_dev, width = attention_output.shape
    seg_count = segment_adapter.shape[1]
    seg_len = rows_dev // seg_count
    store, rank, _ = shrink_matrix_store.shape
    n_dp, n_tp = lax.axis_size("dp"), lax.axis_size("tp")
    me = lax.axis_index("dp").reshape(1)
    rows = steps * rows_dev
    count = steps * seg_count
    shift = store.bit_length() - 1
    big = 2 * rows
    far = range(2, n_dp)

    x = attention_output.reshape(rows, width)
    shrink_store = shrink_matrix_store.reshape(store * rank, width)
    expand_store = expand_matrix_store.reshape(store * rank, width)
    weight = output_projection_weight

    def swap(v, axis, k):
        n = lax.axis_size(axis)
        return lax.ppermute(v, axis, [(i, i ^ k) for i in range(n)])

    def butterfly(v, axis, op):
        k = 1
        while k < lax.axis_size(axis):
            v = op(v, swap(v, axis, k))
            k *= 2
        return v

    def answer(dists, got, known):
        scored, told, slots = scores(me, known, dists, got, shrink_store)
        return slots, told, butterfly(scored, "tp", jnp.add)

    def total_of(parts):
        if len(parts) == 1:
            return parts[0]
        return functools.reduce(jnp.add, [v.astype(jnp.float32) for v in parts]).astype(jnp.bfloat16)

    def a2a(v):
        return lax.all_to_all(v, "dp", split_axis=0, concat_axis=0, tiled=True)

    def after(v, *others):
        return lax.optimization_barrier((v, others))[0]

    packed = list(packs(
        me,
        segment_adapter.reshape(1, count),
        segment_live_rows.reshape(1, count),
        adapter_store_index.reshape(1, -1),
        x, n_dp, seg_len, shift,
    ))
    table, row_code, self_slots, meta, rounds = packed[:5]
    m = len(far)
    out_far, out_near = packed[5:5 + m], packed[5 + m]
    codes, block_codes = packed[6 + m:7 + 2 * m], packed[7 + 2 * m:]

    in_far = [swap(v, "dp", j) for v, j in zip(out_far, far)]
    in_near = swap(out_near, "dp", 1)

    found, _, self_part = answer([None], [after(x, table)], self_slots)
    (self_delta,) = deltas(found, self_part, expand_store)

    at = after(lax.axis_index("tp").reshape(1), table)
    cols = weight.shape[1] // n_tp
    shares = {k: share(at ^ k, x, weight, cols) for k in reversed(range(n_tp))}
    (in_far, in_near, shares), _ = lax.optimization_barrier(((in_far, in_near, shares), self_delta))

    found, rounds, part = answer(list(far) + [1], in_far + [in_near], rounds)
    in_far, shares, _ = lax.optimization_barrier((in_far, shares, rounds))
    in_relay = swap(jnp.concatenate([v[:SHARED] for v in in_far]), "dp", 1)
    direct = deltas(found, part, expand_store, me, n_dp)
    block = a2a(direct[-1])

    adds = {k: [shares[k]] for k in shares}
    for k in range(1, n_tp, 2):
        adds[k ^ 1].append(swap(adds.pop(k)[0], "tp", 1))
    for k in range(2, n_tp, 2):
        adds[k] = [total_of(adds[k])]

    in_relay, direct, adds = lax.optimization_barrier((in_relay, direct, adds))
    found, _, part = answer([RELAY], [in_relay], rounds)
    part, adds = lax.optimization_barrier((part, adds))
    (relayed,) = deltas(found, part, expand_store)
    relayed = swap(relayed, "dp", 1)
    bit = 2
    while bit < n_tp:
        for k in sorted((k for k in adds if k & bit), reverse=True):
            adds[k ^ bit].append(swap(total_of(adds.pop(k)), "tp", bit))
        bit *= 2
    relayed, block, near, direct = lax.optimization_barrier((relayed, block, direct[m], direct))
    back = [swap(direct[i] + relayed[i * SHARED:(i + 1) * SHARED], "dp", j) for i, j in enumerate(far)]
    back.append(swap(near, "dp", 1))
    adds = adds[0] + [self_delta]
    rounds = butterfly(rounds, "rep", jnp.maximum)[0, 0]

    def late_round(i, out):
        tab, rows_in, rows_meta, places = lax.optimization_barrier((table, x, meta, row_code, i))[:4]
        pos, alive = tab[0], tab[1]
        dist = (pos >> shift) ^ me[0]
        held = [None, jnp.int32(NEAR)]
        for j in range(2, n_dp, 2):
            extra = jnp.maximum(jnp.sum(jnp.where(dist == j, alive, 0)) - OWN, 0)
            held += [jnp.int32(OWN + 2 * SHARED), OWN + jnp.maximum(2 * SHARED - extra, 0)]
        x_meta = jnp.concatenate([rows_in, rows_meta], axis=1)
        code = [j * big + held[j] + i * ROUND + jnp.arange(ROUND, dtype=jnp.int32) for j in range(1, n_dp)]
        got = []
        for j, c in zip(range(1, n_dp), code):
            pick = (c[:, None] == places.reshape(1, rows)).astype(jnp.bfloat16)
            v = jnp.dot(pick, x_meta, preferred_element_type=jnp.float32).astype(jnp.bfloat16)
            got.append(swap(v, "dp", j))
        found, _, part = answer(list(range(1, n_dp)), got, rounds.reshape(1, 1))
        total = out.astype(jnp.float32)
        for j, c, v in zip(range(1, n_dp), code, deltas(found, part, expand_store)):
            put = (places == c[None, :]).astype(jnp.bfloat16)
            total = total + jnp.dot(put, swap(v, "dp", j), preferred_element_type=jnp.float32)
        return total.astype(jnp.bfloat16)

    out = finish(me, row_code, codes, block_codes, back, block, adds)
    out = lax.fori_loop(0, rounds, late_round, out)
    return out.reshape(steps, rows_dev, width)


def solution(mesh):
    return jax.shard_map(
        per_device,
        mesh=mesh,
        in_specs=(
            P(None, ("rep", "dp"), "tp"),
            P("tp", None),
            P("dp", None, "tp"),
            P("dp", None, "tp"),
            P(None, ("rep", "dp")),
            P(None, ("rep", "dp")),
            P("rep"),
        ),
        out_specs=P(None, ("rep", "dp"), "tp"),
        check_vma=False,
    )
```

```python
import functools

import jax
import jax.numpy as jnp
from jax import lax
from jax.experimental import pallas as pl
from jax.experimental.pallas import tpu as pltpu
from jax.sharding import PartitionSpec as P

NEAR = 208
OWN = 72
SHARED = 64
ROUND = 64
META = 128
RELAY = -1
VMEM = 48 * 2**20
FREE = pl.CostEstimate(flops=0, bytes_accessed=0, transcendentals=0)


def group_of(shape):
    return lax.broadcasted_iota(jnp.int32, shape, 1) // 16


def row_of(shape):
    return lax.broadcasted_iota(jnp.int32, shape, 0) % 8


def fold(v):
    for shift in (64, 32, 16):
        v = v + pltpu.roll(v, shift, axis=1)
    return v


def score_kernel(dists, block, *refs):
    me_ref, known_ref, refs = refs[0], refs[1], refs[2:]
    m = len(dists)
    count = m - block + (block > 0)
    got, a_ref, refs = refs[:count], refs[count], refs[count + 1:]
    out_ref, told_ref, slots, acc = refs[0], refs[1], refs[2:-1], refs[-1]
    g = pl.program_id(0)
    per, width = a_ref.shape[0] // 16, a_ref.shape[1]

    def view(i, low, high):
        if i < block:
            return got[0][me_ref[0] ^ (i + 1), :, low:high]
        return got[i - block + (block > 0)][:, low:high]

    @pl.when(g == 0)
    def _():
        acc[...] = jnp.zeros_like(acc)
        told_ref[...] = known_ref[0:1, 0:1]
        for i, dist in enumerate(dists):
            if dist is None:
                slots[i][...] = known_ref[...]
                continue
            meta = view(i, width, width + META).astype(jnp.float32).astype(jnp.int32)
            if dist == RELAY:
                dist = (2 + lax.broadcasted_iota(jnp.int32, (meta.shape[0], 1), 0) // SHARED) ^ 1
            slots[i][...] = jnp.where(meta[:, 1:2] == dist, meta[:, 0:1] - 1, -1)
            told_ref[...] = jnp.maximum(told_ref[...], meta[0:1, 2:3])

    off = 0
    for i in range(m):
        n = slots[i].shape[0]
        s = lax.dot_general(
            view(i, 0, width), a_ref[...], (((1,), (1,)), ((), ())), preferred_element_type=jnp.float32
        )
        s = jnp.where(group_of(s.shape) + g * per == slots[i][...], s, 0.0)
        v = s[:, :128]
        for c in range(128, s.shape[1], 128):
            v = v + s[:, c:c + 128]
        acc[off:off + n, :] += v
        off += n

    @pl.when(g == pl.num_programs(0) - 1)
    def _():
        off = 0
        for i in range(m):
            n = slots[i].shape[0]
            v = fold(acc[off:off + n, :])
            v = jnp.where(group_of(v.shape) == row_of(v.shape), v, 0.0)
            out_ref[off // 8:(off + n) // 8, :] = jnp.sum(v.reshape(n // 8, 8, 128), axis=1)
            off += n


def whole(shape):
    return pl.BlockSpec(shape, lambda g: (0,) * len(shape))


def scores(me, known, dists, got, store):
    block = got[0].shape[0] - 1 if got[0].ndim == 3 else 0
    sizes = [OWN] * block + [v.shape[0] for v in got if v.ndim == 2]
    total, width = sum(sizes), store.shape[1]
    blk = 256
    out = pl.pallas_call(
        functools.partial(score_kernel, tuple(dists), block),
        grid=(store.shape[0] // blk,),
        in_specs=[pl.BlockSpec(memory_space=pltpu.SMEM), whole(known.shape)]
        + [whole(v.shape) for v in got] + [pl.BlockSpec((blk, width), lambda g: (g, 0))],
        out_specs=[whole((total // 8, 128)), whole((1, 1))] + [whole((n, 1)) for n in sizes],
        out_shape=[jax.ShapeDtypeStruct((total // 8, 128), jnp.float32), jax.ShapeDtypeStruct((1, 1), jnp.int32)]
        + [jax.ShapeDtypeStruct((n, 1), jnp.int32) for n in sizes],
        scratch_shapes=[pltpu.VMEM((total, 128), jnp.float32)],
        compiler_params=pltpu.CompilerParams(vmem_limit_bytes=VMEM),
        cost_estimate=FREE,
        name="scores",
    )(me, known, *got, store)
    return out[0], out[1], list(out[2:])


def spread_out(slots, packed, depth, spread, off):
    for i in range(len(slots)):
        n = slots[i].shape[0]
        v = packed[off // 8:(off + n) // 8, :]
        v = jnp.broadcast_to(v[:, None, :], (n // 8, 8, 128)).reshape(n, 128)
        group = group_of(v.shape)
        v = fold(jnp.where(group == row_of(v.shape), v, 0.0))
        for c in range(depth // 128):
            hit = group + c * 8 == slots[i][...]
            spread[i][:, c * 128:(c + 1) * 128] = jnp.where(hit, v, 0.0).astype(jnp.bfloat16)
        off += n


def delta_kernel(m, skip, block, me_ref, *refs):
    slots, packed, b_ref, outs, spread = refs[:m], refs[m], refs[m + 1], refs[m + 2:-m], refs[-m:]

    @pl.when(pl.program_id(0) == 0)
    def _():
        spread_out(slots, packed, b_ref.shape[0], spread, skip)

    if block:
        outs[0][me_ref[0]] = jnp.zeros(outs[0].shape[1:], outs[0].dtype)
    for i in range(m):
        v = jnp.dot(spread[i][...], b_ref[...], preferred_element_type=jnp.float32).astype(jnp.bfloat16)
        if i < block:
            outs[0][me_ref[0] ^ (i + 1)] = v
        else:
            outs[i - block + (block > 0)][...] = v


def deltas(me, slots, packed, store, skip=0, block=0):
    depth, width = store.shape
    cols = width // 4
    sizes = [v.shape[0] for v in slots]
    part = lambda n: pl.BlockSpec((n, cols), lambda g: (0, g))
    outs = [pl.BlockSpec((block + 1, OWN, cols), lambda g: (0, 0, g))] if block else []
    shapes = [(block + 1, OWN, width)] if block else []
    outs += [part(n) for n in sizes[block:]]
    shapes += [(n, width) for n in sizes[block:]]
    return list(pl.pallas_call(
        functools.partial(delta_kernel, len(slots), skip, block),
        grid=(width // cols,),
        in_specs=[pl.BlockSpec(memory_space=pltpu.SMEM)] + [whole(v.shape) for v in slots]
        + [whole(packed.shape), part(depth)],
        out_specs=outs,
        out_shape=[jax.ShapeDtypeStruct(v, jnp.bfloat16) for v in shapes],
        scratch_shapes=[pltpu.VMEM((n, depth), jnp.bfloat16) for n in sizes],
        compiler_params=pltpu.CompilerParams(vmem_limit_bytes=VMEM),
        cost_estimate=FREE,
        name="deltas",
    )(me, *slots, packed, store))


def finish_kernel(m, n_dp, me_ref, row_ref, *refs):
    codes, block_codes = refs[:m], refs[m:m + n_dp - 1]
    back, block, adds, out_ref = refs[m + n_dp - 1:2 * m + n_dp - 1], refs[2 * m + n_dp - 1], refs[2 * m + n_dp:-1], refs[-1]
    total = adds[0][...].astype(jnp.float32)
    for v in adds[1:]:
        total += v[...].astype(jnp.float32)
    codes = [c[...] for c in codes + block_codes]
    back = [b[...] for b in back] + [block[me_ref[0] ^ (1 + i)] for i in range(n_dp - 1)]
    for code, b in zip(codes, back):
        put = jnp.where(row_ref[...] == code, 1.0, 0.0).astype(jnp.bfloat16)
        total += jnp.dot(put, b, preferred_element_type=jnp.float32)
    out_ref[...] = total.astype(out_ref.dtype)


def finish(me, row_code, codes, block_codes, back, block, adds):
    rows, width = adds[0].shape
    cols = width // 4
    n_dp = block.shape[0]
    part = lambda v: pl.BlockSpec((v.shape[0], cols), lambda g: (0, g))
    return pl.pallas_call(
        functools.partial(finish_kernel, len(codes), n_dp),
        grid=(width // cols,),
        in_specs=[pl.BlockSpec(memory_space=pltpu.SMEM), whole(row_code.shape)]
        + [whole(v.shape) for v in codes + block_codes] + [part(v) for v in back]
        + [pl.BlockSpec((n_dp, OWN, cols), lambda g: (0, 0, g))] + [part(v) for v in adds],
        out_specs=pl.BlockSpec((rows, cols), lambda g: (0, g)),
        out_shape=jax.ShapeDtypeStruct((rows, width), jnp.bfloat16),
        compiler_params=pltpu.CompilerParams(vmem_limit_bytes=VMEM),
        name="finish",
    )(me, row_code, *codes, *block_codes, *back, block, *adds)


def column(row):
    n = row.shape[1]
    eye = lax.broadcasted_iota(jnp.int32, (n, n), 0) == lax.broadcasted_iota(jnp.int32, (n, n), 1)
    return jnp.sum(jnp.where(eye, jnp.broadcast_to(row, (n, n)), 0), axis=1, keepdims=True)


def row(col):
    n = col.shape[0]
    eye = lax.broadcasted_iota(jnp.int32, (n, n), 0) == lax.broadcasted_iota(jnp.int32, (n, n), 1)
    return jnp.sum(jnp.where(eye, jnp.broadcast_to(col, (n, n)), 0), axis=0, keepdims=True)


def segments(pos, alive, device, shift):
    n = pos.shape[1]
    dist = (pos >> shift) ^ device
    i = lax.broadcasted_iota(jnp.int32, (n, n), 0)
    j = lax.broadcasted_iota(jnp.int32, (n, n), 1)
    before = (column(dist) == dist) & (i < j)
    start = jnp.sum(jnp.where(before, column(alive), 0), axis=0, keepdims=True)
    return dist, start


def total(dist, alive, j):
    return jnp.sum(jnp.where(dist == j, alive, 0), axis=1, keepdims=True)


def over_of(dist, alive, j):
    return jnp.maximum(total(dist, alive, j - j % 2) - OWN, 0)


def iota_of(n, axis):
    return lax.broadcasted_iota(jnp.int32, (n, 1) if axis == 0 else (1, n), axis)


def near_code(big, axis):
    return big + OWN + iota_of(NEAR - OWN, axis)


def own_code(big, j, axis):
    return j * big + iota_of(OWN, axis)


def shared_code(big, j, over, axis):
    f = iota_of(SHARED, axis) + (j % 2) * SHARED
    even = j - j % 2
    return OWN + jnp.where(f < over, even * big + f, (even + 1) * big + f - over)


def flat_column(v):
    a, b = v.shape
    i = lax.broadcasted_iota(jnp.int32, (a * b, b), 0)
    j = lax.broadcasted_iota(jnp.int32, (a * b, b), 1)
    out = jnp.zeros((a * b, b), jnp.int32)
    for k in range(a):
        out += jnp.where(i - j == k * b, v[k:k + 1, :], 0)
    return jnp.sum(out, axis=1, keepdims=True)


def pack_kernel(n_dp, seg_len, shift, me_ref, ids_ref, lives_ref, index_ref, x_ref,
                table_ref, row_ref, self_ref, meta_ref, rounds_ref, block, *outs):
    me = me_ref[0]
    count, (rows, width) = ids_ref.shape[0] * ids_ref.shape[1], x_ref.shape
    big = 2 * rows
    lives = row(flat_column(lives_ref[...]))
    hit = flat_column(ids_ref[...]) == lax.broadcasted_iota(jnp.int32, (count, index_ref.shape[1]), 1)
    pos = row(jnp.sum(jnp.where(hit, index_ref[...], 0), axis=1, keepdims=True))
    table_ref[0:1, :] = pos
    table_ref[1:2, :] = lives
    dist, start = segments(pos, lives, me, shift)
    code = dist * big + start
    slot = pos & ((1 << shift) - 1)

    def spread(value, axis):
        shape = (count, rows) if axis == 1 else (rows, count)
        r = lax.broadcasted_iota(jnp.int32, shape, axis)
        seg = lax.broadcasted_iota(jnp.int32, shape, 1 - axis)
        v = column(value) if axis == 1 else value
        return jnp.sum(jnp.where(r // seg_len == seg, v, 0), axis=1 - axis, keepdims=True)

    def rows_code(axis):
        lane = iota_of(rows, axis) % seg_len
        return jnp.where(lane < spread(lives, axis), spread(code, axis) + lane, -1)

    by_row, by_lane = rows_code(0), rows_code(1)
    row_slot, row_dist = spread(slot, 0), spread(dist, 0)
    row_ref[...] = by_row
    self_ref[...] = jnp.where((by_row >= 0) & (row_dist == 0), row_slot, -1)
    lane = lax.broadcasted_iota(jnp.int32, (rows, META), 1)
    meta = jnp.where(lane == 0, row_slot + 1, jnp.where(lane == 1, row_dist, 0))
    meta = meta.astype(jnp.float32).astype(jnp.bfloat16)
    meta_ref[...] = meta

    left = total(dist, lives, 1) - NEAR
    for j in range(2, n_dp):
        held = OWN + 2 * SHARED if j % 2 == 0 else OWN + jnp.maximum(2 * SHARED - over_of(dist, lives, j), 0)
        left = jnp.maximum(left, total(dist, lives, j) - held)
    rounds = (jnp.maximum(left, 0) + ROUND - 1) // ROUND
    rounds_ref[...] = rounds
    told = jnp.where(lax.broadcasted_iota(jnp.int32, (1, META), 1) == 2, rounds.astype(jnp.float32), 0.0)

    def chosen(c):
        pick = jnp.where(c == by_lane, 1.0, 0.0).astype(jnp.bfloat16)
        v = jnp.dot(pick, x_ref[...], preferred_element_type=jnp.float32).astype(jnp.bfloat16)
        return v, (jnp.dot(pick, meta, preferred_element_type=jnp.float32) + told).astype(jnp.bfloat16)

    far = range(2, n_dp)
    block[me] = jnp.zeros(block.shape[1:], block.dtype)
    for j in range(1, n_dp):
        v, u = chosen(own_code(big, j, 0))
        block[me ^ j, :, :width] = v
        block[me ^ j, :, width:] = u
    codes = [shared_code(big, j, over_of(dist, lives, j), 0) for j in far] + [near_code(big, 0)]
    m = len(codes)
    for c, out in zip(codes, outs[:m]):
        out[:, :width], out[:, width:] = chosen(c)
    lanes = [shared_code(big, j, over_of(dist, lives, j), 1) for j in far] + [near_code(big, 1)]
    lanes += [own_code(big, j, 1) for j in range(1, n_dp)]
    for c, out in zip(lanes, outs[m:]):
        out[...] = c


def vmem(count):
    return [pl.BlockSpec(memory_space=pltpu.VMEM) for _ in range(count)]


def packs(me, ids, lives, index, x, n_dp, seg_len, shift):
    count, (rows, width) = ids.shape[0] * ids.shape[1], x.shape
    sizes = [SHARED] * (n_dp - 2) + [NEAR - OWN]
    shapes = [((2, count), jnp.int32), ((rows, 1), jnp.int32), ((rows, 1), jnp.int32)]
    shapes += [((rows, META), jnp.bfloat16), ((1, 1), jnp.int32), ((n_dp, OWN, width + META), jnp.bfloat16)]
    shapes += [((n, width + META), jnp.bfloat16) for n in sizes]
    shapes += [((1, n), jnp.int32) for n in sizes + [OWN] * (n_dp - 1)]
    return pl.pallas_call(
        functools.partial(pack_kernel, n_dp, seg_len, shift),
        in_specs=[pl.BlockSpec(memory_space=pltpu.SMEM)] + vmem(4),
        out_specs=vmem(len(shapes)),
        out_shape=[jax.ShapeDtypeStruct(*v) for v in shapes],
        compiler_params=pltpu.CompilerParams(vmem_limit_bytes=VMEM),
        cost_estimate=FREE,
        name="pack",
    )(me, ids, lives, index, x)


def share_kernel(at_ref, x_ref, w_ref, out_ref):
    out_ref[...] = jnp.dot(x_ref[...], w_ref[...], preferred_element_type=jnp.float32).astype(jnp.bfloat16)


def share(at, x, weight, cols):
    rows, depth = x.shape
    tile = min(512, cols)
    return pl.pallas_call(
        share_kernel,
        grid_spec=pltpu.PrefetchScalarGridSpec(
            num_scalar_prefetch=1,
            grid=(cols // tile,),
            in_specs=[
                pl.BlockSpec((rows, depth), lambda g, at: (0, 0)),
                pl.BlockSpec((depth, tile), lambda g, at: (0, at[0] * (cols // tile) + g)),
            ],
            out_specs=pl.BlockSpec((rows, tile), lambda g, at: (0, g)),
        ),
        out_shape=jax.ShapeDtypeStruct((rows, cols), jnp.bfloat16),
        compiler_params=pltpu.CompilerParams(vmem_limit_bytes=VMEM),
        cost_estimate=FREE,
        name="share",
    )(at, x, weight)


def per_device(
    attention_output,
    output_projection_weight,
    shrink_matrix_store,
    expand_matrix_store,
    segment_adapter,
    segment_live_rows,
    adapter_store_index,
):
    steps, rows_dev, width = attention_output.shape
    seg_count = segment_adapter.shape[1]
    seg_len = rows_dev // seg_count
    store, rank, _ = shrink_matrix_store.shape
    n_dp, n_tp = lax.axis_size("dp"), lax.axis_size("tp")
    me = lax.axis_index("dp").reshape(1)
    rows = steps * rows_dev
    count = steps * seg_count
    shift = store.bit_length() - 1
    big = 2 * rows
    far = range(2, n_dp)

    x = attention_output.reshape(rows, width)
    shrink_store = shrink_matrix_store.reshape(store * rank, width)
    expand_store = expand_matrix_store.reshape(store * rank, width)
    weight = output_projection_weight

    def swap(v, axis, k):
        n = lax.axis_size(axis)
        return lax.ppermute(v, axis, [(i, i ^ k) for i in range(n)])

    def butterfly(v, axis, op):
        k = 1
        while k < lax.axis_size(axis):
            v = op(v, swap(v, axis, k))
            k *= 2
        return v

    def answer(dists, got, known):
        scored, told, slots = scores(me, known, dists, got, shrink_store)
        return slots, told, butterfly(scored, "tp", jnp.add)

    def total_of(parts):
        if len(parts) == 1:
            return parts[0]
        return functools.reduce(jnp.add, [v.astype(jnp.float32) for v in parts]).astype(jnp.bfloat16)

    def a2a(v):
        return lax.all_to_all(v, "dp", split_axis=0, concat_axis=0, tiled=True)

    def after(v, *others):
        return lax.optimization_barrier((v, others))[0]

    packed = list(packs(
        me, segment_adapter, segment_live_rows, adapter_store_index.reshape(1, -1), x, n_dp, seg_len, shift
    ))
    table, row_code, self_slots, meta, rounds, block = packed[:6]
    m = len(far)
    out_shared, out_near, codes = packed[6:6 + m], packed[6 + m], packed[7 + m:]
    codes, block_codes = codes[:m + 1], codes[m + 1:]

    in_shared = [swap(v, "dp", j) for v, j in zip(out_shared, far)]
    in_near = swap(out_near, "dp", 1)

    self_found, _, self_part = answer([None], [after(x, table)], self_slots)
    block = a2a(after(block, self_part))

    at = after(lax.axis_index("tp").reshape(1), self_part)
    cols = weight.shape[1] // n_tp
    early = [k for k in reversed(range(n_tp)) if k >= n_tp // 2]
    shares = {k: share(at ^ k, x, weight, cols) for k in early}

    in_shared, in_near, shares = lax.optimization_barrier((in_shared, in_near, shares))
    in_relay = jnp.concatenate(in_shared)
    at = after(at, in_relay)
    in_relay = swap(in_relay, "dp", 1)
    for k in reversed(range(n_tp)):
        if k not in early:
            shares[k] = share(at ^ k, x, weight, cols)
    (self_delta,) = deltas(me, self_found, after(self_part, in_relay), expand_store)

    adds = {k: [shares[k]] for k in shares}
    for k in range(1, n_tp, 2):
        adds[k ^ 1].append(swap(adds.pop(k)[0], "tp", 1))
    for k in range(2, n_tp, 2):
        adds[k] = [total_of(adds[k])]

    got, self_delta, adds = lax.optimization_barrier(
        ([block] + in_shared + [in_near, in_relay], self_delta, adds)
    )
    found, rounds, part = answer(list(range(1, n_dp)) + list(far) + [1, RELAY], got, rounds)
    part, adds = lax.optimization_barrier((part, adds))
    skip = sum(v.shape[0] for v in found[:-1])
    (relayed,) = deltas(me, found[-1:], part, expand_store, skip)
    late = deltas(me, found[:-1], after(part, relayed), expand_store, 0, n_dp - 1)
    relayed = swap(relayed, "dp", 1)
    block = a2a(late[0])
    bit = 2
    while bit < n_tp:
        for k in sorted((k for k in adds if k & bit), reverse=True):
            adds[k ^ bit].append(swap(total_of(adds.pop(k)), "tp", bit))
        bit *= 2
    relayed, block, late = lax.optimization_barrier((relayed, block, late[1:]))
    back = [swap(late[i] + relayed[i * SHARED:(i + 1) * SHARED], "dp", j) for i, j in enumerate(far)]
    back.append(swap(late[m], "dp", 1))
    adds = adds[0] + [self_delta]
    rounds = butterfly(rounds, "rep", jnp.maximum)[0, 0]

    def late_round(i, out):
        tab, rows_in, rows_meta, places = lax.optimization_barrier((table, x, meta, row_code, i))[:4]
        pos, alive = tab[0], tab[1]
        dist = (pos >> shift) ^ me[0]
        held = [None, jnp.int32(NEAR)]
        for j in range(2, n_dp, 2):
            extra = jnp.maximum(jnp.sum(jnp.where(dist == j, alive, 0)) - OWN, 0)
            held += [jnp.int32(OWN + 2 * SHARED), OWN + jnp.maximum(2 * SHARED - extra, 0)]
        x_meta = jnp.concatenate([rows_in, rows_meta], axis=1)
        code = [j * big + held[j] + i * ROUND + jnp.arange(ROUND, dtype=jnp.int32) for j in range(1, n_dp)]
        got = []
        for j, c in zip(range(1, n_dp), code):
            pick = (c[:, None] == places.reshape(1, rows)).astype(jnp.bfloat16)
            v = jnp.dot(pick, x_meta, preferred_element_type=jnp.float32).astype(jnp.bfloat16)
            got.append(swap(v, "dp", j))
        found, _, part = answer(list(range(1, n_dp)), got, rounds.reshape(1, 1))
        total = out.astype(jnp.float32)
        for j, c, v in zip(range(1, n_dp), code, deltas(me, found, part, expand_store)):
            put = (places == c[None, :]).astype(jnp.bfloat16)
            total = total + jnp.dot(put, swap(v, "dp", j), preferred_element_type=jnp.float32)
        return total.astype(jnp.bfloat16)

    out = finish(me, row_code, codes, block_codes, back, block, adds)
    out = lax.fori_loop(0, rounds, late_round, out)
    return out.reshape(steps, rows_dev, width)


def solution(mesh):
    return jax.shard_map(
        per_device,
        mesh=mesh,
        in_specs=(
            P(None, ("rep", "dp"), "tp"),
            P("tp", None),
            P("dp", None, "tp"),
            P("dp", None, "tp"),
            P(None, ("rep", "dp")),
            P(None, ("rep", "dp")),
            P("rep"),
        ),
        out_specs=P(None, ("rep", "dp"), "tp"),
        check_vma=False,
    )
```

```python
import functools

import jax
import jax.numpy as jnp
from jax import lax
from jax.experimental import pallas as pl
from jax.experimental.pallas import tpu as pltpu
from jax.sharding import PartitionSpec as P

NEAR = 208
OWN = 72
SHARED = 64
ROUND = 64
META = 128
RELAY = -1
VMEM = 48 * 2**20
FREE = pl.CostEstimate(flops=0, bytes_accessed=0, transcendentals=0)


def group_of(shape):
    return lax.broadcasted_iota(jnp.int32, shape, 1) // 16


def row_of(shape):
    return lax.broadcasted_iota(jnp.int32, shape, 0) % 8


def fold(v):
    for shift in (64, 32, 16):
        v = v + pltpu.roll(v, shift, axis=1)
    return v


def score_kernel(dists, block, *refs):
    me_ref, known_ref, refs = refs[0], refs[1], refs[2:]
    m = len(dists)
    got, a_ref, refs = refs[:1 if block else m], refs[1 if block else m], refs[(2 if block else m + 1):]
    out_ref, told_ref, slots, acc = refs[0], refs[1], refs[2:-1], refs[-1]
    g = pl.program_id(0)
    per, width = a_ref.shape[0] // 16, a_ref.shape[1]

    def view(i, low, high):
        return got[0][me_ref[0] ^ (i + 1), :, low:high] if block else got[i][:, low:high]

    @pl.when(g == 0)
    def _():
        acc[...] = jnp.zeros_like(acc)
        told_ref[...] = known_ref[0:1, 0:1]
        for i, dist in enumerate(dists):
            if dist is None:
                slots[i][...] = known_ref[...]
                continue
            meta = view(i, width, width + META).astype(jnp.float32).astype(jnp.int32)
            if dist == RELAY:
                dist = (2 + lax.broadcasted_iota(jnp.int32, (meta.shape[0], 1), 0) // SHARED) ^ 1
            slots[i][...] = jnp.where(meta[:, 1:2] == dist, meta[:, 0:1] - 1, -1)
            told_ref[...] = jnp.maximum(told_ref[...], meta[0:1, 2:3])

    off = 0
    turned = a_ref[...].T
    for i in range(m):
        n = slots[i].shape[0]
        s = jnp.dot(view(i, 0, width), turned, preferred_element_type=jnp.float32)
        s = jnp.where(group_of(s.shape) + g * per == slots[i][...], s, 0.0)
        v = s[:, :128]
        for c in range(128, s.shape[1], 128):
            v = v + s[:, c:c + 128]
        acc[off:off + n, :] += v
        off += n

    @pl.when(g == pl.num_programs(0) - 1)
    def _():
        off = 0
        for i in range(m):
            n = slots[i].shape[0]
            v = fold(acc[off:off + n, :])
            v = jnp.where(group_of(v.shape) == row_of(v.shape), v, 0.0)
            out_ref[off // 8:(off + n) // 8, :] = jnp.sum(v.reshape(n // 8, 8, 128), axis=1)
            off += n


def whole(shape):
    return pl.BlockSpec(shape, lambda g: (0,) * len(shape))


def scores(me, known, dists, got, store):
    block = got[0].ndim == 3
    sizes = [got[0].shape[1]] * len(dists) if block else [v.shape[0] for v in got]
    total, width = sum(sizes), store.shape[1]
    blk = 256
    out = pl.pallas_call(
        functools.partial(score_kernel, tuple(dists), block),
        grid=(store.shape[0] // blk,),
        in_specs=[pl.BlockSpec(memory_space=pltpu.SMEM), whole(known.shape)]
        + [whole(v.shape) for v in got] + [pl.BlockSpec((blk, width), lambda g: (g, 0))],
        out_specs=[whole((total // 8, 128)), whole((1, 1))] + [whole((n, 1)) for n in sizes],
        out_shape=[jax.ShapeDtypeStruct((total // 8, 128), jnp.float32), jax.ShapeDtypeStruct((1, 1), jnp.int32)]
        + [jax.ShapeDtypeStruct((n, 1), jnp.int32) for n in sizes],
        scratch_shapes=[pltpu.VMEM((total, 128), jnp.float32)],
        compiler_params=pltpu.CompilerParams(vmem_limit_bytes=VMEM),
        cost_estimate=FREE,
        name="scores",
    )(me, known, *got, store)
    return out[0], out[1], list(out[2:])


def spread_out(slots, packed, depth, spread):
    off = 0
    for i in range(len(slots)):
        n = slots[i].shape[0]
        v = packed[off // 8:(off + n) // 8, :]
        v = jnp.broadcast_to(v[:, None, :], (n // 8, 8, 128)).reshape(n, 128)
        group = group_of(v.shape)
        v = fold(jnp.where(group == row_of(v.shape), v, 0.0))
        for c in range(depth // 128):
            hit = group + c * 8 == slots[i][...]
            spread[i][:, c * 128:(c + 1) * 128] = jnp.where(hit, v, 0.0).astype(jnp.bfloat16)
        off += n


def delta_kernel(m, *refs):
    slots, packed, b_ref, outs, spread = refs[:m], refs[m], refs[m + 1], refs[m + 2:-m], refs[-m:]

    @pl.when(pl.program_id(0) == 0)
    def _():
        spread_out(slots, packed, b_ref.shape[0], spread)

    for i in range(m):
        outs[i][...] = jnp.dot(spread[i][...], b_ref[...], preferred_element_type=jnp.float32).astype(jnp.bfloat16)


def direct_kernel(n_dp, me_ref, *refs):
    m = n_dp - 1
    slots, packed, b_ref, outs, spread = refs[:m], refs[m], refs[m + 1], refs[m + 2:-m], refs[-m:]
    me = me_ref[0]

    @pl.when(pl.program_id(0) == 0)
    def _():
        spread_out(slots, packed, b_ref.shape[0], spread)

    block = outs[-1]
    block[me] = jnp.zeros(block.shape[1:], block.dtype)
    for i in range(m):
        v = jnp.dot(spread[i][...], b_ref[...], preferred_element_type=jnp.float32)
        if i < m - 1:
            outs[i][...] = v[:SHARED].astype(jnp.bfloat16)
            block[me ^ (i + 2)] = v[SHARED:].astype(jnp.bfloat16)
        else:
            block[me ^ 1] = v[:OWN].astype(jnp.bfloat16)
            outs[i][...] = v[OWN:].astype(jnp.bfloat16)


def deltas(slots, packed, store, me=None, n_dp=None):
    depth, width = store.shape
    cols = width // 4
    part = lambda n: pl.BlockSpec((n, cols), lambda g: (0, g))
    ins = [whole(v.shape) for v in slots] + [whole(packed.shape), part(depth)]
    if me is None:
        kernel, first, args = functools.partial(delta_kernel, len(slots)), [], []
        sizes, shapes = [v.shape[0] for v in slots], []
        outs = [part(n) for n in sizes]
    else:
        kernel, first, args = functools.partial(direct_kernel, n_dp), [pl.BlockSpec(memory_space=pltpu.SMEM)], [me]
        sizes, shapes = [SHARED] * (n_dp - 2) + [NEAR - OWN], [(n_dp, OWN, width)]
        outs = [part(n) for n in sizes] + [pl.BlockSpec((n_dp, OWN, cols), lambda g: (0, 0, g))]
    shapes = [(n, width) for n in sizes] + shapes
    return list(pl.pallas_call(
        kernel,
        grid=(width // cols,),
        in_specs=first + ins,
        out_specs=outs,
        out_shape=[pltpu.HBM(v, jnp.bfloat16) for v in shapes],
        scratch_shapes=[pltpu.VMEM((v.shape[0], depth), jnp.bfloat16) for v in slots],
        compiler_params=pltpu.CompilerParams(vmem_limit_bytes=VMEM),
        cost_estimate=FREE,
        name="deltas",
    )(*args, *slots, packed, store))


def place_kernel(first, m, blocks, me_ref, row_ref, codes_ref, *refs):
    back, refs = refs[:m], refs[m:]
    pieces = [b[...] for b in back]
    if blocks:
        pieces += [refs[0][me_ref[0] ^ (1 + i)] for i in range(blocks)]
        refs = refs[1:]
    total = refs[0][...].astype(jnp.float32)
    for v in refs[1:-1]:
        total += v[...].astype(jnp.float32)
    for i, b in enumerate(pieces):
        code = codes_ref[first + i:first + i + 1, :b.shape[0]]
        put = jnp.where(row_ref[...] == code, 1.0, 0.0).astype(jnp.bfloat16)
        total += jnp.dot(put, b, preferred_element_type=jnp.float32)
    refs[-1][...] = total.astype(refs[-1].dtype)


def place(me, row_code, codes, first, back, block, adds, kind):
    rows, width = adds[0].shape
    cols = width // 4
    part = lambda v: pl.BlockSpec((v.shape[0], cols), lambda g: (0, g))
    blocks = [pl.BlockSpec((v.shape[0], OWN, cols), lambda g: (0, 0, g)) for v in block]
    return pl.pallas_call(
        functools.partial(place_kernel, first, len(back), sum(v.shape[0] - 1 for v in block)),
        grid=(width // cols,),
        in_specs=[pl.BlockSpec(memory_space=pltpu.SMEM), whole(row_code.shape), whole(codes.shape)]
        + [part(v) for v in back] + blocks + [part(v) for v in adds],
        out_specs=pl.BlockSpec((rows, cols), lambda g: (0, g)),
        out_shape=jax.ShapeDtypeStruct((rows, width), kind),
        compiler_params=pltpu.CompilerParams(vmem_limit_bytes=VMEM),
        cost_estimate=FREE,
        name="place",
    )(me, row_code, codes, *back, *block, *adds)


def column(row):
    n = row.shape[1]
    eye = lax.broadcasted_iota(jnp.int32, (n, n), 0) == lax.broadcasted_iota(jnp.int32, (n, n), 1)
    return jnp.sum(jnp.where(eye, jnp.broadcast_to(row, (n, n)), 0), axis=1, keepdims=True)


def row(col):
    n = col.shape[0]
    eye = lax.broadcasted_iota(jnp.int32, (n, n), 0) == lax.broadcasted_iota(jnp.int32, (n, n), 1)
    return jnp.sum(jnp.where(eye, jnp.broadcast_to(col, (n, n)), 0), axis=0, keepdims=True)


def segments(pos, alive, device, shift):
    n = pos.shape[1]
    dist = (pos >> shift) ^ device
    i = lax.broadcasted_iota(jnp.int32, (n, n), 0)
    j = lax.broadcasted_iota(jnp.int32, (n, n), 1)
    before = (column(dist) == dist) & (i < j)
    start = jnp.sum(jnp.where(before, column(alive), 0), axis=0, keepdims=True)
    return dist, start


def total(dist, alive, j):
    return jnp.sum(jnp.where(dist == j, alive, 0), axis=1, keepdims=True)


def over_of(dist, alive, j):
    return jnp.maximum(total(dist, alive, j - j % 2) - OWN, 0)


def iota_of(n, axis):
    return lax.broadcasted_iota(jnp.int32, (n, 1) if axis == 0 else (1, n), axis)


def near_code(big, axis):
    return big + iota_of(NEAR, axis)


def own_code(big, j, axis):
    return j * big + iota_of(OWN, axis)


def shared_code(big, j, over, axis):
    f = iota_of(SHARED, axis) + (j % 2) * SHARED
    even = j - j % 2
    return OWN + jnp.where(f < over, even * big + f, (even + 1) * big + f - over)


def far_code(big, j, over, axis):
    f = iota_of(SHARED + OWN, axis)
    g = f + (j % 2) * SHARED
    even = j - j % 2
    code = OWN + jnp.where(g < over, even * big + g, (even + 1) * big + g - over)
    return jnp.where(f < SHARED, code, j * big + f - SHARED)


def pack_kernel(n_dp, seg_len, shift, me_ref, ids_ref, lives_ref, index_ref, x_ref,
                table_ref, row_ref, self_ref, meta_ref, rounds_ref, *outs):
    me = me_ref[0]
    count, (rows, width) = ids_ref.shape[1], x_ref.shape
    big = 2 * rows
    lives = lives_ref[...]
    hit = column(ids_ref[...]) == lax.broadcasted_iota(jnp.int32, (count, index_ref.shape[1]), 1)
    pos = row(jnp.sum(jnp.where(hit, index_ref[...], 0), axis=1, keepdims=True))
    table_ref[0:1, :] = pos
    table_ref[1:2, :] = lives
    dist, start = segments(pos, lives, me, shift)
    code = dist * big + start
    slot = pos & ((1 << shift) - 1)

    def spread(value, axis):
        shape = (count, rows) if axis == 1 else (rows, count)
        r = lax.broadcasted_iota(jnp.int32, shape, axis)
        seg = lax.broadcasted_iota(jnp.int32, shape, 1 - axis)
        v = column(value) if axis == 1 else value
        return jnp.sum(jnp.where(r // seg_len == seg, v, 0), axis=1 - axis, keepdims=True)

    def rows_code(axis):
        lane = iota_of(rows, axis) % seg_len
        return jnp.where(lane < spread(lives, axis), spread(code, axis) + lane, -1)

    by_row, by_lane = rows_code(0), rows_code(1)
    row_slot, row_dist = spread(slot, 0), spread(dist, 0)
    row_ref[...] = by_row
    self_ref[...] = jnp.where((by_row >= 0) & (row_dist == 0), row_slot, -1)
    lane = lax.broadcasted_iota(jnp.int32, (rows, META), 1)
    meta = jnp.where(lane == 0, row_slot + 1, jnp.where(lane == 1, row_dist, 0))
    meta = meta.astype(jnp.float32).astype(jnp.bfloat16)
    meta_ref[...] = meta

    left = total(dist, lives, 1) - NEAR
    for j in range(2, n_dp):
        held = OWN + 2 * SHARED if j % 2 == 0 else OWN + jnp.maximum(2 * SHARED - over_of(dist, lives, j), 0)
        left = jnp.maximum(left, total(dist, lives, j) - held)
    rounds = (jnp.maximum(left, 0) + ROUND - 1) // ROUND
    rounds_ref[...] = rounds
    told = jnp.where(lax.broadcasted_iota(jnp.int32, (1, META), 1) == 2, rounds.astype(jnp.float32), 0.0)

    far = range(2, n_dp)
    codes = [far_code(big, j, over_of(dist, lives, j), 0) for j in far] + [near_code(big, 0)]
    m = len(codes)
    for c, out in zip(codes, outs[:m]):
        pick = jnp.where(c == by_lane, 1.0, 0.0).astype(jnp.bfloat16)
        out[:, :width] = jnp.dot(pick, x_ref[...], preferred_element_type=jnp.float32).astype(jnp.bfloat16)
        out[:, width:] = (jnp.dot(pick, meta, preferred_element_type=jnp.float32) + told).astype(jnp.bfloat16)
    lanes = [shared_code(big, j, over_of(dist, lives, j), 1) for j in far]
    lanes += [big + OWN + iota_of(NEAR - OWN, 1)]
    lanes += [own_code(big, j, 1) for j in range(1, n_dp)]
    for i, c in enumerate(lanes):
        outs[m][i:i + 1, :c.shape[1]] = c


def vmem(count):
    return [pl.BlockSpec(memory_space=pltpu.VMEM) for _ in range(count)]


def packs(me, ids, lives, index, x, n_dp, seg_len, shift):
    count, (rows, width) = ids.shape[1], x.shape
    sizes = [SHARED + OWN] * (n_dp - 2) + [NEAR]
    shapes = [((2, count), jnp.int32), ((rows, 1), jnp.int32), ((rows, 1), jnp.int32)]
    shapes += [((rows, META), jnp.bfloat16), ((1, 1), jnp.int32)]
    shapes += [((n, width + META), jnp.bfloat16) for n in sizes] + [((2 * n_dp - 2, 256), jnp.int32)]
    return pl.pallas_call(
        functools.partial(pack_kernel, n_dp, seg_len, shift),
        in_specs=[pl.BlockSpec(memory_space=pltpu.SMEM)] + vmem(4),
        out_specs=vmem(len(shapes)),
        out_shape=[jax.ShapeDtypeStruct(*v) for v in shapes],
        compiler_params=pltpu.CompilerParams(vmem_limit_bytes=VMEM),
        cost_estimate=FREE,
        name="pack",
    )(me, ids, lives, index, x)


def share_kernel(at_ref, x_ref, w_ref, out_ref):
    out_ref[...] = jnp.dot(x_ref[...], w_ref[...], preferred_element_type=jnp.float32).astype(jnp.bfloat16)


def share(at, x, weight, cols):
    rows, depth = x.shape
    tile = min(512, cols)
    return pl.pallas_call(
        share_kernel,
        grid_spec=pltpu.PrefetchScalarGridSpec(
            num_scalar_prefetch=1,
            grid=(cols // tile,),
            in_specs=[
                pl.BlockSpec((rows, depth), lambda g, at: (0, 0)),
                pl.BlockSpec((depth, tile), lambda g, at: (0, at[0] * (cols // tile) + g)),
            ],
            out_specs=pl.BlockSpec((rows, tile), lambda g, at: (0, g)),
        ),
        out_shape=pltpu.HBM((rows, cols), jnp.bfloat16),
        compiler_params=pltpu.CompilerParams(vmem_limit_bytes=VMEM),
        cost_estimate=FREE,
        name="share",
    )(at, x, weight)


def per_device(
    attention_output,
    output_projection_weight,
    shrink_matrix_store,
    expand_matrix_store,
    segment_adapter,
    segment_live_rows,
    adapter_store_index,
):
    steps, rows_dev, width = attention_output.shape
    seg_count = segment_adapter.shape[1]
    seg_len = rows_dev // seg_count
    store, rank, _ = shrink_matrix_store.shape
    n_dp, n_tp = lax.axis_size("dp"), lax.axis_size("tp")
    me = lax.axis_index("dp").reshape(1)
    rows = steps * rows_dev
    count = steps * seg_count
    shift = store.bit_length() - 1
    big = 2 * rows
    far = range(2, n_dp)

    x = attention_output.reshape(rows, width)
    shrink_store = shrink_matrix_store.reshape(store * rank, width)
    expand_store = expand_matrix_store.reshape(store * rank, width)
    weight = output_projection_weight

    def swap(v, axis, k):
        n = lax.axis_size(axis)
        return lax.ppermute(v, axis, [(i, i ^ k) for i in range(n)])

    def butterfly(v, axis, op):
        k = lax.axis_size(axis) // 2
        while k:
            v = op(v, swap(v, axis, k))
            k //= 2
        return v

    def answer(dists, got, known):
        scored, told, slots = scores(me, known, dists, got, shrink_store)
        return slots, told, butterfly(scored, "tp", jnp.add)

    def total_of(parts):
        if len(parts) == 1:
            return parts[0]
        return functools.reduce(jnp.add, [v.astype(jnp.float32) for v in parts]).astype(jnp.bfloat16)

    def a2a(v):
        return lax.all_to_all(v, "dp", split_axis=0, concat_axis=0, tiled=True)

    def after(v, *others):
        return lax.optimization_barrier((v, others))[0]

    packed = list(packs(
        me,
        segment_adapter.reshape(1, count),
        segment_live_rows.reshape(1, count),
        adapter_store_index.reshape(1, -1),
        x, n_dp, seg_len, shift,
    ))
    table, row_code, self_slots, meta, rounds = packed[:5]
    m = len(far)
    out_far, out_near = packed[5:5 + m], packed[5 + m]
    codes = packed[6 + m]

    in_far = [swap(v, "dp", j) for v, j in zip(out_far, far)]
    in_near = swap(out_near, "dp", 1)

    found, _, self_part = answer([None], [after(x, table)], self_slots)
    (self_delta,) = deltas(found, self_part, expand_store)

    at = after(lax.axis_index("tp").reshape(1), table)
    cols = weight.shape[1] // n_tp
    shares = {k: share(at ^ k, x, weight, cols) for k in reversed(range(n_tp))}
    (in_far, in_near, shares), _ = lax.optimization_barrier(((in_far, in_near, shares), self_delta))

    found, rounds, part = answer(list(far) + [1], in_far + [in_near], rounds)
    in_far, shares, _ = lax.optimization_barrier((in_far, shares, rounds))
    in_relay = swap(jnp.concatenate([v[:SHARED] for v in in_far]), "dp", 1)
    direct = deltas(found, part, expand_store, me, n_dp)
    block = a2a(direct[-1])

    adds = {k: [shares[k]] for k in shares}
    for k in range(1, n_tp, 2):
        adds[k ^ 1].append(swap(adds.pop(k)[0], "tp", 1))
    for k in range(2, n_tp, 2):
        adds[k] = [total_of(adds[k])]

    in_relay, direct, adds = lax.optimization_barrier((in_relay, direct, adds))
    found, _, part = answer([RELAY], [in_relay], rounds)
    part, adds = lax.optimization_barrier((part, adds))
    (relayed,) = deltas(found, part, expand_store)
    relayed = swap(relayed, "dp", 1)
    some, adds[0] = adds[0], []
    bit = 2
    while bit < n_tp:
        for k in sorted((k for k in adds if k & bit), reverse=True):
            adds[k ^ bit].append(swap(total_of(adds.pop(k)), "tp", bit))
        bit *= 2
    some = place(me, row_code, codes, m + 1, [], [block], some + [self_delta], jnp.float32)
    relayed, some, near, direct = lax.optimization_barrier((relayed, some, direct[m], direct))
    back = [swap(direct[i] + relayed[i * SHARED:(i + 1) * SHARED], "dp", j) for i, j in enumerate(far)]
    back.append(swap(near, "dp", 1))
    rounds = butterfly(rounds, "rep", jnp.maximum)[0, 0]

    def late_round(i, out):
        tab, rows_in, rows_meta, places = lax.optimization_barrier((table, x, meta, row_code, i))[:4]
        pos, alive = tab[0], tab[1]
        dist = (pos >> shift) ^ me[0]
        held = [None, jnp.int32(NEAR)]
        for j in range(2, n_dp, 2):
            extra = jnp.maximum(jnp.sum(jnp.where(dist == j, alive, 0)) - OWN, 0)
            held += [jnp.int32(OWN + 2 * SHARED), OWN + jnp.maximum(2 * SHARED - extra, 0)]
        x_meta = jnp.concatenate([rows_in, rows_meta], axis=1)
        code = [j * big + held[j] + i * ROUND + jnp.arange(ROUND, dtype=jnp.int32) for j in range(1, n_dp)]
        got = []
        for j, c in zip(range(1, n_dp), code):
            pick = (c[:, None] == places.reshape(1, rows)).astype(jnp.bfloat16)
            v = jnp.dot(pick, x_meta, preferred_element_type=jnp.float32).astype(jnp.bfloat16)
            got.append(swap(v, "dp", j))
        found, _, part = answer(list(range(1, n_dp)), got, rounds.reshape(1, 1))
        total = out.astype(jnp.float32)
        for j, c, v in zip(range(1, n_dp), code, deltas(found, part, expand_store)):
            put = (places == c[None, :]).astype(jnp.bfloat16)
            total = total + jnp.dot(put, swap(v, "dp", j), preferred_element_type=jnp.float32)
        return total.astype(jnp.bfloat16)

    out = place(me, row_code, codes, 0, back, [], [some] + adds[0], jnp.bfloat16)
    out = lax.fori_loop(0, rounds, late_round, out)
    return out.reshape(steps, rows_dev, width)


def solution(mesh):
    return jax.shard_map(
        per_device,
        mesh=mesh,
        in_specs=(
            P(None, ("rep", "dp"), "tp"),
            P("tp", None),
            P("dp", None, "tp"),
            P("dp", None, "tp"),
            P(None, ("rep", "dp")),
            P(None, ("rep", "dp")),
            P("rep"),
        ),
        out_specs=P(None, ("rep", "dp"), "tp"),
        check_vma=False,
    )
```

```python
import functools

import jax
import jax.numpy as jnp
from jax import lax
from jax.experimental import pallas as pl
from jax.experimental.pallas import tpu as pltpu
from jax.sharding import PartitionSpec as P

NEAR = 208
OWN = 72
SHARED = 64
ROUND = 64
META = 128
RELAY = -1
VMEM = 48 * 2**20
FREE = pl.CostEstimate(flops=0, bytes_accessed=0, transcendentals=0)


def group_of(shape):
    return lax.broadcasted_iota(jnp.int32, shape, 1) // 16


def row_of(shape):
    return lax.broadcasted_iota(jnp.int32, shape, 0) % 8


def fold(v):
    for shift in (64, 32, 16):
        v = v + pltpu.roll(v, shift, axis=1)
    return v


def score_kernel(dists, block, *refs):
    me_ref, known_ref, refs = refs[0], refs[1], refs[2:]
    m = len(dists)
    got, a_ref, refs = refs[:1 if block else m], refs[1 if block else m], refs[(2 if block else m + 1):]
    out_ref, told_ref, slots, acc = refs[0], refs[1], refs[2:-1], refs[-1]
    g = pl.program_id(0)
    per, width = a_ref.shape[0] // 16, a_ref.shape[1]

    def view(i, low, high):
        return got[0][me_ref[0] ^ (i + 1), :, low:high] if block else got[i][:, low:high]

    @pl.when(g == 0)
    def _():
        acc[...] = jnp.zeros_like(acc)
        told_ref[...] = known_ref[0:1, 0:1]
        for i, dist in enumerate(dists):
            if dist is None:
                slots[i][...] = known_ref[...]
                continue
            meta = view(i, width, width + META).astype(jnp.float32).astype(jnp.int32)
            if dist == RELAY:
                dist = (2 + lax.broadcasted_iota(jnp.int32, (meta.shape[0], 1), 0) // SHARED) ^ 1
            slots[i][...] = jnp.where(meta[:, 1:2] == dist, meta[:, 0:1] - 1, -1)
            told_ref[...] = jnp.maximum(told_ref[...], meta[0:1, 2:3])

    off = 0
    turned = a_ref[...].T
    for i in range(m):
        n = slots[i].shape[0]
        s = jnp.dot(view(i, 0, width), turned, preferred_element_type=jnp.float32)
        s = jnp.where(group_of(s.shape) + g * per == slots[i][...], s, 0.0)
        v = s[:, :128]
        for c in range(128, s.shape[1], 128):
            v = v + s[:, c:c + 128]
        acc[off:off + n, :] += v
        off += n

    @pl.when(g == pl.num_programs(0) - 1)
    def _():
        off = 0
        for i in range(m):
            n = slots[i].shape[0]
            v = fold(acc[off:off + n, :])
            v = jnp.where(group_of(v.shape) == row_of(v.shape), v, 0.0)
            out_ref[off // 8:(off + n) // 8, :] = jnp.sum(v.reshape(n // 8, 8, 128), axis=1)
            off += n


def whole(shape):
    return pl.BlockSpec(shape, lambda g: (0,) * len(shape))


def scores(me, known, dists, got, store):
    block = got[0].ndim == 3
    sizes = [got[0].shape[1]] * len(dists) if block else [v.shape[0] for v in got]
    total, width = sum(sizes), store.shape[1]
    blk = 256
    out = pl.pallas_call(
        functools.partial(score_kernel, tuple(dists), block),
        grid=(store.shape[0] // blk,),
        in_specs=[pl.BlockSpec(memory_space=pltpu.SMEM), whole(known.shape)]
        + [whole(v.shape) for v in got] + [pl.BlockSpec((blk, width), lambda g: (g, 0))],
        out_specs=[whole((total // 8, 128)), whole((1, 1))] + [whole((n, 1)) for n in sizes],
        out_shape=[jax.ShapeDtypeStruct((total // 8, 128), jnp.float32), jax.ShapeDtypeStruct((1, 1), jnp.int32)]
        + [jax.ShapeDtypeStruct((n, 1), jnp.int32) for n in sizes],
        scratch_shapes=[pltpu.VMEM((total, 128), jnp.float32)],
        compiler_params=pltpu.CompilerParams(vmem_limit_bytes=VMEM),
        cost_estimate=FREE,
        name="scores",
    )(me, known, *got, store)
    return out[0], out[1], list(out[2:])


def spread_out(slots, packed, depth, spread):
    off = 0
    for i in range(len(slots)):
        n = slots[i].shape[0]
        v = packed[off // 8:(off + n) // 8, :]
        v = jnp.broadcast_to(v[:, None, :], (n // 8, 8, 128)).reshape(n, 128)
        group = group_of(v.shape)
        v = fold(jnp.where(group == row_of(v.shape), v, 0.0))
        for c in range(depth // 128):
            hit = group + c * 8 == slots[i][...]
            spread[i][:, c * 128:(c + 1) * 128] = jnp.where(hit, v, 0.0).astype(jnp.bfloat16)
        off += n


def delta_kernel(m, *refs):
    slots, packed, b_ref, outs, spread = refs[:m], refs[m], refs[m + 1], refs[m + 2:-m], refs[-m:]

    @pl.when(pl.program_id(0) == 0)
    def _():
        spread_out(slots, packed, b_ref.shape[0], spread)

    for i in range(m):
        outs[i][...] = jnp.dot(spread[i][...], b_ref[...], preferred_element_type=jnp.float32).astype(jnp.bfloat16)


def direct_kernel(n_dp, me_ref, *refs):
    m = n_dp - 1
    slots, packed, b_ref, outs, spread = refs[:m], refs[m], refs[m + 1], refs[m + 2:-m], refs[-m:]
    me = me_ref[0]

    @pl.when(pl.program_id(0) == 0)
    def _():
        spread_out(slots, packed, b_ref.shape[0], spread)

    block = outs[-1]
    block[me] = jnp.zeros(block.shape[1:], block.dtype)
    for i in range(m):
        v = jnp.dot(spread[i][...], b_ref[...], preferred_element_type=jnp.float32)
        if i < m - 1:
            outs[i][...] = v[:SHARED].astype(jnp.bfloat16)
            block[me ^ (i + 2)] = v[SHARED:].astype(jnp.bfloat16)
        else:
            block[me ^ 1] = v[:OWN].astype(jnp.bfloat16)
            outs[i][...] = v[OWN:].astype(jnp.bfloat16)


def deltas(slots, packed, store, me=None, n_dp=None):
    depth, width = store.shape
    cols = width // 4
    part = lambda n: pl.BlockSpec((n, cols), lambda g: (0, g))
    ins = [whole(v.shape) for v in slots] + [whole(packed.shape), part(depth)]
    if me is None:
        kernel, first, args = functools.partial(delta_kernel, len(slots)), [], []
        sizes, shapes = [v.shape[0] for v in slots], []
        outs = [part(n) for n in sizes]
    else:
        kernel, first, args = functools.partial(direct_kernel, n_dp), [pl.BlockSpec(memory_space=pltpu.SMEM)], [me]
        sizes, shapes = [SHARED] * (n_dp - 2) + [NEAR - OWN], [(n_dp, OWN, width)]
        outs = [part(n) for n in sizes] + [pl.BlockSpec((n_dp, OWN, cols), lambda g: (0, 0, g))]
    shapes = [(n, width) for n in sizes] + shapes
    return list(pl.pallas_call(
        kernel,
        grid=(width // cols,),
        in_specs=first + ins,
        out_specs=outs,
        out_shape=[pltpu.HBM(v, jnp.bfloat16) for v in shapes],
        scratch_shapes=[pltpu.VMEM((v.shape[0], depth), jnp.bfloat16) for v in slots],
        compiler_params=pltpu.CompilerParams(vmem_limit_bytes=VMEM),
        cost_estimate=FREE,
        name="deltas",
    )(*args, *slots, packed, store))


def place_kernel(first, m, blocks, me_ref, row_ref, codes_ref, *refs):
    back, refs = refs[:m], refs[m:]
    pieces = [b[...] for b in back]
    if blocks:
        pieces += [refs[0][me_ref[0] ^ (1 + i)] for i in range(blocks)]
        refs = refs[1:]
    total = refs[0][...].astype(jnp.float32)
    for v in refs[1:-1]:
        total += v[...].astype(jnp.float32)
    for i, b in enumerate(pieces):
        code = codes_ref[first + i:first + i + 1, :b.shape[0]]
        put = jnp.where(row_ref[...] == code, 1.0, 0.0).astype(jnp.bfloat16)
        total += jnp.dot(put, b, preferred_element_type=jnp.float32)
    refs[-1][...] = total.astype(refs[-1].dtype)


def place(me, row_code, codes, first, back, block, adds, kind):
    rows, width = adds[0].shape
    cols = width // 4
    part = lambda v: pl.BlockSpec((v.shape[0], cols), lambda g: (0, g))
    blocks = [pl.BlockSpec((v.shape[0], OWN, cols), lambda g: (0, 0, g)) for v in block]
    return pl.pallas_call(
        functools.partial(place_kernel, first, len(back), sum(v.shape[0] - 1 for v in block)),
        grid=(width // cols,),
        in_specs=[pl.BlockSpec(memory_space=pltpu.SMEM), whole(row_code.shape), whole(codes.shape)]
        + [part(v) for v in back] + blocks + [part(v) for v in adds],
        out_specs=pl.BlockSpec((rows, cols), lambda g: (0, g)),
        out_shape=jax.ShapeDtypeStruct((rows, width), kind),
        compiler_params=pltpu.CompilerParams(vmem_limit_bytes=VMEM),
        cost_estimate=FREE,
        name="place",
    )(me, row_code, codes, *back, *block, *adds)


def column(row):
    n = row.shape[1]
    eye = lax.broadcasted_iota(jnp.int32, (n, n), 0) == lax.broadcasted_iota(jnp.int32, (n, n), 1)
    return jnp.sum(jnp.where(eye, jnp.broadcast_to(row, (n, n)), 0), axis=1, keepdims=True)


def row(col):
    n = col.shape[0]
    eye = lax.broadcasted_iota(jnp.int32, (n, n), 0) == lax.broadcasted_iota(jnp.int32, (n, n), 1)
    return jnp.sum(jnp.where(eye, jnp.broadcast_to(col, (n, n)), 0), axis=0, keepdims=True)


def segments(pos, alive, device, shift):
    n = pos.shape[1]
    dist = (pos >> shift) ^ device
    i = lax.broadcasted_iota(jnp.int32, (n, n), 0)
    j = lax.broadcasted_iota(jnp.int32, (n, n), 1)
    before = (column(dist) == dist) & (i < j)
    start = jnp.sum(jnp.where(before, column(alive), 0), axis=0, keepdims=True)
    return dist, start


def total(dist, alive, j):
    return jnp.sum(jnp.where(dist == j, alive, 0), axis=1, keepdims=True)


def over_of(dist, alive, j):
    return jnp.maximum(total(dist, alive, j - j % 2) - OWN, 0)


def iota_of(n, axis):
    return lax.broadcasted_iota(jnp.int32, (n, 1) if axis == 0 else (1, n), axis)


def near_code(big, axis):
    return big + iota_of(NEAR, axis)


def own_code(big, j, axis):
    return j * big + iota_of(OWN, axis)


def shared_code(big, j, over, axis):
    f = iota_of(SHARED, axis) + (j % 2) * SHARED
    even = j - j % 2
    return OWN + jnp.where(f < over, even * big + f, (even + 1) * big + f - over)


def far_code(big, j, over, axis):
    f = iota_of(SHARED + OWN, axis)
    g = f + (j % 2) * SHARED
    even = j - j % 2
    code = OWN + jnp.where(g < over, even * big + g, (even + 1) * big + g - over)
    return jnp.where(f < SHARED, code, j * big + f - SHARED)


def pack_kernel(n_dp, seg_len, shift, me_ref, ids_ref, lives_ref, index_ref, x_ref,
                table_ref, row_ref, self_ref, meta_ref, rounds_ref, *outs):
    me = me_ref[0]
    count, (rows, width) = ids_ref.shape[1], x_ref.shape
    big = 2 * rows
    lives = lives_ref[...]
    hit = column(ids_ref[...]) == lax.broadcasted_iota(jnp.int32, (count, index_ref.shape[1]), 1)
    pos = row(jnp.sum(jnp.where(hit, index_ref[...], 0), axis=1, keepdims=True))
    table_ref[0:1, :] = pos
    table_ref[1:2, :] = lives
    dist, start = segments(pos, lives, me, shift)
    code = dist * big + start
    slot = pos & ((1 << shift) - 1)

    def spread(value, axis):
        shape = (count, rows) if axis == 1 else (rows, count)
        r = lax.broadcasted_iota(jnp.int32, shape, axis)
        seg = lax.broadcasted_iota(jnp.int32, shape, 1 - axis)
        v = column(value) if axis == 1 else value
        return jnp.sum(jnp.where(r // seg_len == seg, v, 0), axis=1 - axis, keepdims=True)

    def rows_code(axis):
        lane = iota_of(rows, axis) % seg_len
        return jnp.where(lane < spread(lives, axis), spread(code, axis) + lane, -1)

    by_row, by_lane = rows_code(0), rows_code(1)
    row_slot, row_dist = spread(slot, 0), spread(dist, 0)
    row_ref[...] = by_row
    self_ref[...] = jnp.where((by_row >= 0) & (row_dist == 0), row_slot, -1)
    lane = lax.broadcasted_iota(jnp.int32, (rows, META), 1)
    meta = jnp.where(lane == 0, row_slot + 1, jnp.where(lane == 1, row_dist, 0))
    meta = meta.astype(jnp.float32).astype(jnp.bfloat16)
    meta_ref[...] = meta

    left = total(dist, lives, 1) - NEAR
    for j in range(2, n_dp):
        held = OWN + 2 * SHARED if j % 2 == 0 else OWN + jnp.maximum(2 * SHARED - over_of(dist, lives, j), 0)
        left = jnp.maximum(left, total(dist, lives, j) - held)
    rounds = (jnp.maximum(left, 0) + ROUND - 1) // ROUND
    rounds_ref[...] = rounds
    told = jnp.where(lax.broadcasted_iota(jnp.int32, (1, META), 1) == 2, rounds.astype(jnp.float32), 0.0)

    far = range(2, n_dp)
    codes = [far_code(big, j, over_of(dist, lives, j), 0) for j in far] + [near_code(big, 0)]
    m = len(codes)
    for c, out in zip(codes, outs[:m]):
        pick = jnp.where(c == by_lane, 1.0, 0.0).astype(jnp.bfloat16)
        out[:, :width] = jnp.dot(pick, x_ref[...], preferred_element_type=jnp.float32).astype(jnp.bfloat16)
        out[:, width:] = (jnp.dot(pick, meta, preferred_element_type=jnp.float32) + told).astype(jnp.bfloat16)
    lanes = [shared_code(big, j, over_of(dist, lives, j), 1) for j in far]
    lanes += [big + OWN + iota_of(NEAR - OWN, 1)]
    lanes += [own_code(big, j, 1) for j in range(1, n_dp)]
    for i, c in enumerate(lanes):
        outs[m][i:i + 1, :c.shape[1]] = c


def vmem(count):
    return [pl.BlockSpec(memory_space=pltpu.VMEM) for _ in range(count)]


def packs(me, ids, lives, index, x, n_dp, seg_len, shift):
    count, (rows, width) = ids.shape[1], x.shape
    sizes = [SHARED + OWN] * (n_dp - 2) + [NEAR]
    shapes = [((2, count), jnp.int32), ((rows, 1), jnp.int32), ((rows, 1), jnp.int32)]
    shapes += [((rows, META), jnp.bfloat16), ((1, 1), jnp.int32)]
    shapes += [((n, width + META), jnp.bfloat16) for n in sizes] + [((2 * n_dp - 2, 256), jnp.int32)]
    return pl.pallas_call(
        functools.partial(pack_kernel, n_dp, seg_len, shift),
        in_specs=[pl.BlockSpec(memory_space=pltpu.SMEM)] + vmem(4),
        out_specs=vmem(len(shapes)),
        out_shape=[jax.ShapeDtypeStruct(*v) for v in shapes],
        compiler_params=pltpu.CompilerParams(vmem_limit_bytes=VMEM),
        cost_estimate=FREE,
        name="pack",
    )(me, ids, lives, index, x)


def share_kernel(at_ref, x_ref, w_ref, out_ref):
    out_ref[...] = jnp.dot(x_ref[...], w_ref[...], preferred_element_type=jnp.float32).astype(jnp.bfloat16)


def share(at, x, weight, cols):
    rows, depth = x.shape
    tile = min(512, cols)
    return pl.pallas_call(
        share_kernel,
        grid_spec=pltpu.PrefetchScalarGridSpec(
            num_scalar_prefetch=1,
            grid=(cols // tile,),
            in_specs=[
                pl.BlockSpec((rows, depth), lambda g, at: (0, 0)),
                pl.BlockSpec((depth, tile), lambda g, at: (0, at[0] * (cols // tile) + g)),
            ],
            out_specs=pl.BlockSpec((rows, tile), lambda g, at: (0, g)),
        ),
        out_shape=pltpu.HBM((rows, cols), jnp.bfloat16),
        compiler_params=pltpu.CompilerParams(vmem_limit_bytes=VMEM),
        cost_estimate=FREE,
        name="share",
    )(at, x, weight)


def per_device(
    attention_output,
    output_projection_weight,
    shrink_matrix_store,
    expand_matrix_store,
    segment_adapter,
    segment_live_rows,
    adapter_store_index,
):
    steps, rows_dev, width = attention_output.shape
    seg_count = segment_adapter.shape[1]
    seg_len = rows_dev // seg_count
    store, rank, _ = shrink_matrix_store.shape
    n_dp, n_tp = lax.axis_size("dp"), lax.axis_size("tp")
    me = lax.axis_index("dp").reshape(1)
    rows = steps * rows_dev
    count = steps * seg_count
    shift = store.bit_length() - 1
    big = 2 * rows
    far = range(2, n_dp)

    x = attention_output.reshape(rows, width)
    shrink_store = shrink_matrix_store.reshape(store * rank, width)
    expand_store = expand_matrix_store.reshape(store * rank, width)
    weight = output_projection_weight

    def swap(v, axis, k):
        n = lax.axis_size(axis)
        return lax.ppermute(v, axis, [(i, i ^ k) for i in range(n)])

    def butterfly(v, axis, op):
        k = lax.axis_size(axis) // 2
        while k:
            v = op(v, swap(v, axis, k))
            k //= 2
        return v

    def answer(dists, got, known):
        scored, told, slots = scores(me, known, dists, got, shrink_store)
        return slots, told, butterfly(scored, "tp", jnp.add)

    def total_of(parts):
        if len(parts) == 1:
            return parts[0]
        return functools.reduce(jnp.add, [v.astype(jnp.float32) for v in parts]).astype(jnp.bfloat16)

    def a2a(v):
        return lax.all_to_all(v, "dp", split_axis=0, concat_axis=0, tiled=True)

    def after(v, *others):
        return lax.optimization_barrier((v, others))[0]

    packed = list(packs(
        me,
        segment_adapter.reshape(1, count),
        segment_live_rows.reshape(1, count),
        adapter_store_index.reshape(1, -1),
        x, n_dp, seg_len, shift,
    ))
    table, row_code, self_slots, meta, rounds = packed[:5]
    m = len(far)
    out_far, out_near = packed[5:5 + m], packed[5 + m]
    codes = packed[6 + m]

    in_far = [swap(v, "dp", j) for v, j in zip(out_far, far)]
    in_near = swap(out_near, "dp", 1)

    found, _, self_part = answer([None], [after(x, table)], self_slots)
    (self_delta,) = deltas(found, self_part, expand_store)

    at = after(lax.axis_index("tp").reshape(1), table)
    cols = weight.shape[1] // n_tp
    shares = {k: share(at ^ k, x, weight, cols) for k in reversed(range(n_tp))}
    (in_far, in_near, shares), _ = lax.optimization_barrier(((in_far, in_near, shares), self_delta))

    in_relay = jnp.concatenate([v[:SHARED] for v in in_far])
    in_far, in_relay = lax.optimization_barrier((in_far, in_relay))
    in_relay = swap(in_relay, "dp", 1)
    found, rounds, part = answer(list(far) + [1], in_far + [in_near], rounds)
    shares, _ = lax.optimization_barrier((shares, rounds))
    direct = deltas(found, part, expand_store, me, n_dp)
    block = a2a(direct[-1])

    adds = {k: [shares[k]] for k in shares}
    for k in range(1, n_tp, 2):
        adds[k ^ 1].append(swap(adds.pop(k)[0], "tp", 1))
    in_relay, direct = lax.optimization_barrier((in_relay, direct))
    found, scored, part = answer([RELAY], [in_relay], rounds)
    adds, _ = lax.optimization_barrier((adds, scored))
    for k in range(2, n_tp, 2):
        adds[k] = [total_of(adds[k])]
    part, adds = lax.optimization_barrier((part, adds))
    (relayed,) = deltas(found, part, expand_store)
    relayed = swap(relayed, "dp", 1)
    some, adds[0] = adds[0], []
    bit = 2
    while bit < n_tp:
        for k in sorted((k for k in adds if k & bit), reverse=True):
            adds[k ^ bit].append(swap(total_of(adds.pop(k)), "tp", bit))
        bit *= 2
    near = after(direct[m], block)
    some = place(me, row_code, codes, m + 1, [], [block], some + [self_delta], jnp.float32)
    relayed, some, direct = lax.optimization_barrier((relayed, some, direct))
    back = [swap(direct[i] + relayed[i * SHARED:(i + 1) * SHARED], "dp", j) for i, j in enumerate(far)]
    back.append(swap(near, "dp", 1))
    rounds = butterfly(rounds, "rep", jnp.maximum)[0, 0]

    def late_round(i, out):
        tab, rows_in, rows_meta, places = lax.optimization_barrier((table, x, meta, row_code, i))[:4]
        pos, alive = tab[0], tab[1]
        dist = (pos >> shift) ^ me[0]
        held = [None, jnp.int32(NEAR)]
        for j in range(2, n_dp, 2):
            extra = jnp.maximum(jnp.sum(jnp.where(dist == j, alive, 0)) - OWN, 0)
            held += [jnp.int32(OWN + 2 * SHARED), OWN + jnp.maximum(2 * SHARED - extra, 0)]
        x_meta = jnp.concatenate([rows_in, rows_meta], axis=1)
        code = [j * big + held[j] + i * ROUND + jnp.arange(ROUND, dtype=jnp.int32) for j in range(1, n_dp)]
        got = []
        for j, c in zip(range(1, n_dp), code):
            pick = (c[:, None] == places.reshape(1, rows)).astype(jnp.bfloat16)
            v = jnp.dot(pick, x_meta, preferred_element_type=jnp.float32).astype(jnp.bfloat16)
            got.append(swap(v, "dp", j))
        found, _, part = answer(list(range(1, n_dp)), got, rounds.reshape(1, 1))
        total = out.astype(jnp.float32)
        for j, c, v in zip(range(1, n_dp), code, deltas(found, part, expand_store)):
            put = (places == c[None, :]).astype(jnp.bfloat16)
            total = total + jnp.dot(put, swap(v, "dp", j), preferred_element_type=jnp.float32)
        return total.astype(jnp.bfloat16)

    out = place(me, row_code, codes, 0, back, [], [some] + adds[0], jnp.bfloat16)
    out = lax.fori_loop(0, rounds, late_round, out)
    return out.reshape(steps, rows_dev, width)


def solution(mesh):
    return jax.shard_map(
        per_device,
        mesh=mesh,
        in_specs=(
            P(None, ("rep", "dp"), "tp"),
            P("tp", None),
            P("dp", None, "tp"),
            P("dp", None, "tp"),
            P(None, ("rep", "dp")),
            P(None, ("rep", "dp")),
            P("rep"),
        ),
        out_specs=P(None, ("rep", "dp"), "tp"),
        check_vma=False,
    )
```

```python
import functools

import jax
import jax.numpy as jnp
from jax import lax
from jax.experimental import pallas as pl
from jax.experimental.pallas import tpu as pltpu
from jax.sharding import PartitionSpec as P

NEAR = 208
OWN = 72
SHARED = 64
ROUND = 64
META = 128
RELAY = -1
VMEM = 48 * 2**20
FREE = pl.CostEstimate(flops=0, bytes_accessed=0, transcendentals=0)


def group_of(shape):
    return lax.broadcasted_iota(jnp.int32, shape, 1) // 16


def row_of(shape):
    return lax.broadcasted_iota(jnp.int32, shape, 0) % 8


def fold(v):
    for shift in (64, 32, 16):
        v = v + pltpu.roll(v, shift, axis=1)
    return v


def score_kernel(dists, block, *refs):
    me_ref, known_ref, refs = refs[0], refs[1], refs[2:]
    m = len(dists)
    got, a_ref, refs = refs[:1 if block else m], refs[1 if block else m], refs[(2 if block else m + 1):]
    out_ref, told_ref, slots, acc = refs[0], refs[1], refs[2:-1], refs[-1]
    g = pl.program_id(0)
    per, width = a_ref.shape[0] // 16, a_ref.shape[1]

    def view(i, low, high):
        return got[0][me_ref[0] ^ (i + 1), :, low:high] if block else got[i][:, low:high]

    @pl.when(g == 0)
    def _():
        acc[...] = jnp.zeros_like(acc)
        told_ref[...] = known_ref[0:1, 0:1]
        for i, dist in enumerate(dists):
            if dist is None:
                slots[i][...] = known_ref[...]
                continue
            meta = view(i, width, width + META).astype(jnp.float32).astype(jnp.int32)
            if dist == RELAY:
                dist = (2 + lax.broadcasted_iota(jnp.int32, (meta.shape[0], 1), 0) // SHARED) ^ 1
            slots[i][...] = jnp.where(meta[:, 1:2] == dist, meta[:, 0:1] - 1, -1)
            told_ref[...] = jnp.maximum(told_ref[...], meta[0:1, 2:3])

    off = 0
    turned = a_ref[...].T
    for i in range(m):
        n = slots[i].shape[0]
        s = jnp.dot(view(i, 0, width), turned, preferred_element_type=jnp.float32)
        s = jnp.where(group_of(s.shape) + g * per == slots[i][...], s, 0.0)
        v = s[:, :128]
        for c in range(128, s.shape[1], 128):
            v = v + s[:, c:c + 128]
        acc[off:off + n, :] += v
        off += n

    @pl.when(g == pl.num_programs(0) - 1)
    def _():
        off = 0
        for i in range(m):
            n = slots[i].shape[0]
            v = fold(acc[off:off + n, :])
            v = jnp.where(group_of(v.shape) == row_of(v.shape), v, 0.0)
            out_ref[off // 8:(off + n) // 8, :] = jnp.sum(v.reshape(n // 8, 8, 128), axis=1)
            off += n


def whole(shape):
    return pl.BlockSpec(shape, lambda g: (0,) * len(shape))


def scores(me, known, dists, got, store):
    block = got[0].ndim == 3
    sizes = [got[0].shape[1]] * len(dists) if block else [v.shape[0] for v in got]
    total, width = sum(sizes), store.shape[1]
    blk = 256
    out = pl.pallas_call(
        functools.partial(score_kernel, tuple(dists), block),
        grid=(store.shape[0] // blk,),
        in_specs=[pl.BlockSpec(memory_space=pltpu.SMEM), whole(known.shape)]
        + [whole(v.shape) for v in got] + [pl.BlockSpec((blk, width), lambda g: (g, 0))],
        out_specs=[whole((total // 8, 128)), whole((1, 1))] + [whole((n, 1)) for n in sizes],
        out_shape=[jax.ShapeDtypeStruct((total // 8, 128), jnp.float32), jax.ShapeDtypeStruct((1, 1), jnp.int32)]
        + [jax.ShapeDtypeStruct((n, 1), jnp.int32) for n in sizes],
        scratch_shapes=[pltpu.VMEM((total, 128), jnp.float32)],
        compiler_params=pltpu.CompilerParams(vmem_limit_bytes=VMEM),
        cost_estimate=FREE,
        name="scores",
    )(me, known, *got, store)
    return out[0], out[1], list(out[2:])


def spread_out(slots, packed, depth, spread):
    off = 0
    for i in range(len(slots)):
        n = slots[i].shape[0]
        v = packed[off // 8:(off + n) // 8, :]
        v = jnp.broadcast_to(v[:, None, :], (n // 8, 8, 128)).reshape(n, 128)
        group = group_of(v.shape)
        v = fold(jnp.where(group == row_of(v.shape), v, 0.0))
        for c in range(depth // 128):
            hit = group + c * 8 == slots[i][...]
            spread[i][:, c * 128:(c + 1) * 128] = jnp.where(hit, v, 0.0).astype(jnp.bfloat16)
        off += n


def delta_kernel(m, *refs):
    slots, packed, b_ref, outs, spread = refs[:m], refs[m], refs[m + 1], refs[m + 2:-m], refs[-m:]

    @pl.when(pl.program_id(0) == 0)
    def _():
        spread_out(slots, packed, b_ref.shape[0], spread)

    for i in range(m):
        outs[i][...] = jnp.dot(spread[i][...], b_ref[...], preferred_element_type=jnp.float32).astype(jnp.bfloat16)


def direct_kernel(n_dp, me_ref, *refs):
    m = n_dp - 1
    slots, packed, b_ref, outs, spread = refs[:m], refs[m], refs[m + 1], refs[m + 2:-m], refs[-m:]
    me = me_ref[0]

    @pl.when(pl.program_id(0) == 0)
    def _():
        spread_out(slots, packed, b_ref.shape[0], spread)

    block = outs[-1]
    block[me] = jnp.zeros(block.shape[1:], block.dtype)
    for i in range(m):
        v = jnp.dot(spread[i][...], b_ref[...], preferred_element_type=jnp.float32)
        if i < m - 1:
            outs[i][...] = v[:SHARED].astype(jnp.bfloat16)
            block[me ^ (i + 2)] = v[SHARED:].astype(jnp.bfloat16)
        else:
            block[me ^ 1] = v[:OWN].astype(jnp.bfloat16)
            outs[i][...] = v[OWN:].astype(jnp.bfloat16)


def deltas(slots, packed, store, me=None, n_dp=None):
    depth, width = store.shape
    cols = width // 4
    part = lambda n: pl.BlockSpec((n, cols), lambda g: (0, g))
    ins = [whole(v.shape) for v in slots] + [whole(packed.shape), part(depth)]
    if me is None:
        kernel, first, args = functools.partial(delta_kernel, len(slots)), [], []
        sizes, shapes = [v.shape[0] for v in slots], []
        outs = [part(n) for n in sizes]
    else:
        kernel, first, args = functools.partial(direct_kernel, n_dp), [pl.BlockSpec(memory_space=pltpu.SMEM)], [me]
        sizes, shapes = [SHARED] * (n_dp - 2) + [NEAR - OWN], [(n_dp, OWN, width)]
        outs = [part(n) for n in sizes] + [pl.BlockSpec((n_dp, OWN, cols), lambda g: (0, 0, g))]
    shapes = [(n, width) for n in sizes] + shapes
    return list(pl.pallas_call(
        kernel,
        grid=(width // cols,),
        in_specs=first + ins,
        out_specs=outs,
        out_shape=[pltpu.HBM(v, jnp.bfloat16) for v in shapes],
        scratch_shapes=[pltpu.VMEM((v.shape[0], depth), jnp.bfloat16) for v in slots],
        compiler_params=pltpu.CompilerParams(vmem_limit_bytes=VMEM),
        cost_estimate=FREE,
        name="deltas",
    )(*args, *slots, packed, store))


def place_kernel(first, m, blocks, me_ref, row_ref, codes_ref, *refs):
    back, refs = refs[:m], refs[m:]
    pieces = [b[...] for b in back]
    if blocks:
        pieces += [refs[0][me_ref[0] ^ (1 + i)] for i in range(blocks)]
        refs = refs[1:]
    total = refs[0][...].astype(jnp.float32)
    for v in refs[1:-1]:
        total += v[...].astype(jnp.float32)
    for i, b in enumerate(pieces):
        code = codes_ref[first + i:first + i + 1, :b.shape[0]]
        put = jnp.where(row_ref[...] == code, 1.0, 0.0).astype(jnp.bfloat16)
        total += jnp.dot(put, b, preferred_element_type=jnp.float32)
    refs[-1][...] = total.astype(refs[-1].dtype)


def place(me, row_code, codes, first, back, block, adds, kind):
    rows, width = adds[0].shape
    cols = width // 4
    part = lambda v: pl.BlockSpec((v.shape[0], cols), lambda g: (0, g))
    blocks = [pl.BlockSpec((v.shape[0], OWN, cols), lambda g: (0, 0, g)) for v in block]
    return pl.pallas_call(
        functools.partial(place_kernel, first, len(back), sum(v.shape[0] - 1 for v in block)),
        grid=(width // cols,),
        in_specs=[pl.BlockSpec(memory_space=pltpu.SMEM), whole(row_code.shape), whole(codes.shape)]
        + [part(v) for v in back] + blocks + [part(v) for v in adds],
        out_specs=pl.BlockSpec((rows, cols), lambda g: (0, g)),
        out_shape=jax.ShapeDtypeStruct((rows, width), kind),
        compiler_params=pltpu.CompilerParams(vmem_limit_bytes=VMEM),
        cost_estimate=FREE,
        name="place",
    )(me, row_code, codes, *back, *block, *adds)


def column(row):
    n = row.shape[1]
    eye = lax.broadcasted_iota(jnp.int32, (n, n), 0) == lax.broadcasted_iota(jnp.int32, (n, n), 1)
    return jnp.sum(jnp.where(eye, jnp.broadcast_to(row, (n, n)), 0), axis=1, keepdims=True)


def row(col):
    n = col.shape[0]
    eye = lax.broadcasted_iota(jnp.int32, (n, n), 0) == lax.broadcasted_iota(jnp.int32, (n, n), 1)
    return jnp.sum(jnp.where(eye, jnp.broadcast_to(col, (n, n)), 0), axis=0, keepdims=True)


def segments(pos, alive, device, shift):
    n = pos.shape[1]
    dist = (pos >> shift) ^ device
    i = lax.broadcasted_iota(jnp.int32, (n, n), 0)
    j = lax.broadcasted_iota(jnp.int32, (n, n), 1)
    before = (column(dist) == dist) & (i < j)
    start = jnp.sum(jnp.where(before, column(alive), 0), axis=0, keepdims=True)
    return dist, start


def total(dist, alive, j):
    return jnp.sum(jnp.where(dist == j, alive, 0), axis=1, keepdims=True)


def over_of(dist, alive, j):
    return jnp.maximum(total(dist, alive, j - j % 2) - OWN, 0)


def iota_of(n, axis):
    return lax.broadcasted_iota(jnp.int32, (n, 1) if axis == 0 else (1, n), axis)


def near_code(big, axis):
    return big + iota_of(NEAR, axis)


def own_code(big, j, axis):
    return j * big + iota_of(OWN, axis)


def shared_code(big, j, over, axis):
    f = iota_of(SHARED, axis) + (j % 2) * SHARED
    even = j - j % 2
    return OWN + jnp.where(f < over, even * big + f, (even + 1) * big + f - over)


def far_code(big, j, over, axis):
    f = iota_of(SHARED + OWN, axis)
    g = f + (j % 2) * SHARED
    even = j - j % 2
    code = OWN + jnp.where(g < over, even * big + g, (even + 1) * big + g - over)
    return jnp.where(f < SHARED, code, j * big + f - SHARED)


def pack_kernel(n_dp, seg_len, shift, me_ref, ids_ref, lives_ref, index_ref, x_ref,
                table_ref, row_ref, self_ref, meta_ref, rounds_ref, *outs):
    me = me_ref[0]
    count, (rows, width) = ids_ref.shape[1], x_ref.shape
    big = 2 * rows
    lives = lives_ref[...]
    hit = column(ids_ref[...]) == lax.broadcasted_iota(jnp.int32, (count, index_ref.shape[1]), 1)
    pos = row(jnp.sum(jnp.where(hit, index_ref[...], 0), axis=1, keepdims=True))
    table_ref[0:1, :] = pos
    table_ref[1:2, :] = lives
    dist, start = segments(pos, lives, me, shift)
    code = dist * big + start
    slot = pos & ((1 << shift) - 1)

    def spread(value, axis):
        shape = (count, rows) if axis == 1 else (rows, count)
        r = lax.broadcasted_iota(jnp.int32, shape, axis)
        seg = lax.broadcasted_iota(jnp.int32, shape, 1 - axis)
        v = column(value) if axis == 1 else value
        return jnp.sum(jnp.where(r // seg_len == seg, v, 0), axis=1 - axis, keepdims=True)

    def rows_code(axis):
        lane = iota_of(rows, axis) % seg_len
        return jnp.where(lane < spread(lives, axis), spread(code, axis) + lane, -1)

    by_row, by_lane = rows_code(0), rows_code(1)
    row_slot, row_dist = spread(slot, 0), spread(dist, 0)
    row_ref[...] = by_row
    self_ref[...] = jnp.where((by_row >= 0) & (row_dist == 0), row_slot, -1)
    lane = lax.broadcasted_iota(jnp.int32, (rows, META), 1)
    meta = jnp.where(lane == 0, row_slot + 1, jnp.where(lane == 1, row_dist, 0))
    meta = meta.astype(jnp.float32).astype(jnp.bfloat16)
    meta_ref[...] = meta

    left = total(dist, lives, 1) - NEAR
    for j in range(2, n_dp):
        held = OWN + 2 * SHARED if j % 2 == 0 else OWN + jnp.maximum(2 * SHARED - over_of(dist, lives, j), 0)
        left = jnp.maximum(left, total(dist, lives, j) - held)
    rounds = (jnp.maximum(left, 0) + ROUND - 1) // ROUND
    rounds_ref[...] = rounds
    told = jnp.where(lax.broadcasted_iota(jnp.int32, (1, META), 1) == 2, rounds.astype(jnp.float32), 0.0)

    far = range(2, n_dp)
    codes = [far_code(big, j, over_of(dist, lives, j), 0) for j in far] + [near_code(big, 0)]
    m = len(codes)
    for c, out in zip(codes, outs[:m]):
        pick = jnp.where(c == by_lane, 1.0, 0.0).astype(jnp.bfloat16)
        out[:, :width] = jnp.dot(pick, x_ref[...], preferred_element_type=jnp.float32).astype(jnp.bfloat16)
        out[:, width:] = (jnp.dot(pick, meta, preferred_element_type=jnp.float32) + told).astype(jnp.bfloat16)
    lanes = [shared_code(big, j, over_of(dist, lives, j), 1) for j in far]
    lanes += [big + OWN + iota_of(NEAR - OWN, 1)]
    lanes += [own_code(big, j, 1) for j in range(1, n_dp)]
    for i, c in enumerate(lanes):
        outs[m][i:i + 1, :c.shape[1]] = c


def vmem(count):
    return [pl.BlockSpec(memory_space=pltpu.VMEM) for _ in range(count)]


def packs(me, ids, lives, index, x, n_dp, seg_len, shift):
    count, (rows, width) = ids.shape[1], x.shape
    sizes = [SHARED + OWN] * (n_dp - 2) + [NEAR]
    shapes = [((2, count), jnp.int32), ((rows, 1), jnp.int32), ((rows, 1), jnp.int32)]
    shapes += [((rows, META), jnp.bfloat16), ((1, 1), jnp.int32)]
    shapes += [((n, width + META), jnp.bfloat16) for n in sizes] + [((2 * n_dp - 2, 256), jnp.int32)]
    return pl.pallas_call(
        functools.partial(pack_kernel, n_dp, seg_len, shift),
        in_specs=[pl.BlockSpec(memory_space=pltpu.SMEM)] + vmem(4),
        out_specs=vmem(len(shapes)),
        out_shape=[jax.ShapeDtypeStruct(*v) for v in shapes],
        compiler_params=pltpu.CompilerParams(vmem_limit_bytes=VMEM),
        cost_estimate=FREE,
        name="pack",
    )(me, ids, lives, index, x)


def share_kernel(at_ref, x_ref, w_ref, out_ref):
    out_ref[...] = jnp.dot(x_ref[...], w_ref[...], preferred_element_type=jnp.float32).astype(jnp.bfloat16)


def share(at, x, weight, cols):
    rows, depth = x.shape
    tile = min(512, cols)
    return pl.pallas_call(
        share_kernel,
        grid_spec=pltpu.PrefetchScalarGridSpec(
            num_scalar_prefetch=1,
            grid=(cols // tile,),
            in_specs=[
                pl.BlockSpec((rows, depth), lambda g, at: (0, 0)),
                pl.BlockSpec((depth, tile), lambda g, at: (0, at[0] * (cols // tile) + g)),
            ],
            out_specs=pl.BlockSpec((rows, tile), lambda g, at: (0, g)),
        ),
        out_shape=pltpu.HBM((rows, cols), jnp.bfloat16),
        compiler_params=pltpu.CompilerParams(vmem_limit_bytes=VMEM),
        cost_estimate=FREE,
        name="share",
    )(at, x, weight)


def per_device(
    attention_output,
    output_projection_weight,
    shrink_matrix_store,
    expand_matrix_store,
    segment_adapter,
    segment_live_rows,
    adapter_store_index,
):
    steps, rows_dev, width = attention_output.shape
    seg_count = segment_adapter.shape[1]
    seg_len = rows_dev // seg_count
    store, rank, _ = shrink_matrix_store.shape
    n_dp, n_tp = lax.axis_size("dp"), lax.axis_size("tp")
    me = lax.axis_index("dp").reshape(1)
    rows = steps * rows_dev
    count = steps * seg_count
    shift = store.bit_length() - 1
    big = 2 * rows
    far = range(2, n_dp)

    x = attention_output.reshape(rows, width)
    shrink_store = shrink_matrix_store.reshape(store * rank, width)
    expand_store = expand_matrix_store.reshape(store * rank, width)
    weight = output_projection_weight

    def swap(v, axis, k):
        n = lax.axis_size(axis)
        return lax.ppermute(v, axis, [(i, i ^ k) for i in range(n)])

    def butterfly(v, axis, op):
        k = lax.axis_size(axis) // 2
        while k:
            v = op(v, swap(v, axis, k))
            k //= 2
        return v

    def answer(dists, got, known):
        scored, told, slots = scores(me, known, dists, got, shrink_store)
        return slots, told, butterfly(scored, "tp", jnp.add)

    def total_of(parts):
        if len(parts) == 1:
            return parts[0]
        return functools.reduce(jnp.add, [v.astype(jnp.float32) for v in parts]).astype(jnp.bfloat16)

    def a2a(v):
        return lax.all_to_all(v, "dp", split_axis=0, concat_axis=0, tiled=True)

    def after(v, *others):
        return lax.optimization_barrier((v, others))[0]

    packed = list(packs(
        me,
        segment_adapter.reshape(1, count),
        segment_live_rows.reshape(1, count),
        adapter_store_index.reshape(1, -1),
        x, n_dp, seg_len, shift,
    ))
    table, row_code, self_slots, meta, rounds = packed[:5]
    m = len(far)
    out_far, out_near = packed[5:5 + m], packed[5 + m]
    codes = packed[6 + m]

    in_far = [swap(v, "dp", j) for v, j in zip(out_far, far)]
    in_near = swap(out_near, "dp", 1)

    self_found, _, self_part = answer([None], [after(x, table)], self_slots)

    at = after(lax.axis_index("tp").reshape(1), table)
    cols = weight.shape[1] // n_tp
    shares = {k: share(at ^ k, x, weight, cols) for k in reversed(range(n_tp))}
    (in_far, in_near, shares), _ = lax.optimization_barrier(((in_far, in_near, shares), self_part))

    found, rounds, part = answer(list(far) + [1], in_far + [in_near], rounds)
    in_far, shares, _ = lax.optimization_barrier((in_far, shares, rounds))
    in_relay = swap(jnp.concatenate([v[:SHARED] for v in in_far]), "dp", 1)
    direct = deltas(found, part, expand_store, me, n_dp)
    block = a2a(direct[-1])

    adds = {k: [shares[k]] for k in shares}
    for k in range(1, n_tp, 2):
        adds[k ^ 1].append(swap(adds.pop(k)[0], "tp", 1))
    for k in range(2, n_tp, 2):
        adds[k] = [total_of(adds[k])]

    in_relay, direct, adds = lax.optimization_barrier((in_relay, direct, adds))
    found, _, part = answer([RELAY], [in_relay], rounds)
    part, adds = lax.optimization_barrier((part, adds))
    (relayed,) = deltas(found, part, expand_store)
    (self_delta,) = deltas(self_found, after(self_part, relayed), expand_store)
    relayed = swap(relayed, "dp", 1)
    some, adds[0] = adds[0], []
    bit = 2
    while bit < n_tp:
        for k in sorted((k for k in adds if k & bit), reverse=True):
            adds[k ^ bit].append(swap(total_of(adds.pop(k)), "tp", bit))
        bit *= 2
    some = place(me, row_code, codes, m + 1, [], [block], some + [self_delta], jnp.float32)
    relayed, some, near, direct = lax.optimization_barrier((relayed, some, direct[m], direct))
    back = [swap(direct[i] + relayed[i * SHARED:(i + 1) * SHARED], "dp", j) for i, j in enumerate(far)]
    back.append(swap(near, "dp", 1))
    rounds = butterfly(rounds, "rep", jnp.maximum)[0, 0]

    def late_round(i, out):
        tab, rows_in, rows_meta, places = lax.optimization_barrier((table, x, meta, row_code, i))[:4]
        pos, alive = tab[0], tab[1]
        dist = (pos >> shift) ^ me[0]
        held = [None, jnp.int32(NEAR)]
        for j in range(2, n_dp, 2):
            extra = jnp.maximum(jnp.sum(jnp.where(dist == j, alive, 0)) - OWN, 0)
            held += [jnp.int32(OWN + 2 * SHARED), OWN + jnp.maximum(2 * SHARED - extra, 0)]
        x_meta = jnp.concatenate([rows_in, rows_meta], axis=1)
        code = [j * big + held[j] + i * ROUND + jnp.arange(ROUND, dtype=jnp.int32) for j in range(1, n_dp)]
        got = []
        for j, c in zip(range(1, n_dp), code):
            pick = (c[:, None] == places.reshape(1, rows)).astype(jnp.bfloat16)
            v = jnp.dot(pick, x_meta, preferred_element_type=jnp.float32).astype(jnp.bfloat16)
            got.append(swap(v, "dp", j))
        found, _, part = answer(list(range(1, n_dp)), got, rounds.reshape(1, 1))
        total = out.astype(jnp.float32)
        for j, c, v in zip(range(1, n_dp), code, deltas(found, part, expand_store)):
            put = (places == c[None, :]).astype(jnp.bfloat16)
            total = total + jnp.dot(put, swap(v, "dp", j), preferred_element_type=jnp.float32)
        return total.astype(jnp.bfloat16)

    out = place(me, row_code, codes, 0, back, [], [some] + adds[0], jnp.bfloat16)
    out = lax.fori_loop(0, rounds, late_round, out)
    return out.reshape(steps, rows_dev, width)


def solution(mesh):
    return jax.shard_map(
        per_device,
        mesh=mesh,
        in_specs=(
            P(None, ("rep", "dp"), "tp"),
            P("tp", None),
            P("dp", None, "tp"),
            P("dp", None, "tp"),
            P(None, ("rep", "dp")),
            P(None, ("rep", "dp")),
            P("rep"),
        ),
        out_specs=P(None, ("rep", "dp"), "tp"),
        check_vma=False,
    )
```

```python
import functools

import jax
import jax.numpy as jnp
from jax import lax
from jax.experimental import pallas as pl
from jax.experimental.pallas import tpu as pltpu
from jax.sharding import PartitionSpec as P

NEAR = 208
OWN = 72
SHARED = 64
ROUND = 64
META = 128
RELAY = -1
VMEM = 48 * 2**20
FREE = pl.CostEstimate(flops=0, bytes_accessed=0, transcendentals=0)


def group_of(shape):
    return lax.broadcasted_iota(jnp.int32, shape, 1) // 16


def row_of(shape):
    return lax.broadcasted_iota(jnp.int32, shape, 0) % 8


def fold(v):
    for shift in (64, 32, 16):
        v = v + pltpu.roll(v, shift, axis=1)
    return v


def score_kernel(dists, block, *refs):
    me_ref, known_ref, refs = refs[0], refs[1], refs[2:]
    m = len(dists)
    got, a_ref, refs = refs[:1 if block else m], refs[1 if block else m], refs[(2 if block else m + 1):]
    out_ref, told_ref, slots, acc = refs[0], refs[1], refs[2:-1], refs[-1]
    g = pl.program_id(0)
    per, width = a_ref.shape[0] // 16, a_ref.shape[1]

    def view(i, low, high):
        return got[0][me_ref[0] ^ (i + 1), :, low:high] if block else got[i][:, low:high]

    @pl.when(g == 0)
    def _():
        acc[...] = jnp.zeros_like(acc)
        told_ref[...] = known_ref[0:1, 0:1]
        for i, dist in enumerate(dists):
            if dist is None:
                slots[i][...] = known_ref[...]
                continue
            meta = view(i, width, width + META).astype(jnp.float32).astype(jnp.int32)
            if dist == RELAY:
                dist = (2 + lax.broadcasted_iota(jnp.int32, (meta.shape[0], 1), 0) // SHARED) ^ 1
            slots[i][...] = jnp.where(meta[:, 1:2] == dist, meta[:, 0:1] - 1, -1)
            told_ref[...] = jnp.maximum(told_ref[...], meta[0:1, 2:3])

    off = 0
    turned = a_ref[...].T
    for i in range(m):
        n = slots[i].shape[0]
        s = jnp.dot(view(i, 0, width), turned, preferred_element_type=jnp.float32)
        s = jnp.where(group_of(s.shape) + g * per == slots[i][...], s, 0.0)
        v = s[:, :128]
        for c in range(128, s.shape[1], 128):
            v = v + s[:, c:c + 128]
        acc[off:off + n, :] += v
        off += n

    @pl.when(g == pl.num_programs(0) - 1)
    def _():
        off = 0
        for i in range(m):
            n = slots[i].shape[0]
            v = fold(acc[off:off + n, :])
            v = jnp.where(group_of(v.shape) == row_of(v.shape), v, 0.0)
            out_ref[off // 8:(off + n) // 8, :] = jnp.sum(v.reshape(n // 8, 8, 128), axis=1)
            off += n


def whole(shape):
    return pl.BlockSpec(shape, lambda g: (0,) * len(shape))


def scores(me, known, dists, got, store):
    block = got[0].ndim == 3
    sizes = [got[0].shape[1]] * len(dists) if block else [v.shape[0] for v in got]
    total, width = sum(sizes), store.shape[1]
    blk = 256
    out = pl.pallas_call(
        functools.partial(score_kernel, tuple(dists), block),
        grid=(store.shape[0] // blk,),
        in_specs=[pl.BlockSpec(memory_space=pltpu.SMEM), whole(known.shape)]
        + [whole(v.shape) for v in got] + [pl.BlockSpec((blk, width), lambda g: (g, 0))],
        out_specs=[whole((total // 8, 128)), whole((1, 1))] + [whole((n, 1)) for n in sizes],
        out_shape=[jax.ShapeDtypeStruct((total // 8, 128), jnp.float32), jax.ShapeDtypeStruct((1, 1), jnp.int32)]
        + [jax.ShapeDtypeStruct((n, 1), jnp.int32) for n in sizes],
        scratch_shapes=[pltpu.VMEM((total, 128), jnp.float32)],
        compiler_params=pltpu.CompilerParams(vmem_limit_bytes=VMEM),
        cost_estimate=FREE,
        name="scores",
    )(me, known, *got, store)
    return out[0], out[1], list(out[2:])


def spread_out(slots, packed, depth, spread):
    off = 0
    for i in range(len(slots)):
        n = slots[i].shape[0]
        v = packed[off // 8:(off + n) // 8, :]
        v = jnp.broadcast_to(v[:, None, :], (n // 8, 8, 128)).reshape(n, 128)
        group = group_of(v.shape)
        v = fold(jnp.where(group == row_of(v.shape), v, 0.0))
        for c in range(depth // 128):
            hit = group + c * 8 == slots[i][...]
            spread[i][:, c * 128:(c + 1) * 128] = jnp.where(hit, v, 0.0).astype(jnp.bfloat16)
        off += n


def delta_kernel(m, *refs):
    slots, packed, b_ref, outs, spread = refs[:m], refs[m], refs[m + 1], refs[m + 2:-m], refs[-m:]

    @pl.when(pl.program_id(0) == 0)
    def _():
        spread_out(slots, packed, b_ref.shape[0], spread)

    for i in range(m):
        outs[i][...] = jnp.dot(spread[i][...], b_ref[...], preferred_element_type=jnp.float32).astype(jnp.bfloat16)


def direct_kernel(n_dp, me_ref, *refs):
    m = n_dp - 1
    slots, packed, b_ref, outs, spread = refs[:m], refs[m], refs[m + 1], refs[m + 2:-m], refs[-m:]
    me = me_ref[0]

    @pl.when(pl.program_id(0) == 0)
    def _():
        spread_out(slots, packed, b_ref.shape[0], spread)

    block = outs[-1]
    block[me] = jnp.zeros(block.shape[1:], block.dtype)
    for i in range(m):
        v = jnp.dot(spread[i][...], b_ref[...], preferred_element_type=jnp.float32)
        if i < m - 1:
            outs[i][...] = v[:SHARED].astype(jnp.bfloat16)
            block[me ^ (i + 2)] = v[SHARED:].astype(jnp.bfloat16)
        else:
            block[me ^ 1] = v[:OWN].astype(jnp.bfloat16)
            outs[i][...] = v[OWN:].astype(jnp.bfloat16)


def deltas(slots, packed, store, me=None, n_dp=None):
    depth, width = store.shape
    cols = width // 4
    part = lambda n: pl.BlockSpec((n, cols), lambda g: (0, g))
    ins = [whole(v.shape) for v in slots] + [whole(packed.shape), part(depth)]
    if me is None:
        kernel, first, args = functools.partial(delta_kernel, len(slots)), [], []
        sizes, shapes = [v.shape[0] for v in slots], []
        outs = [part(n) for n in sizes]
    else:
        kernel, first, args = functools.partial(direct_kernel, n_dp), [pl.BlockSpec(memory_space=pltpu.SMEM)], [me]
        sizes, shapes = [SHARED] * (n_dp - 2) + [NEAR - OWN], [(n_dp, OWN, width)]
        outs = [part(n) for n in sizes] + [pl.BlockSpec((n_dp, OWN, cols), lambda g: (0, 0, g))]
    shapes = [(n, width) for n in sizes] + shapes
    return list(pl.pallas_call(
        kernel,
        grid=(width // cols,),
        in_specs=first + ins,
        out_specs=outs,
        out_shape=[pltpu.HBM(v, jnp.bfloat16) for v in shapes],
        scratch_shapes=[pltpu.VMEM((v.shape[0], depth), jnp.bfloat16) for v in slots],
        compiler_params=pltpu.CompilerParams(vmem_limit_bytes=VMEM),
        cost_estimate=FREE,
        name="deltas",
    )(*args, *slots, packed, store))


def place_kernel(first, m, blocks, me_ref, row_ref, codes_ref, *refs):
    back, refs = refs[:m], refs[m:]
    pieces = [b[...] for b in back]
    if blocks:
        pieces += [refs[0][me_ref[0] ^ (1 + i)] for i in range(blocks)]
        refs = refs[1:]
    total = refs[0][...].astype(jnp.float32)
    for v in refs[1:-1]:
        total += v[...].astype(jnp.float32)
    for i, b in enumerate(pieces):
        code = codes_ref[first + i:first + i + 1, :b.shape[0]]
        put = jnp.where(row_ref[...] == code, 1.0, 0.0).astype(jnp.bfloat16)
        total += jnp.dot(put, b, preferred_element_type=jnp.float32)
    refs[-1][...] = total.astype(refs[-1].dtype)


def place(me, row_code, codes, first, back, block, adds, kind):
    rows, width = adds[0].shape
    cols = width // 4
    part = lambda v: pl.BlockSpec((v.shape[0], cols), lambda g: (0, g))
    blocks = [pl.BlockSpec((v.shape[0], OWN, cols), lambda g: (0, 0, g)) for v in block]
    return pl.pallas_call(
        functools.partial(place_kernel, first, len(back), sum(v.shape[0] - 1 for v in block)),
        grid=(width // cols,),
        in_specs=[pl.BlockSpec(memory_space=pltpu.SMEM), whole(row_code.shape), whole(codes.shape)]
        + [part(v) for v in back] + blocks + [part(v) for v in adds],
        out_specs=pl.BlockSpec((rows, cols), lambda g: (0, g)),
        out_shape=jax.ShapeDtypeStruct((rows, width), kind),
        compiler_params=pltpu.CompilerParams(vmem_limit_bytes=VMEM),
        cost_estimate=FREE,
        name="place",
    )(me, row_code, codes, *back, *block, *adds)


def column(row):
    n = row.shape[1]
    eye = lax.broadcasted_iota(jnp.int32, (n, n), 0) == lax.broadcasted_iota(jnp.int32, (n, n), 1)
    return jnp.sum(jnp.where(eye, jnp.broadcast_to(row, (n, n)), 0), axis=1, keepdims=True)


def row(col):
    n = col.shape[0]
    eye = lax.broadcasted_iota(jnp.int32, (n, n), 0) == lax.broadcasted_iota(jnp.int32, (n, n), 1)
    return jnp.sum(jnp.where(eye, jnp.broadcast_to(col, (n, n)), 0), axis=0, keepdims=True)


def segments(pos, alive, device, shift):
    n = pos.shape[1]
    dist = (pos >> shift) ^ device
    i = lax.broadcasted_iota(jnp.int32, (n, n), 0)
    j = lax.broadcasted_iota(jnp.int32, (n, n), 1)
    before = (column(dist) == dist) & (i < j)
    start = jnp.sum(jnp.where(before, column(alive), 0), axis=0, keepdims=True)
    return dist, start


def total(dist, alive, j):
    return jnp.sum(jnp.where(dist == j, alive, 0), axis=1, keepdims=True)


def over_of(dist, alive, j):
    return jnp.maximum(total(dist, alive, j - j % 2) - OWN, 0)


def iota_of(n, axis):
    return lax.broadcasted_iota(jnp.int32, (n, 1) if axis == 0 else (1, n), axis)


def near_code(big, axis):
    return big + iota_of(NEAR, axis)


def own_code(big, j, axis):
    return j * big + iota_of(OWN, axis)


def shared_code(big, j, over, axis):
    f = iota_of(SHARED, axis) + (j % 2) * SHARED
    even = j - j % 2
    return OWN + jnp.where(f < over, even * big + f, (even + 1) * big + f - over)


def far_code(big, j, over, axis):
    f = iota_of(SHARED + OWN, axis)
    g = f + (j % 2) * SHARED
    even = j - j % 2
    code = OWN + jnp.where(g < over, even * big + g, (even + 1) * big + g - over)
    return jnp.where(f < SHARED, code, j * big + f - SHARED)


def pack_kernel(n_dp, seg_len, shift, me_ref, ids_ref, lives_ref, index_ref, x_ref,
                table_ref, row_ref, self_ref, meta_ref, rounds_ref, *outs):
    me = me_ref[0]
    count, (rows, width) = ids_ref.shape[1], x_ref.shape
    big = 2 * rows
    lives = lives_ref[...]
    hit = column(ids_ref[...]) == lax.broadcasted_iota(jnp.int32, (count, index_ref.shape[1]), 1)
    pos = row(jnp.sum(jnp.where(hit, index_ref[...], 0), axis=1, keepdims=True))
    table_ref[0:1, :] = pos
    table_ref[1:2, :] = lives
    dist, start = segments(pos, lives, me, shift)
    code = dist * big + start
    slot = pos & ((1 << shift) - 1)

    def spread(value, axis):
        shape = (count, rows) if axis == 1 else (rows, count)
        r = lax.broadcasted_iota(jnp.int32, shape, axis)
        seg = lax.broadcasted_iota(jnp.int32, shape, 1 - axis)
        v = column(value) if axis == 1 else value
        return jnp.sum(jnp.where(r // seg_len == seg, v, 0), axis=1 - axis, keepdims=True)

    def rows_code(axis):
        lane = iota_of(rows, axis) % seg_len
        return jnp.where(lane < spread(lives, axis), spread(code, axis) + lane, -1)

    by_row, by_lane = rows_code(0), rows_code(1)
    row_slot, row_dist = spread(slot, 0), spread(dist, 0)
    row_ref[...] = by_row
    self_ref[...] = jnp.where((by_row >= 0) & (row_dist == 0), row_slot, -1)
    lane = lax.broadcasted_iota(jnp.int32, (rows, META), 1)
    meta = jnp.where(lane == 0, row_slot + 1, jnp.where(lane == 1, row_dist, 0))
    meta = meta.astype(jnp.float32).astype(jnp.bfloat16)
    meta_ref[...] = meta

    left = total(dist, lives, 1) - NEAR
    for j in range(2, n_dp):
        held = OWN + 2 * SHARED if j % 2 == 0 else OWN + jnp.maximum(2 * SHARED - over_of(dist, lives, j), 0)
        left = jnp.maximum(left, total(dist, lives, j) - held)
    rounds = (jnp.maximum(left, 0) + ROUND - 1) // ROUND
    rounds_ref[...] = rounds
    told = jnp.where(lax.broadcasted_iota(jnp.int32, (1, META), 1) == 2, rounds.astype(jnp.float32), 0.0)

    far = range(2, n_dp)
    codes = [far_code(big, j, over_of(dist, lives, j), 0) for j in far] + [near_code(big, 0)]
    m = len(codes)
    for c, out in zip(codes, outs[:m]):
        pick = jnp.where(c == by_lane, 1.0, 0.0).astype(jnp.bfloat16)
        out[:, :width] = jnp.dot(pick, x_ref[...], preferred_element_type=jnp.float32).astype(jnp.bfloat16)
        out[:, width:] = (jnp.dot(pick, meta, preferred_element_type=jnp.float32) + told).astype(jnp.bfloat16)
    lanes = [shared_code(big, j, over_of(dist, lives, j), 1) for j in far]
    lanes += [big + OWN + iota_of(NEAR - OWN, 1)]
    lanes += [own_code(big, j, 1) for j in range(1, n_dp)]
    for i, c in enumerate(lanes):
        outs[m][i:i + 1, :c.shape[1]] = c


def vmem(count):
    return [pl.BlockSpec(memory_space=pltpu.VMEM) for _ in range(count)]


def packs(me, ids, lives, index, x, n_dp, seg_len, shift):
    count, (rows, width) = ids.shape[1], x.shape
    sizes = [SHARED + OWN] * (n_dp - 2) + [NEAR]
    shapes = [((2, count), jnp.int32), ((rows, 1), jnp.int32), ((rows, 1), jnp.int32)]
    shapes += [((rows, META), jnp.bfloat16), ((1, 1), jnp.int32)]
    shapes += [((n, width + META), jnp.bfloat16) for n in sizes] + [((2 * n_dp - 2, 256), jnp.int32)]
    return pl.pallas_call(
        functools.partial(pack_kernel, n_dp, seg_len, shift),
        in_specs=[pl.BlockSpec(memory_space=pltpu.SMEM)] + vmem(4),
        out_specs=vmem(len(shapes)),
        out_shape=[jax.ShapeDtypeStruct(*v) for v in shapes],
        compiler_params=pltpu.CompilerParams(vmem_limit_bytes=VMEM),
        cost_estimate=FREE,
        name="pack",
    )(me, ids, lives, index, x)


def share_kernel(at_ref, x_ref, w_ref, out_ref):
    out_ref[...] = jnp.dot(x_ref[...], w_ref[...], preferred_element_type=jnp.float32).astype(jnp.bfloat16)


def share(at, x, weight, cols):
    rows, depth = x.shape
    tile = min(512, cols)
    return pl.pallas_call(
        share_kernel,
        grid_spec=pltpu.PrefetchScalarGridSpec(
            num_scalar_prefetch=1,
            grid=(cols // tile,),
            in_specs=[
                pl.BlockSpec((rows, depth), lambda g, at: (0, 0)),
                pl.BlockSpec((depth, tile), lambda g, at: (0, at[0] * (cols // tile) + g)),
            ],
            out_specs=pl.BlockSpec((rows, tile), lambda g, at: (0, g)),
        ),
        out_shape=pltpu.HBM((rows, cols), jnp.bfloat16),
        compiler_params=pltpu.CompilerParams(vmem_limit_bytes=VMEM),
        cost_estimate=FREE,
        name="share",
    )(at, x, weight)


def per_device(
    attention_output,
    output_projection_weight,
    shrink_matrix_store,
    expand_matrix_store,
    segment_adapter,
    segment_live_rows,
    adapter_store_index,
):
    steps, rows_dev, width = attention_output.shape
    seg_count = segment_adapter.shape[1]
    seg_len = rows_dev // seg_count
    store, rank, _ = shrink_matrix_store.shape
    n_dp, n_tp = lax.axis_size("dp"), lax.axis_size("tp")
    me = lax.axis_index("dp").reshape(1)
    rows = steps * rows_dev
    count = steps * seg_count
    shift = store.bit_length() - 1
    big = 2 * rows
    far = range(2, n_dp)

    x = attention_output.reshape(rows, width)
    shrink_store = shrink_matrix_store.reshape(store * rank, width)
    expand_store = expand_matrix_store.reshape(store * rank, width)
    weight = output_projection_weight

    def swap(v, axis, k):
        n = lax.axis_size(axis)
        return lax.ppermute(v, axis, [(i, i ^ k) for i in range(n)])

    def butterfly(v, axis, op):
        k = lax.axis_size(axis) // 2
        while k:
            v = op(v, swap(v, axis, k))
            k //= 2
        return v

    def answer(dists, got, known):
        scored, told, slots = scores(me, known, dists, got, shrink_store)
        return slots, told, butterfly(scored, "tp", jnp.add)

    def total_of(parts):
        if len(parts) == 1:
            return parts[0]
        return functools.reduce(jnp.add, [v.astype(jnp.float32) for v in parts]).astype(jnp.bfloat16)

    def a2a(v):
        return lax.all_to_all(v, "dp", split_axis=0, concat_axis=0, tiled=True)

    def after(v, *others):
        return lax.optimization_barrier((v, others))[0]

    packed = list(packs(
        me,
        segment_adapter.reshape(1, count),
        segment_live_rows.reshape(1, count),
        adapter_store_index.reshape(1, -1),
        x, n_dp, seg_len, shift,
    ))
    table, row_code, self_slots, meta, rounds = packed[:5]
    m = len(far)
    out_far, out_near = packed[5:5 + m], packed[5 + m]
    codes = packed[6 + m]

    in_far = [swap(v, "dp", j) for v, j in zip(out_far, far)]
    in_near = swap(out_near, "dp", 1)

    self_found, _, self_part = answer([None], [after(x, table)], self_slots)

    at = after(lax.axis_index("tp").reshape(1), table)
    cols = weight.shape[1] // n_tp
    shares = {k: share(at ^ k, x, weight, cols) for k in reversed(range(n_tp))}
    (in_far, in_near, shares), _ = lax.optimization_barrier(((in_far, in_near, shares), self_part))

    found, rounds, part = answer(list(far) + [1], in_far + [in_near], rounds)
    in_far, shares, _ = lax.optimization_barrier((in_far, shares, rounds))
    in_relay = swap(jnp.concatenate([v[:SHARED] for v in in_far]), "dp", 1)
    direct = deltas(found, part, expand_store, me, n_dp)
    block = a2a(direct[-1])

    adds = {k: [shares[k]] for k in shares}
    for k in range(1, n_tp, 2):
        adds[k ^ 1].append(swap(adds.pop(k)[0], "tp", 1))
    for k in range(2, n_tp, 2):
        adds[k] = [total_of(adds[k])]

    in_relay, direct, adds = lax.optimization_barrier((in_relay, direct, adds))
    found, _, part = answer([RELAY], [in_relay], rounds)
    part, adds = lax.optimization_barrier((part, adds))
    (relayed,) = deltas(found, part, expand_store)
    (self_delta,) = deltas(self_found, after(self_part, relayed), expand_store)
    relayed = swap(relayed, "dp", 1)
    some, adds[0] = adds[0], []
    bit = 2
    while bit < n_tp:
        for k in sorted((k for k in adds if k & bit), reverse=True):
            adds[k ^ bit].append(swap(total_of(adds.pop(k)), "tp", bit))
        bit *= 2
    near = after(direct[m], block)
    some = place(me, row_code, codes, m + 1, [], [block], some + [self_delta], jnp.float32)
    relayed, some, direct = lax.optimization_barrier((relayed, some, direct))
    back = [swap(direct[i] + relayed[i * SHARED:(i + 1) * SHARED], "dp", j) for i, j in enumerate(far)]
    back.append(swap(near, "dp", 1))
    rounds = butterfly(rounds, "rep", jnp.maximum)[0, 0]

    def late_round(i, out):
        tab, rows_in, rows_meta, places = lax.optimization_barrier((table, x, meta, row_code, i))[:4]
        pos, alive = tab[0], tab[1]
        dist = (pos >> shift) ^ me[0]
        held = [None, jnp.int32(NEAR)]
        for j in range(2, n_dp, 2):
            extra = jnp.maximum(jnp.sum(jnp.where(dist == j, alive, 0)) - OWN, 0)
            held += [jnp.int32(OWN + 2 * SHARED), OWN + jnp.maximum(2 * SHARED - extra, 0)]
        x_meta = jnp.concatenate([rows_in, rows_meta], axis=1)
        code = [j * big + held[j] + i * ROUND + jnp.arange(ROUND, dtype=jnp.int32) for j in range(1, n_dp)]
        got = []
        for j, c in zip(range(1, n_dp), code):
            pick = (c[:, None] == places.reshape(1, rows)).astype(jnp.bfloat16)
            v = jnp.dot(pick, x_meta, preferred_element_type=jnp.float32).astype(jnp.bfloat16)
            got.append(swap(v, "dp", j))
        found, _, part = answer(list(range(1, n_dp)), got, rounds.reshape(1, 1))
        total = out.astype(jnp.float32)
        for j, c, v in zip(range(1, n_dp), code, deltas(found, part, expand_store)):
            put = (places == c[None, :]).astype(jnp.bfloat16)
            total = total + jnp.dot(put, swap(v, "dp", j), preferred_element_type=jnp.float32)
        return total.astype(jnp.bfloat16)

    out = place(me, row_code, codes, 0, back, [], [some] + adds[0], jnp.bfloat16)
    out = lax.fori_loop(0, rounds, late_round, out)
    return out.reshape(steps, rows_dev, width)


def solution(mesh):
    return jax.shard_map(
        per_device,
        mesh=mesh,
        in_specs=(
            P(None, ("rep", "dp"), "tp"),
            P("tp", None),
            P("dp", None, "tp"),
            P("dp", None, "tp"),
            P(None, ("rep", "dp")),
            P(None, ("rep", "dp")),
            P("rep"),
        ),
        out_specs=P(None, ("rep", "dp"), "tp"),
        check_vma=False,
    )
```
